32 devices in a mesh: groups: 2 (over y), cells: 8 (over z, x), freq: 2 (over core).
Axes of the slice: x: 2, y: 2, z: 4, core: 2. Of those that a mesh axis runs over, the one named last changes fastest.
Arguments:
- adjoint: float32 [2, 256], P(None, ('groups', 'cells')), parts along dimension 1, may hold values from -6 to 6
- target_x: float32 [256], P(('groups', 'cells')), parts along dimension 0, may hold values from 0 to 1024
- target_y: float32 [256], P(('groups', 'cells')), parts along dimension 0, may hold values from 0 to 8
- target_z: float32 [256], P(('groups', 'cells')), parts along dimension 0, may hold values from 256 to 512
- assignment: int32 [256], P(('groups', 'cells')), parts along dimension 0, may hold values from 0 to 63
- level_codes: int32 [16384], P(('groups', 'cells', 'freq')), parts along dimension 0, may hold values from 0 to 15
- cell_params: bfloat16 [8, 16384], P(None, ('groups', 'cells', 'freq')), parts along dimension 1, may hold values from -5 to 5
- level_table: bfloat16 [16, 256], replicated, may hold values from -4 to 4
- w_proj: bfloat16 [8, 256], replicated, may hold values from -2 to 2
- w_one: bfloat16 [256, 256], replicated, may hold values from -0.375 to 0.375
- b_one: float32 [256], replicated, may hold values from -3 to 3
- w_two: bfloat16 [256, 256], replicated, may hold values from -0.375 to 0.375
- b_two: float32 [256], replicated, may hold values from -3 to 3
- w_out: bfloat16 [256, 128], replicated, may hold values from -0.375 to 0.375
Outputs:
- grad_out: float32 [512, 128], P('groups'), parts along dimension 0
- grad_w2: float32 [512, 256], P('groups'), parts along dimension 0
- grad_b2: float32 [512], P('groups'), parts along dimension 0
- grad_w1: float32 [512, 256], P('groups'), parts along dimension 0
- grad_b1: float32 [512], P('groups'), parts along dimension 0
- grad_table: float32 [32, 256], P('groups'), parts along dimension 0
- grad_proj: float32 [16, 256], P('groups'), parts along dimension 0
- grad_params: float32 [8, 16384], P(None, ('groups', 'cells', 'freq')), parts along dimension 1
The draws below stay inside these ranges and needn't reach their ends.
There are 2 independent parts, one for each index of `groups`. The reference program is written for one: setup_inputs(seed, part) draws one part's arguments, and reference() takes and returns one part's arrays. A program takes and returns all parts, laid end to end along the dimension named above; an argument that names none is the same for every part. Nothing has to cross between parts.
All inputs are finite; a program needn't handle non-finite values.
Results may differ from the reference program's by a relative error of at most 0.01.
Values may be sent and summed in bfloat16 or wider, within the bound.
No kernel may reach another device: no remote copies, remote signals or barrier semaphores. Data moves between devices by JAX's collectives and lax.ppermute only.
A program may use at most 64 MiB of HBM per device.

```python
import math
import jax
import jax.numpy as jnp
from jax import lax

F = 64
H = 256
LEVELS = 16
NP = 8
SIDE = 1024
CELLS = 8192
TARGETS = 128


def touch_ends(entries, key, smallest, largest):
    extent = entries.shape
    place = [jax.random.randint(jax.random.fold_in(key, axis), (), 0, extent[axis]) for axis in range(len(extent))]
    entries = entries.at[tuple(place)].set(smallest)
    longest = extent.index(max(extent))
    place[longest] = (place[longest] + 1) % extent[longest]
    return entries.at[tuple(place)].set(largest)


def block_levels(stream_key, dims, shards, low, high):
    def one(axis_at, parts):
        draws = jax.random.uniform(jax.random.fold_in(jax.random.fold_in(stream_key, 6), axis_at), (parts,), jnp.float32, low / len(shards), high / len(shards))
        return jnp.repeat(jnp.exp(draws), dims[axis_at] // parts).reshape((-1,) + (1,) * (len(dims) - axis_at - 1))

    factor_of = one(*shards[0])
    for cut in shards[1:]:
        factor_of = factor_of * one(*cut)
    return factor_of


def centred(key, extent, scale, most, pieces=(), kind=jnp.bfloat16):
    result = scale * jax.random.normal(key, extent, jnp.float32)
    if pieces:
        result = result * block_levels(key, extent, pieces, -0.22, 0.18)
    return jnp.clip(result, -most, most).astype(kind)


def setup_inputs(seed: int = 0, part: int = 0) -> dict:
    arg_keys = jax.random.split(jax.random.key(seed), 15)
    own_keys = jax.random.split(jax.random.fold_in(arg_keys[14], part), 15)
    adjoint = centred(own_keys[0], (2, TARGETS), 1.0, 6.0, ((1, 8),), jnp.float32)
    target_x = jnp.clip(1024.0 * jax.random.uniform(own_keys[1], (TARGETS,), jnp.float32) ** block_levels(own_keys[1], (TARGETS,), ((0, 8),), -0.2, 0.2), 0.0, 1024.0)
    target_y = jnp.clip(8.0 * jax.random.uniform(own_keys[2], (TARGETS,), jnp.float32) ** block_levels(own_keys[2], (TARGETS,), ((0, 8),), -0.2, 0.2), 0.0, 8.0)
    target_z = jnp.clip(256.0 + 256.0 * jax.random.uniform(own_keys[3], (TARGETS,), jnp.float32) ** block_levels(own_keys[3], (TARGETS,), ((0, 8),), -0.2, 0.2), 256.0, 512.0)
    assignment = touch_ends(jax.random.randint(own_keys[4], (TARGETS,), 0, F), jax.random.fold_in(own_keys[4], 1), 0, F - 1).astype(jnp.int32)
    level_codes = touch_ends(jax.random.randint(own_keys[5], (CELLS,), 0, LEVELS), jax.random.fold_in(own_keys[5], 1), 0, LEVELS - 1).astype(jnp.int32)
    cell_params = centred(own_keys[6], (NP, CELLS), 1.0, 5.0, ((1, 16),))
    level_table = centred(arg_keys[7], (LEVELS, H), 0.7, 4.0)
    w_proj = centred(arg_keys[8], (NP, H), NP ** -0.5, 2.0)
    w_one = centred(arg_keys[9], (H, H), H ** -0.5, 0.375)
    b_one = centred(arg_keys[10], (H,), 0.5, 3.0, (), jnp.float32)
    w_two = centred(arg_keys[11], (H, H), H ** -0.5, 0.375)
    b_two = centred(arg_keys[12], (H,), 0.5, 3.0, (), jnp.float32)
    w_out = centred(arg_keys[13], (H, 2 * F), H ** -0.5, 0.375)
    return dict(adjoint=adjoint, target_x=target_x, target_y=target_y, target_z=target_z, assignment=assignment, level_codes=level_codes, cell_params=cell_params, level_table=level_table, w_proj=w_proj, w_one=w_one, b_one=b_one, w_two=w_two, b_two=b_two, w_out=w_out)


wave_low = 1.0
wave_high = 3.0
kernel_gain = 150.0

def silu_slope(value):
    sigma = jax.nn.sigmoid(value)
    return sigma * (1.0 + value * (1.0 - sigma))

def contract(left, right, left_dim, right_dim):
    return lax.dot_general(left, right, (((left_dim,), (right_dim,)), ((), ())), preferred_element_type=jnp.float32)

def kernel_tile(point_x, point_y, point_z, freq_value, cell_col, cell_row, count_freq):
    wave = wave_low + (wave_high - wave_low) * freq_value / (count_freq - 1)
    offset_x = point_x[:, None] - cell_col[None, :]
    offset_y = point_y[:, None] - cell_row[None, :]
    square = offset_x * offset_x + offset_y * offset_y + (point_z * point_z)[:, None]
    distance = jnp.sqrt(square)
    amplitude = kernel_gain * point_z[:, None] / square
    phase = wave[:, None] * distance
    return ((amplitude * jnp.cos(phase)).astype(jnp.bfloat16), (amplitude * jnp.sin(phase)).astype(jnp.bfloat16))

def forward_pass(level_codes, cell_params, level_table, w_proj, w_one, b_one, w_two, b_two):
    levels = level_table.shape[0]
    onehot = (level_codes[:, None] == jnp.arange(levels, dtype=jnp.int32)[None, :]).astype(jnp.bfloat16)
    hidden_in = (jnp.dot(onehot, level_table, preferred_element_type=jnp.float32) + contract(cell_params, w_proj, 0, 0)).astype(jnp.bfloat16)
    pre_one = jnp.dot(hidden_in, w_one, preferred_element_type=jnp.float32) + b_one
    act_one = jax.nn.silu(pre_one).astype(jnp.bfloat16)
    pre_two = jnp.dot(act_one, w_two, preferred_element_type=jnp.float32) + b_two
    act_two = jax.nn.silu(pre_two).astype(jnp.bfloat16)
    return (onehot, hidden_in, pre_one, act_one, pre_two, act_two)

def upper_grads(spectra, w_out, act_one, pre_two, act_two):
    back_two = contract(spectra, w_out, 0, 1)
    delta_two = (back_two * silu_slope(pre_two)).astype(jnp.bfloat16)
    grad_out = contract(act_two, spectra, 0, 1)
    grad_w2 = contract(act_one, delta_two, 0, 0)
    grad_b2 = lax.optimization_barrier(jnp.sum(delta_two.astype(jnp.float32), axis=0))
    return ((grad_out, grad_w2, grad_b2), delta_two)

def lower_grads(delta_two, w_two, w_one, pre_one, hidden_in, onehot, cell_params, w_proj):
    back_one = contract(delta_two, w_two, 1, 1)
    delta_one = (back_one * silu_slope(pre_one)).astype(jnp.bfloat16)
    grad_w1 = contract(hidden_in, delta_one, 0, 0)
    grad_b1 = lax.optimization_barrier(jnp.sum(delta_one.astype(jnp.float32), axis=0))
    back_zero = contract(delta_one, w_one, 1, 1).astype(jnp.bfloat16)
    grad_table = contract(onehot, back_zero, 0, 0)
    grad_proj = contract(cell_params, back_zero, 1, 0)
    grad_params = contract(w_proj, back_zero, 1, 1)
    return ((grad_w1, grad_b1, grad_table, grad_proj), grad_params)

def reference(adjoint, target_x, target_y, target_z, assignment, level_codes, cell_params, level_table, w_proj, w_one, b_one, w_two, b_two, w_out):
    adj_round = lax.optimization_barrier(adjoint.astype(jnp.bfloat16)).astype(jnp.float32)
    freq_value = assignment.astype(jnp.float32)
    blocks = CELLS // SIDE
    scale = 1.0 / math.sqrt(CELLS)

    def step(carry, block):
        start = block * SIDE
        index = start + jnp.arange(SIDE, dtype=jnp.int32)
        cell_col = (index % SIDE).astype(jnp.float32)
        cell_row = (index // SIDE).astype(jnp.float32)
        kre, kim = kernel_tile(target_x, target_y, target_z, freq_value, cell_col, cell_row, F)
        kre, kim = lax.optimization_barrier((kre, kim))
        kre = kre.astype(jnp.float32)
        kim = kim.astype(jnp.float32)
        real_part = jax.ops.segment_sum(kre * adj_round[0][:, None] + kim * adj_round[1][:, None], assignment, num_segments=F)
        imag_part = jax.ops.segment_sum(kre * adj_round[1][:, None] - kim * adj_round[0][:, None], assignment, num_segments=F)
        spectra = jnp.concatenate([real_part, imag_part], axis=0).astype(jnp.bfloat16)
        codes_block = lax.dynamic_slice_in_dim(level_codes, start, SIDE)
        params_block = lax.dynamic_slice_in_dim(cell_params, start, SIDE, axis=1)
        onehot, hidden_in, pre_one, act_one, pre_two, act_two = forward_pass(codes_block, params_block, level_table, w_proj, w_one, b_one, w_two, b_two)
        upper, delta_two = upper_grads(spectra, w_out, act_one, pre_two, act_two)
        lower, grad_params = lower_grads(delta_two, w_two, w_one, pre_one, hidden_in, onehot, params_block, w_proj)
        carry = tuple((total + term for total, term in zip(carry, upper + lower)))
        return (carry, grad_params)
    init = (jnp.zeros((H, 2 * F), jnp.float32), jnp.zeros((H, H), jnp.float32), jnp.zeros((H,), jnp.float32), jnp.zeros((H, H), jnp.float32), jnp.zeros((H,), jnp.float32), jnp.zeros((LEVELS, H), jnp.float32), jnp.zeros((NP, H), jnp.float32))
    totals, params_grads = lax.scan(step, init, jnp.arange(blocks, dtype=jnp.int32))
    grad_params = jnp.moveaxis(params_grads, 0, 1).reshape(NP, CELLS)
    return (totals[0] * scale, totals[1] * scale, totals[2] * scale, totals[3] * scale, totals[4] * scale, totals[5] * scale, totals[6] * scale, grad_params)
```

```python
import functools
import math

import jax
import jax.numpy as jnp
from jax import lax
from jax.experimental import pallas as pl
from jax.experimental.pallas import tpu as pltpu
from jax.sharding import PartitionSpec as P

SIDE = 1024

wave_low = 1.0
wave_high = 3.0
kernel_gain = 150.0

F32 = jnp.float32
BF16 = jnp.bfloat16
VMEM_BYTES = 40 * 1024 * 1024


def silu_slope(value):
    sigma = jax.nn.sigmoid(value)
    return sigma * (1.0 + value * (1.0 - sigma))


def contract(left, right, left_dim, right_dim):
    return lax.dot_general(
        left, right, (((left_dim,), (right_dim,)), ((), ())), preferred_element_type=jnp.float32
    )


def kernel_tile(point_x, point_y, point_z, freq_value, cell_col, cell_row, count_freq):
    wave = wave_low + (wave_high - wave_low) * freq_value / (count_freq - 1)
    offset_x = point_x[:, None] - cell_col[None, :]
    offset_y = point_y[:, None] - cell_row[None, :]
    square = offset_x * offset_x + offset_y * offset_y + (point_z * point_z)[:, None]
    distance = jnp.sqrt(square)
    amplitude = kernel_gain * point_z[:, None] / square
    phase = wave[:, None] * distance
    return (
        (amplitude * jnp.cos(phase)).astype(jnp.bfloat16),
        (amplitude * jnp.sin(phase)).astype(jnp.bfloat16),
    )


def forward_pass(level_codes, cell_params, level_table, w_proj, w_one, b_one, w_two, b_two):
    levels = level_table.shape[0]
    onehot = (level_codes[:, None] == jnp.arange(levels, dtype=jnp.int32)[None, :]).astype(
        jnp.bfloat16
    )
    hidden_in = (
        jnp.dot(onehot, level_table, preferred_element_type=jnp.float32)
        + contract(cell_params, w_proj, 0, 0)
    ).astype(jnp.bfloat16)
    pre_one = jnp.dot(hidden_in, w_one, preferred_element_type=jnp.float32) + b_one
    act_one = jax.nn.silu(pre_one).astype(jnp.bfloat16)
    pre_two = jnp.dot(act_one, w_two, preferred_element_type=jnp.float32) + b_two
    act_two = jax.nn.silu(pre_two).astype(jnp.bfloat16)
    return (onehot, hidden_in, pre_one, act_one, pre_two, act_two)


def upper_grads(spectra, w_out, act_one, pre_two, act_two):
    back_two = contract(spectra, w_out, 0, 1)
    delta_two = (back_two * silu_slope(pre_two)).astype(jnp.bfloat16)
    grad_out = contract(act_two, spectra, 0, 1)
    grad_w2 = contract(act_one, delta_two, 0, 0)
    grad_b2 = jnp.sum(delta_two.astype(jnp.float32), axis=0)
    return ((grad_out, grad_w2, grad_b2), delta_two)


def lower_grads(delta_two, w_two, w_one, pre_one, hidden_in, onehot, cell_params, w_proj):
    back_one = contract(delta_two, w_two, 1, 1)
    delta_one = (back_one * silu_slope(pre_one)).astype(jnp.bfloat16)
    grad_w1 = contract(hidden_in, delta_one, 0, 0)
    grad_b1 = jnp.sum(delta_one.astype(jnp.float32), axis=0)
    back_zero = contract(delta_one, w_one, 1, 1).astype(jnp.bfloat16)
    grad_table = contract(onehot, back_zero, 0, 0)
    grad_proj = contract(cell_params, back_zero, 1, 0)
    grad_params = contract(w_proj, back_zero, 1, 1)
    return ((grad_w1, grad_b1, grad_table, grad_proj), grad_params)


def general_body(
    adjoint,
    target_x,
    target_y,
    target_z,
    assignment,
    level_codes,
    cell_params,
    level_table,
    w_proj,
    w_one,
    b_one,
    w_two,
    b_two,
    w_out,
):
    cell_count = level_codes.shape[0]
    freq_count = w_out.shape[1] // 2
    freq_size = lax.axis_size("freq")
    cell_rank = lax.axis_index("cells")
    freq_rank = lax.axis_index("freq")
    first_cell = (cell_rank * freq_size + freq_rank) * cell_count
    index = first_cell + jnp.arange(cell_count, dtype=jnp.int32)
    cell_col = (index % SIDE).astype(jnp.float32)
    cell_row = (index // SIDE).astype(jnp.float32)
    freq_grid = jnp.arange(freq_count, dtype=jnp.int32).astype(jnp.float32)
    stacked = jnp.concatenate(
        [
            adjoint,
            target_x[None, :],
            target_y[None, :],
            target_z[None, :],
            assignment.astype(jnp.float32)[None, :],
        ],
        axis=0,
    )
    total = jnp.zeros((2 * freq_count, cell_count), jnp.float32)
    piece = lax.all_gather(stacked, "cells", axis=1, tiled=True)
    length = piece.shape[1]
    block_len = math.gcd(length, 256)
    sections = piece.reshape(6, length // block_len, block_len).transpose(1, 0, 2)

    def inner(accum, rows):
        adj_round = rows[0:2].astype(jnp.bfloat16)
        kre, kim = kernel_tile(rows[2], rows[3], rows[4], rows[5], cell_col, cell_row, freq_count)
        select = (rows[5][:, None] == freq_grid[None, :]).astype(jnp.bfloat16)
        part_a = select * adj_round[0][:, None]
        part_b = select * adj_round[1][:, None]
        left_re = jnp.concatenate([part_a, part_b], axis=1)
        left_im = jnp.concatenate([part_b, -part_a], axis=1)
        return (accum + contract(left_re, kre, 0, 0) + contract(left_im, kim, 0, 0), None)

    total, unused = lax.scan(inner, total, sections)
    local_spec = total.astype(jnp.bfloat16)
    scale = 1.0 / math.sqrt(cell_count * lax.axis_size("cells") * freq_size)
    onehot, hidden_in, pre_one, act_one, pre_two, act_two = forward_pass(
        level_codes, cell_params, level_table, w_proj, w_one, b_one, w_two, b_two
    )
    upper, delta_two = upper_grads(local_spec, w_out, act_one, pre_two, act_two)
    lower, grad_params = lower_grads(
        delta_two, w_two, w_one, pre_one, hidden_in, onehot, cell_params, w_proj
    )
    totals = lax.psum(tuple(term * scale for term in upper + lower), ("cells", "freq"))
    return totals + (grad_params,)


def split(value, parts):
    pieces = []
    for _ in range(parts):
        piece = value.astype(BF16)
        pieces.append(piece.astype(F32))
        value = value - piece.astype(F32)
    return pieces


def pack_kernel(adj_ref, x_ref, y_ref, z_ref, assign_ref, codes_ref, params_ref, out_ref, rows):
    count = x_ref.shape[1]
    cells = codes_ref.shape[1]
    rows[...] = jnp.zeros_like(rows)
    rows[0:2, 0:count] = adj_ref[...]
    at = 2
    for ref in (x_ref, y_ref, z_ref):
        for piece in split(ref[...], 3):
            rows[at : at + 1, 0:count] = piece
            at += 1
    rows[at : at + 1, 0:count] = assign_ref[...].astype(F32)
    out_ref[:, 0:cells] = jnp.concatenate(
        [params_ref[...].astype(F32), jnp.broadcast_to(codes_ref[...].astype(F32), (8, cells))],
        axis=0,
    ).astype(BF16)
    out_ref[:, cells:] = rows[...].T[0:count].astype(BF16)


def weight_kernel(
    table_ref, proj_ref, w1_ref, b1_ref, w2_ref, b2_ref, wo_ref,
    first_ref, second_ref, bias_ref, back_two_ref, back_one_ref, params_ref, embed_ref,
):
    levels, hidden = table_ref.shape
    stack = jnp.concatenate([table_ref[...].astype(F32), proj_ref[...].astype(F32)], axis=0)
    joined = jnp.dot(stack.astype(BF16), w1_ref[...], preferred_element_type=F32)
    used = levels + proj_ref.shape[0]
    pad = jnp.zeros((7, hidden), F32)
    full = 0.5 * jnp.concatenate([joined, b1_ref[...], pad], axis=0)
    rows = jnp.concatenate(split(full, 3), axis=0)
    fill = 128 - rows.shape[0]
    first_ref[...] = jnp.concatenate([rows, jnp.zeros((fill, hidden), F32)], axis=0).T.astype(BF16)
    second_ref[...] = (0.5 * w2_ref[...].astype(F32)).T.astype(BF16)
    bias_ref[...] = jnp.broadcast_to(0.5 * b2_ref[...], (128, hidden)).T
    back_two_ref[...] = (0.5 * wo_ref[...].astype(F32)).astype(BF16)
    back_one_ref[...] = (0.5 * w2_ref[...].astype(F32)).astype(BF16)
    params_ref[...] = jnp.concatenate(split(joined[levels:used], 2), axis=0).astype(BF16)
    triple = jnp.concatenate([stack, jnp.zeros((8, hidden), F32)], axis=0)
    embed_ref[...] = jnp.concatenate(
        [triple, triple, triple, jnp.zeros((fill, hidden), F32)], axis=0
    ).T.astype(BF16)


def cell_kernel(
    freq_size, step,
    place_ref, gathered_ref, first_ref, second_ref, bias_ref, back_two_ref, back_one_ref, params_ref,
    sums_ref, grad_params_ref,
    where, lift, waves, deltas,
):
    chunks, local, width = gathered_ref.shape
    cells = width - 128
    hidden = second_ref.shape[0]
    freqs = back_two_ref.shape[1] // 2
    targets = chunks * local
    me = place_ref[0]
    freq_rank = place_ref[1]

    parts = []
    for chunk in range(chunks):
        parts.append(gathered_ref[chunk ^ me, :, cells:].astype(F32))
    table = jnp.concatenate(parts, axis=0)
    point_x = (table[:, 2:3] + table[:, 3:4]) + table[:, 4:5]
    point_y = (table[:, 5:6] + table[:, 6:7]) + table[:, 7:8]
    point_z = (table[:, 8:9] + table[:, 9:10]) + table[:, 10:11]
    assign = table[:, 11:12]
    wave = (wave_low + (wave_high - wave_low) * assign / (freqs - 1)) * (0.5 / math.pi)
    full = (targets, 128)
    where[0] = jnp.broadcast_to(point_x, full)
    where[1] = jnp.broadcast_to(point_y, full)
    where[2] = jnp.broadcast_to(point_z * point_z, full)
    where[3] = jnp.broadcast_to(wave, full)
    where[4] = jnp.broadcast_to(kernel_gain * point_z, full)
    grid = lax.broadcasted_iota(jnp.int32, (targets, freqs), 1).astype(F32)
    select = jnp.where(assign == grid, 1.0, 0.0)
    part_a = select * table[:, 0:1]
    part_b = select * table[:, 1:2]
    lift[:, 0:targets] = jnp.concatenate([part_a, part_b], axis=1).T.astype(BF16)
    lift[:, targets:] = jnp.concatenate([part_b, -part_a], axis=1).T.astype(BF16)
    sums_ref[...] = jnp.zeros_like(sums_ref)

    def one(chunk, start):
        slot = chunk ^ me
        base = (chunk * freq_size + freq_rank) * cells + start
        index = base + lax.broadcasted_iota(jnp.int32, (1, step), 1)
        col = (index % SIDE).astype(F32)
        row = (index // SIDE).astype(F32)
        for at in range(0, targets, 16):
            for lane in range(0, step, 128):
                here = pl.ds(at, 16)
                off_x = where[0, here] - col[:, lane : lane + 128]
                off_y = where[1, here] - row[:, lane : lane + 128]
                square = off_x * off_x + off_y * off_y + where[2, here]
                inverse = lax.rsqrt(square)
                turns = where[3, here] * (square * inverse)
                angle = (turns - jnp.round(turns)) * (2.0 * math.pi)
                amplitude = where[4, here] * (inverse * inverse)
                waves[at : at + 16, lane : lane + 128] = (amplitude * jnp.cos(angle)).astype(BF16)
                waves[targets + at : targets + at + 16, lane : lane + 128] = (
                    amplitude * jnp.sin(angle)
                ).astype(BF16)
        spectra = jnp.dot(lift[...], waves[...], preferred_element_type=F32).astype(BF16)

        data = gathered_ref[slot, :, pl.ds(start, step)].astype(F32)
        codes = data[8:16]
        steps = lax.broadcasted_iota(jnp.int32, (8, step), 0).astype(F32)
        feature = jnp.concatenate(
            [
                jnp.where(codes == steps, 1.0, 0.0),
                jnp.where(codes == steps + 8.0, 1.0, 0.0),
                data[0:8],
                jnp.where(steps == 0.0, 1.0, 0.0),
            ],
            axis=0,
        ).astype(BF16)
        tripled = jnp.concatenate(
            [feature, feature, feature, jnp.zeros((32, step), BF16)], axis=0
        )
        half_one = jnp.dot(first_ref[...], tripled, preferred_element_type=F32)
        tanh_one = jnp.tanh(half_one)
        gate_one = 1.0 + tanh_one
        act_one = half_one * gate_one
        slope_one = gate_one + act_one * (1.0 - tanh_one)
        act_one = act_one.astype(BF16)
        half_two = jnp.dot(second_ref[...], act_one, preferred_element_type=F32)
        half_two = half_two + jnp.concatenate([bias_ref[...]] * (step // 128), axis=1)
        tanh_two = jnp.tanh(half_two)
        gate_two = 1.0 + tanh_two
        act_two = half_two * gate_two
        slope_two = gate_two + act_two * (1.0 - tanh_two)
        act_two = act_two.astype(BF16)
        back_two = jnp.dot(back_two_ref[...], spectra, preferred_element_type=F32)
        delta_two = (back_two * slope_two).astype(BF16)
        back_one = jnp.dot(back_one_ref[...], delta_two, preferred_element_type=F32)
        delta_one = (back_one * slope_one).astype(BF16)
        deltas[chunk, :, pl.ds(start, step)] = delta_one
        top = hidden + 2 * freqs
        sums_ref[0:hidden] += contract(act_one, delta_two, 1, 1)
        sums_ref[hidden:top] += contract(spectra, act_two, 1, 1)
        sums_ref[top : top + 32] += contract(feature, delta_one, 1, 1)
        sums_ref[top + 32 : top + 64] += contract(feature, delta_two, 1, 1)

    def each(at, carry):
        one(at // (cells // step), pl.multiple_of((at % (cells // step)) * step, step))
        return carry

    lax.fori_loop(0, chunks * (cells // step), each, 0)
    both = jnp.dot(params_ref[...], deltas[me], preferred_element_type=F32)
    grad_params_ref[...] = both[0:8] + both[8:16]


def finish_kernel(
    scale, own_ref, other_ref, embed_ref, w1_ref,
    out_ref, w2_ref, b2_ref, wone_ref, b1_ref, table_ref, proj_ref,
):
    hidden = w1_ref.shape[0]
    top = hidden + out_ref.shape[1]
    levels = table_ref.shape[0]
    used = levels + proj_ref.shape[0]

    def total(low, high):
        return (own_ref[low:high].astype(F32) + other_ref[low:high].astype(F32)) * scale

    w2_ref[...] = total(0, hidden)
    out_ref[...] = total(hidden, top).T
    feature = total(top, top + 32)
    b1_ref[...] = feature[used : used + 1]
    b2_ref[...] = total(top + 32, top + 64)[used : used + 1]
    pieces = split(feature, 3)
    rows = jnp.concatenate(pieces, axis=0).astype(BF16)
    wone_ref[...] = jnp.dot(embed_ref[:, 0:96], rows, preferred_element_type=F32)
    back = contract(rows, w1_ref[...], 1, 1)
    back = (back[0:32] + back[32:64]) + back[64:96]
    table_ref[...] = back[0:levels]
    proj_ref[...] = back[levels:used]


def small_body(
    adjoint,
    target_x,
    target_y,
    target_z,
    assignment,
    level_codes,
    cell_params,
    level_table,
    w_proj,
    w_one,
    b_one,
    w_two,
    b_two,
    w_out,
):
    cells = level_codes.shape[0]
    local = target_x.shape[0]
    levels, hidden = level_table.shape
    props = w_proj.shape[0]
    freqs = w_out.shape[1] // 2
    chunks = lax.axis_size("cells")
    freq_size = lax.axis_size("freq")
    shape = jax.ShapeDtypeStruct
    params = pltpu.CompilerParams(vmem_limit_bytes=VMEM_BYTES)

    packed = pl.pallas_call(
        pack_kernel,
        out_shape=shape((16, cells + 128), BF16),
        scratch_shapes=[pltpu.VMEM((128, 128), F32)],
        compiler_params=params,
        name="pack_inputs",
    )(
        adjoint, target_x[None, :], target_y[None, :], target_z[None, :], assignment[None, :],
        level_codes[None, :], cell_params,
    )
    gathered = packed[None]
    reach = 1
    while reach < chunks:
        moved = lax.ppermute(gathered, "cells", [(at, at ^ reach) for at in range(chunks)])
        gathered = jnp.concatenate([gathered, moved], axis=0)
        reach *= 2

    first, second, bias, back_two, back_one, proj_rows, embed = pl.pallas_call(
        weight_kernel,
        out_shape=(
            shape((hidden, 128), BF16),
            shape((hidden, hidden), BF16),
            shape((hidden, 128), F32),
            shape((hidden, 2 * freqs), BF16),
            shape((hidden, hidden), BF16),
            shape((2 * props, hidden), BF16),
            shape((hidden, 128), BF16),
        ),
        compiler_params=params,
        name="prepare_weights",
    )(level_table, w_proj, w_one, b_one[None, :], w_two, b_two[None, :], w_out)

    place = jnp.stack([lax.axis_index("cells"), lax.axis_index("freq")]).astype(jnp.int32)
    step = min(256, cells)
    targets = chunks * local
    vmem = pl.BlockSpec(memory_space=pltpu.VMEM)
    sums, grad_params = pl.pallas_call(
        functools.partial(cell_kernel, freq_size, step),
        out_shape=(
            shape((hidden + 2 * freqs + 64, hidden), F32),
            shape((props, cells), F32),
        ),
        in_specs=[pl.BlockSpec(memory_space=pltpu.SMEM)] + [vmem] * 7,
        out_specs=(vmem, vmem),
        scratch_shapes=[
            pltpu.VMEM((5, targets, 128), F32),
            pltpu.VMEM((2 * freqs, 2 * targets), BF16),
            pltpu.VMEM((2 * targets, step), BF16),
            pltpu.VMEM((chunks, hidden, cells), BF16),
        ],
        compiler_params=params,
        name="all_cells",
    )(place, gathered, first, second, bias, back_two, back_one, proj_rows)

    other = lax.ppermute(sums, "freq", [(at, at ^ 1) for at in range(freq_size)])
    scale = 1.0 / math.sqrt(cells * chunks * freq_size)
    grad_out, grad_w2, grad_b2, grad_w1, grad_b1, grad_table, grad_proj = pl.pallas_call(
        functools.partial(finish_kernel, scale),
        out_shape=(
            shape((hidden, 2 * freqs), F32),
            shape((hidden, hidden), F32),
            shape((1, hidden), F32),
            shape((hidden, hidden), F32),
            shape((1, hidden), F32),
            shape((levels, hidden), F32),
            shape((props, hidden), F32),
        ),
        compiler_params=params,
        name="finish_sums",
    )(sums, other, embed, w_one)
    return (
        grad_out, grad_w2, grad_b2[0], grad_w1, grad_b1[0], grad_table, grad_proj, grad_params,
    )


def solution(mesh):
    chunks = mesh.shape["cells"]
    paired = mesh.shape["freq"] == 2 and chunks & (chunks - 1) == 0

    def body(*args):
        local = args[1].shape[0]
        cells = args[5].shape[0]
        hidden = args[9].shape[0]
        suits = (
            paired
            and local == 16
            and cells % 256 == 0
            and chunks * cells * chunks * local <= 1 << 20
            and args[7].shape[0] == 16
            and args[8].shape[0] == 8
            and hidden % 128 == 0
            and args[13].shape[1] == 128
        )
        return (small_body if suits else general_body)(*args)

    placed = (
        P(None, ("groups", "cells")),
        P(("groups", "cells")),
        P(("groups", "cells")),
        P(("groups", "cells")),
        P(("groups", "cells")),
        P(("groups", "cells", "freq")),
        P(None, ("groups", "cells", "freq")),
        P(),
        P(),
        P(),
        P(),
        P(),
        P(),
        P(),
    )
    return jax.shard_map(
        body,
        mesh=mesh,
        in_specs=placed,
        out_specs=(
            P("groups", None),
            P("groups", None),
            P("groups"),
            P("groups", None),
            P("groups"),
            P("groups", None),
            P("groups", None),
            P(None, ("groups", "cells", "freq")),
        ),
        check_vma=False,
    )
```

```python
import functools
import math

import jax
import jax.numpy as jnp
from jax import lax
from jax.experimental import pallas as pl
from jax.experimental.pallas import tpu as pltpu
from jax.sharding import PartitionSpec as P

SIDE = 1024

wave_low = 1.0
wave_high = 3.0
kernel_gain = 150.0

F32 = jnp.float32
BF16 = jnp.bfloat16
VMEM_BYTES = 40 * 1024 * 1024
WHOLE_VMEM = 64 * 1024 * 1024 - 256 * 1024


def silu_slope(value):
    sigma = jax.nn.sigmoid(value)
    return sigma * (1.0 + value * (1.0 - sigma))


def contract(left, right, left_dim, right_dim):
    return lax.dot_general(
        left, right, (((left_dim,), (right_dim,)), ((), ())), preferred_element_type=jnp.float32
    )


def kernel_tile(point_x, point_y, point_z, freq_value, cell_col, cell_row, count_freq):
    wave = wave_low + (wave_high - wave_low) * freq_value / (count_freq - 1)
    offset_x = point_x[:, None] - cell_col[None, :]
    offset_y = point_y[:, None] - cell_row[None, :]
    square = offset_x * offset_x + offset_y * offset_y + (point_z * point_z)[:, None]
    distance = jnp.sqrt(square)
    amplitude = kernel_gain * point_z[:, None] / square
    phase = wave[:, None] * distance
    return (
        (amplitude * jnp.cos(phase)).astype(jnp.bfloat16),
        (amplitude * jnp.sin(phase)).astype(jnp.bfloat16),
    )


def forward_pass(level_codes, cell_params, level_table, w_proj, w_one, b_one, w_two, b_two):
    levels = level_table.shape[0]
    onehot = (level_codes[:, None] == jnp.arange(levels, dtype=jnp.int32)[None, :]).astype(
        jnp.bfloat16
    )
    hidden_in = (
        jnp.dot(onehot, level_table, preferred_element_type=jnp.float32)
        + contract(cell_params, w_proj, 0, 0)
    ).astype(jnp.bfloat16)
    pre_one = jnp.dot(hidden_in, w_one, preferred_element_type=jnp.float32) + b_one
    act_one = jax.nn.silu(pre_one).astype(jnp.bfloat16)
    pre_two = jnp.dot(act_one, w_two, preferred_element_type=jnp.float32) + b_two
    act_two = jax.nn.silu(pre_two).astype(jnp.bfloat16)
    return (onehot, hidden_in, pre_one, act_one, pre_two, act_two)


def upper_grads(spectra, w_out, act_one, pre_two, act_two):
    back_two = contract(spectra, w_out, 0, 1)
    delta_two = (back_two * silu_slope(pre_two)).astype(jnp.bfloat16)
    grad_out = contract(act_two, spectra, 0, 1)
    grad_w2 = contract(act_one, delta_two, 0, 0)
    grad_b2 = jnp.sum(delta_two.astype(jnp.float32), axis=0)
    return ((grad_out, grad_w2, grad_b2), delta_two)


def lower_grads(delta_two, w_two, w_one, pre_one, hidden_in, onehot, cell_params, w_proj):
    back_one = contract(delta_two, w_two, 1, 1)
    delta_one = (back_one * silu_slope(pre_one)).astype(jnp.bfloat16)
    grad_w1 = contract(hidden_in, delta_one, 0, 0)
    grad_b1 = jnp.sum(delta_one.astype(jnp.float32), axis=0)
    back_zero = contract(delta_one, w_one, 1, 1).astype(jnp.bfloat16)
    grad_table = contract(onehot, back_zero, 0, 0)
    grad_proj = contract(cell_params, back_zero, 1, 0)
    grad_params = contract(w_proj, back_zero, 1, 1)
    return ((grad_w1, grad_b1, grad_table, grad_proj), grad_params)


def general_body(
    adjoint,
    target_x,
    target_y,
    target_z,
    assignment,
    level_codes,
    cell_params,
    level_table,
    w_proj,
    w_one,
    b_one,
    w_two,
    b_two,
    w_out,
):
    cell_count = level_codes.shape[0]
    freq_count = w_out.shape[1] // 2
    freq_size = lax.axis_size("freq")
    cell_rank = lax.axis_index("cells")
    freq_rank = lax.axis_index("freq")
    first_cell = (cell_rank * freq_size + freq_rank) * cell_count
    index = first_cell + jnp.arange(cell_count, dtype=jnp.int32)
    cell_col = (index % SIDE).astype(jnp.float32)
    cell_row = (index // SIDE).astype(jnp.float32)
    freq_grid = jnp.arange(freq_count, dtype=jnp.int32).astype(jnp.float32)
    stacked = jnp.concatenate(
        [
            adjoint,
            target_x[None, :],
            target_y[None, :],
            target_z[None, :],
            assignment.astype(jnp.float32)[None, :],
        ],
        axis=0,
    )
    total = jnp.zeros((2 * freq_count, cell_count), jnp.float32)
    piece = lax.all_gather(stacked, "cells", axis=1, tiled=True)
    length = piece.shape[1]
    block_len = math.gcd(length, 256)
    sections = piece.reshape(6, length // block_len, block_len).transpose(1, 0, 2)

    def inner(accum, rows):
        adj_round = rows[0:2].astype(jnp.bfloat16)
        kre, kim = kernel_tile(rows[2], rows[3], rows[4], rows[5], cell_col, cell_row, freq_count)
        select = (rows[5][:, None] == freq_grid[None, :]).astype(jnp.bfloat16)
        part_a = select * adj_round[0][:, None]
        part_b = select * adj_round[1][:, None]
        left_re = jnp.concatenate([part_a, part_b], axis=1)
        left_im = jnp.concatenate([part_b, -part_a], axis=1)
        return (accum + contract(left_re, kre, 0, 0) + contract(left_im, kim, 0, 0), None)

    total, unused = lax.scan(inner, total, sections)
    local_spec = total.astype(jnp.bfloat16)
    scale = 1.0 / math.sqrt(cell_count * lax.axis_size("cells") * freq_size)
    onehot, hidden_in, pre_one, act_one, pre_two, act_two = forward_pass(
        level_codes, cell_params, level_table, w_proj, w_one, b_one, w_two, b_two
    )
    upper, delta_two = upper_grads(local_spec, w_out, act_one, pre_two, act_two)
    lower, grad_params = lower_grads(
        delta_two, w_two, w_one, pre_one, hidden_in, onehot, cell_params, w_proj
    )
    totals = lax.psum(tuple(term * scale for term in upper + lower), ("cells", "freq"))
    return totals + (grad_params,)


def split(value, parts):
    pieces = []
    for _ in range(parts):
        piece = value.astype(BF16)
        pieces.append(piece.astype(F32))
        value = value - piece.astype(F32)
    return pieces


def fetch(sources, buffers, arrived):
    copies = [
        pltpu.make_async_copy(source, buffer, arrived.at[at])
        for at, (source, buffer) in enumerate(zip(sources, buffers))
    ]
    for copy in copies:
        copy.start()
    for copy in copies:
        copy.wait()


def pack_kernel(*refs):
    sources, out_ref, buffers, (rows, arrived) = refs[:7], refs[7], refs[8:15], refs[15:]
    fetch(sources, buffers, arrived)
    adj_ref, x_ref, y_ref, z_ref, assign_ref, codes_ref, params_ref = buffers
    count = x_ref.shape[1]
    cells = codes_ref.shape[1]
    rows[...] = jnp.zeros_like(rows)
    rows[0:2, 0:count] = adj_ref[...]
    at = 2
    for ref in (x_ref, y_ref, z_ref):
        for piece in split(ref[...], 3):
            rows[at : at + 1, 0:count] = piece
            at += 1
    rows[at : at + 1, 0:count] = assign_ref[...].astype(F32)
    out_ref[:, 0:cells] = jnp.concatenate(
        [params_ref[...].astype(F32), jnp.broadcast_to(codes_ref[...].astype(F32), (8, cells))],
        axis=0,
    ).astype(BF16)
    out_ref[:, cells:] = rows[...].T[0:count].astype(BF16)


def weight_kernel(*refs):
    sources, buffers, arrived = refs[:7], refs[14:21], refs[21]
    first_ref, second_ref, bias_ref, back_two_ref, back_one_ref, params_ref, embed_ref = refs[7:14]
    fetch(sources, buffers, arrived)
    table_ref, proj_ref, w1_ref, b1_ref, w2_ref, b2_ref, wo_ref = buffers
    levels, hidden = table_ref.shape
    stack = jnp.concatenate([table_ref[...].astype(F32), proj_ref[...].astype(F32)], axis=0)
    joined = jnp.dot(stack.astype(BF16), w1_ref[...], preferred_element_type=F32)
    used = levels + proj_ref.shape[0]
    pad = jnp.zeros((7, hidden), F32)
    full = 0.5 * jnp.concatenate([joined, b1_ref[...], pad], axis=0)
    rows = jnp.concatenate(split(full, 3), axis=0)
    fill = 128 - rows.shape[0]
    first_ref[...] = jnp.concatenate([rows, jnp.zeros((fill, hidden), F32)], axis=0).T.astype(BF16)
    second_ref[...] = (0.5 * w2_ref[...].astype(F32)).T.astype(BF16)
    bias_ref[...] = jnp.broadcast_to(0.5 * b2_ref[...], (128, hidden)).T
    back_two_ref[...] = (0.5 * wo_ref[...].astype(F32)).astype(BF16)
    back_one_ref[...] = (0.5 * w2_ref[...].astype(F32)).astype(BF16)
    params_ref[...] = jnp.concatenate(split(joined[levels:used], 2), axis=0).astype(BF16)
    triple = jnp.concatenate([stack, jnp.zeros((8, hidden), F32)], axis=0)
    embed_ref[...] = jnp.concatenate(
        [triple, triple, triple, jnp.zeros((fill, hidden), F32)], axis=0
    ).T.astype(BF16)


SINE = (3.1415820121765137, -5.167142868041992, 2.5418989658355713, -0.5546361804008484)
COSINE = (-4.934795379638672, 4.058451175689697, -1.3320938348770142, 0.22008062899112701)


def cell_kernel(
    freq_size, step,
    place_ref, gathered_ref, first_ref, second_ref, bias_ref, back_two_ref, back_one_ref, params_ref,
    sums_ref, grad_params_ref,
    across, where, lift, waves, deltas,
    act_one, act_kept, slope_one, act_two, delta_two, spectra,
):
    chunks, local, width = gathered_ref.shape
    cells = width - 128
    hidden = second_ref.shape[0]
    freqs = back_two_ref.shape[1] // 2
    targets = chunks * local
    me = place_ref[0]
    freq_rank = place_ref[1]
    stride = freq_size * cells

    parts = []
    for chunk in range(chunks):
        parts.append(gathered_ref[chunk ^ me, :, cells:].astype(F32))
    table = jnp.concatenate(parts, axis=0)
    point_x = (table[:, 2:3] + table[:, 3:4]) + table[:, 4:5]
    point_y = (table[:, 5:6] + table[:, 6:7]) + table[:, 7:8]
    point_z = (table[:, 8:9] + table[:, 9:10]) + table[:, 10:11]
    assign = table[:, 11:12]
    wave = (wave_low + (wave_high - wave_low) * assign / (freqs - 1)) * (0.5 / math.pi)
    full = (targets, 128)
    where[0] = jnp.broadcast_to(point_y, full)
    where[1] = jnp.broadcast_to(point_z * point_z, full)
    where[2] = jnp.broadcast_to(wave, full)
    where[3] = jnp.broadcast_to(kernel_gain * point_z, full)
    wide_x = jnp.broadcast_to(point_x, full)
    for lane in range(0, cells, 128):
        index = freq_rank * cells + lane + lax.broadcasted_iota(jnp.int32, (1, 128), 1)
        offset = wide_x - (index % SIDE).astype(F32)
        across[:, lane : lane + 128] = offset * offset
    grid = lax.broadcasted_iota(jnp.int32, (targets, freqs), 1).astype(F32)
    select = jnp.where(assign == grid, 1.0, 0.0)
    part_a = select * table[:, 0:1]
    part_b = select * table[:, 1:2]
    lift[:, 0:targets] = jnp.concatenate([part_a, part_b], axis=1).T.astype(BF16)
    lift[:, targets:] = jnp.concatenate([part_b, -part_a], axis=1).T.astype(BF16)
    sums_ref[...] = jnp.zeros_like(sums_ref)

    per = cells // step
    total = chunks * per
    top = hidden + 2 * freqs
    dot = functools.partial(jnp.dot, preferred_element_type=F32)

    def place(block):
        return block // per, pl.multiple_of(lax.rem(block, per) * step, step)

    def holograms(block, even):
        chunk, start = place(block)
        row = ((chunk * stride + freq_rank * cells) // SIDE).astype(F32)
        for at in range(0, targets, 16):
            here = slice(at, at + 16)
            offset = where[0, here] - row
            rest = offset * offset + where[1, here]
            for lane in range(0, step, 128):
                square = across[here, pl.ds(start + lane, 128)] + rest
                inverse = lax.rsqrt(square)
                turns = where[2, here] * (square * inverse)
                part = turns - jnp.round(turns)
                power = part * part
                sine = part * (((SINE[3] * power + SINE[2]) * power + SINE[1]) * power + SINE[0])
                cosine = (COSINE[2] * power + COSINE[1]) * power + COSINE[0]
                cosine = cosine * power + 1.0
                amplitude = where[3, here] * (inverse * inverse)
                twice = (amplitude + amplitude) * sine
                waves[even, at : at + 16, lane : lane + 128] = (amplitude - twice * sine).astype(BF16)
                waves[even, targets + at : targets + at + 16, lane : lane + 128] = (
                    twice * cosine
                ).astype(BF16)
                yield

    def feature_of(block):
        chunk, start = place(block)
        data = gathered_ref[chunk ^ me, :, pl.ds(start, step)].astype(F32)
        codes = data[8:16]
        steps = lax.broadcasted_iota(jnp.int32, (8, step), 0).astype(F32)
        rows = [
            jnp.where(codes == steps, 1.0, 0.0),
            jnp.where(codes == steps + 8.0, 1.0, 0.0),
            data[0:8],
            jnp.where(steps == 0.0, 1.0, 0.0),
        ]
        return jnp.concatenate(rows, axis=0).astype(BF16)

    def activate(half):
        tanh = jnp.tanh(half)
        gate = 1.0 + tanh
        act = half * gate
        return act.astype(BF16), gate + act * (1.0 - tanh)

    def outer(low, left, right):
        sums_ref[low : low + left.shape[0]] += contract(left, right, 1, 1)

    def lower(block, even):
        chunk, start = place(block)
        feature = feature_of(block)
        delta = delta_two[even]
        back = dot(back_one_ref[...], delta)
        yield
        value = (back * slope_one[even]).astype(BF16)
        deltas[chunk, :, pl.ds(start, step)] = value
        yield
        outer(0, act_kept[even], delta)
        yield
        outer(hidden, spectra[even], act_two[even])
        yield
        outer(top + 32, feature, delta)
        outer(top, feature, value)
        yield

    def upper(block, even):
        spectrum = dot(lift[...], waves[even]).astype(BF16)
        spectra[even] = spectrum
        yield
        act = act_one[even]
        act_kept[even] = act
        half = dot(second_ref[...], act)
        half = half + jnp.concatenate([bias_ref[...]] * (step // 128), axis=1)
        yield
        back = dot(back_two_ref[...], spectrum)
        yield
        act, slope = activate(half)
        act_two[even] = act
        yield
        delta_two[even] = (back * slope).astype(BF16)
        yield

    def begin(block, even):
        feature = feature_of(block)
        rows = [feature] * 3 + [jnp.zeros((32, step), BF16)]
        half = dot(first_ref[...], jnp.concatenate(rows, axis=0))
        yield
        act, slope = activate(half)
        act_one[even] = act
        slope_one[even] = slope
        yield

    stages = (begin, upper, lower)

    def each(at, odd, live=(2, 1, 0)):
        waiting = [stages[lag](at - lag, (odd + lag) % 2) for lag in live]
        points = {2: 5, 1: 5, 0: 2}
        spots = sum(points[lag] for lag in live)
        pieces = (targets // 16) * (step // 128) if 0 in live else 0
        extra = holograms(at, odd)
        done, drawn = 0, 0
        while waiting:
            for stage in list(waiting):
                if next(stage, True) is True:
                    waiting.remove(stage)
                    continue
                done += 1
                while drawn < pieces * done // spots:
                    next(extra)
                    drawn += 1
        if pieces:
            for _ in extra:
                pass

    each(jnp.int32(0), 0, (0,))
    each(jnp.int32(1), 1, (1, 0))

    def run(at, carry):
        each(2 * at, 0)
        each(2 * at + 1, 1)
        return carry

    lax.fori_loop(1, total // 2, run, 0)
    each(jnp.int32(total), 0, (2, 1))
    each(jnp.int32(total + 1), 1, (2,))
    both = jnp.dot(params_ref[...], deltas[me], preferred_element_type=F32)
    grad_params_ref[...] = both[0:8] + both[8:16]


def finish_kernel(
    scale, own_ref, other_ref, embed_ref, w1_ref,
    out_ref, w2_ref, b2_ref, wone_ref, b1_ref, table_ref, proj_ref,
):
    hidden = w1_ref.shape[0]
    top = hidden + out_ref.shape[1]
    levels = table_ref.shape[0]
    used = levels + proj_ref.shape[0]

    def total(low, high):
        return (own_ref[low:high].astype(F32) + other_ref[low:high].astype(F32)) * scale

    w2_ref[...] = total(0, hidden)
    out_ref[...] = total(hidden, top).T
    feature = total(top, top + 32)
    b1_ref[...] = feature[used : used + 1]
    b2_ref[...] = total(top + 32, top + 64)[used : used + 1]
    pieces = split(feature, 3)
    rows = jnp.concatenate(pieces, axis=0).astype(BF16)
    wone_ref[...] = jnp.dot(embed_ref[:, 0:96], rows, preferred_element_type=F32)
    back = contract(rows, w1_ref[...], 1, 1)
    back = (back[0:32] + back[32:64]) + back[64:96]
    table_ref[...] = back[0:levels]
    proj_ref[...] = back[levels:used]


def run_cells(place, gathered, *weights, step, freq_size, local):
    chunks, _, width = gathered.shape
    cells = width - 128
    hidden, out_dim = weights[3].shape
    targets = chunks * local
    vmem = pl.BlockSpec(memory_space=pltpu.VMEM)
    return pl.pallas_call(
        functools.partial(cell_kernel, freq_size, step),
        out_shape=(
            jax.ShapeDtypeStruct((hidden + out_dim + 64, hidden), F32),
            jax.ShapeDtypeStruct((weights[5].shape[0] // 2, cells), F32),
        ),
        in_specs=[pl.BlockSpec(memory_space=pltpu.SMEM)] + [vmem] * 7,
        out_specs=(vmem, vmem),
        scratch_shapes=[
            pltpu.VMEM((targets, cells), F32),
            pltpu.VMEM((4, targets, 128), F32),
            pltpu.VMEM((out_dim, 2 * targets), BF16),
            pltpu.VMEM((2, 2 * targets, step), BF16),
            pltpu.VMEM((chunks, hidden, cells), BF16),
            pltpu.VMEM((2, hidden, step), BF16),
            pltpu.VMEM((2, hidden, step), BF16),
            pltpu.VMEM((2, hidden, step), F32),
            pltpu.VMEM((2, hidden, step), BF16),
            pltpu.VMEM((2, hidden, step), BF16),
            pltpu.VMEM((2, out_dim, step), BF16),
        ],
        compiler_params=pltpu.CompilerParams(vmem_limit_bytes=VMEM_BYTES),
        name="all_cells",
    )(place, gathered, *weights)


def small_body(
    adjoint,
    target_x,
    target_y,
    target_z,
    assignment,
    level_codes,
    cell_params,
    level_table,
    w_proj,
    w_one,
    b_one,
    w_two,
    b_two,
    w_out,
):
    cells = level_codes.shape[0]
    local = target_x.shape[0]
    levels, hidden = level_table.shape
    props = w_proj.shape[0]
    freqs = w_out.shape[1] // 2
    chunks = lax.axis_size("cells")
    freq_size = lax.axis_size("freq")
    shape = jax.ShapeDtypeStruct
    params = pltpu.CompilerParams(vmem_limit_bytes=VMEM_BYTES)

    def fetched(arrays):
        buffers = [pltpu.VMEM(array.shape, array.dtype) for array in arrays]
        return buffers, pltpu.SemaphoreType.DMA((len(arrays),))

    inputs = (
        adjoint, target_x[None, :], target_y[None, :], target_z[None, :], assignment[None, :],
        level_codes[None, :], cell_params,
    )
    buffers, arrived = fetched(inputs)
    packed = pl.pallas_call(
        pack_kernel,
        out_shape=shape((16, cells + 128), BF16),
        in_specs=[pl.BlockSpec(memory_space=pltpu.HBM)] * len(inputs),
        scratch_shapes=buffers + [pltpu.VMEM((128, 128), F32), arrived],
        compiler_params=pltpu.CompilerParams(vmem_limit_bytes=WHOLE_VMEM),
        name="pack_inputs",
    )(*inputs)
    gathered = packed[None]
    reach = 1
    while reach < chunks:
        moved = lax.ppermute(gathered, "cells", [(at, at ^ reach) for at in range(chunks)])
        gathered = jnp.concatenate([gathered, moved], axis=0)
        reach *= 2

    inputs = (level_table, w_proj, w_one, b_one[None, :], w_two, b_two[None, :], w_out)
    buffers, arrived = fetched(inputs)
    first, second, bias, back_two, back_one, proj_rows, embed = pl.pallas_call(
        weight_kernel,
        in_specs=[pl.BlockSpec(memory_space=pltpu.HBM)] * len(inputs),
        scratch_shapes=buffers + [arrived],
        out_shape=(
            shape((hidden, 128), BF16),
            shape((hidden, hidden), BF16),
            shape((hidden, 128), F32),
            shape((hidden, 2 * freqs), BF16),
            shape((hidden, hidden), BF16),
            shape((2 * props, hidden), BF16),
            shape((hidden, 128), BF16),
        ),
        compiler_params=pltpu.CompilerParams(vmem_limit_bytes=WHOLE_VMEM),
        name="prepare_weights",
    )(*inputs)

    place = jnp.stack([lax.axis_index("cells"), lax.axis_index("freq")]).astype(jnp.int32)
    sums, grad_params = run_cells(
        place, gathered, first, second, bias, back_two, back_one, proj_rows,
        step=min(512, cells), freq_size=freq_size, local=local,
    )

    other = lax.ppermute(sums, "freq", [(at, at ^ 1) for at in range(freq_size)])
    scale = 1.0 / math.sqrt(cells * chunks * freq_size)
    grad_out, grad_w2, grad_b2, grad_w1, grad_b1, grad_table, grad_proj = pl.pallas_call(
        functools.partial(finish_kernel, scale),
        out_shape=(
            shape((hidden, 2 * freqs), F32),
            shape((hidden, hidden), F32),
            shape((1, hidden), F32),
            shape((hidden, hidden), F32),
            shape((1, hidden), F32),
            shape((levels, hidden), F32),
            shape((props, hidden), F32),
        ),
        compiler_params=params,
        name="finish_sums",
    )(sums, other, embed, w_one)
    return (
        grad_out, grad_w2, grad_b2[0], grad_w1, grad_b1[0], grad_table, grad_proj, grad_params,
    )


def solution(mesh):
    chunks = mesh.shape["cells"]
    paired = mesh.shape["freq"] == 2 and chunks & (chunks - 1) == 0

    def body(*args):
        local = args[1].shape[0]
        cells = args[5].shape[0]
        hidden = args[9].shape[0]
        suits = (
            paired
            and local == 16
            and cells % 256 == 0
            and chunks * cells * chunks * local <= 1 << 20
            and args[7].shape[0] == 16
            and args[8].shape[0] == 8
            and hidden % 128 == 0
            and mesh.shape["freq"] * cells % SIDE == 0
            and SIDE % cells == 0
            and args[13].shape[1] == 128
        )
        return (small_body if suits else general_body)(*args)

    placed = (
        P(None, ("groups", "cells")),
        P(("groups", "cells")),
        P(("groups", "cells")),
        P(("groups", "cells")),
        P(("groups", "cells")),
        P(("groups", "cells", "freq")),
        P(None, ("groups", "cells", "freq")),
        P(),
        P(),
        P(),
        P(),
        P(),
        P(),
        P(),
    )
    return jax.shard_map(
        body,
        mesh=mesh,
        in_specs=placed,
        out_specs=(
            P("groups", None),
            P("groups", None),
            P("groups"),
            P("groups", None),
            P("groups"),
            P("groups", None),
            P("groups", None),
            P(None, ("groups", "cells", "freq")),
        ),
        check_vma=False,
    )
```

```python
import functools
import math

import jax
import jax.numpy as jnp
from jax import lax
from jax.experimental import pallas as pl
from jax.experimental.pallas import tpu as pltpu
from jax.sharding import PartitionSpec as P

SIDE = 1024

wave_low = 1.0
wave_high = 3.0
kernel_gain = 150.0

F32 = jnp.float32
BF16 = jnp.bfloat16
VMEM_BYTES = 40 * 1024 * 1024
WHOLE_VMEM = 64 * 1024 * 1024 - 256 * 1024


def silu_slope(value):
    sigma = jax.nn.sigmoid(value)
    return sigma * (1.0 + value * (1.0 - sigma))


def contract(left, right, left_dim, right_dim):
    return lax.dot_general(
        left, right, (((left_dim,), (right_dim,)), ((), ())), preferred_element_type=jnp.float32
    )


def kernel_tile(point_x, point_y, point_z, freq_value, cell_col, cell_row, count_freq):
    wave = wave_low + (wave_high - wave_low) * freq_value / (count_freq - 1)
    offset_x = point_x[:, None] - cell_col[None, :]
    offset_y = point_y[:, None] - cell_row[None, :]
    square = offset_x * offset_x + offset_y * offset_y + (point_z * point_z)[:, None]
    distance = jnp.sqrt(square)
    amplitude = kernel_gain * point_z[:, None] / square
    phase = wave[:, None] * distance
    return (
        (amplitude * jnp.cos(phase)).astype(jnp.bfloat16),
        (amplitude * jnp.sin(phase)).astype(jnp.bfloat16),
    )


def forward_pass(level_codes, cell_params, level_table, w_proj, w_one, b_one, w_two, b_two):
    levels = level_table.shape[0]
    onehot = (level_codes[:, None] == jnp.arange(levels, dtype=jnp.int32)[None, :]).astype(
        jnp.bfloat16
    )
    hidden_in = (
        jnp.dot(onehot, level_table, preferred_element_type=jnp.float32)
        + contract(cell_params, w_proj, 0, 0)
    ).astype(jnp.bfloat16)
    pre_one = jnp.dot(hidden_in, w_one, preferred_element_type=jnp.float32) + b_one
    act_one = jax.nn.silu(pre_one).astype(jnp.bfloat16)
    pre_two = jnp.dot(act_one, w_two, preferred_element_type=jnp.float32) + b_two
    act_two = jax.nn.silu(pre_two).astype(jnp.bfloat16)
    return (onehot, hidden_in, pre_one, act_one, pre_two, act_two)


def upper_grads(spectra, w_out, act_one, pre_two, act_two):
    back_two = contract(spectra, w_out, 0, 1)
    delta_two = (back_two * silu_slope(pre_two)).astype(jnp.bfloat16)
    grad_out = contract(act_two, spectra, 0, 1)
    grad_w2 = contract(act_one, delta_two, 0, 0)
    grad_b2 = jnp.sum(delta_two.astype(jnp.float32), axis=0)
    return ((grad_out, grad_w2, grad_b2), delta_two)


def lower_grads(delta_two, w_two, w_one, pre_one, hidden_in, onehot, cell_params, w_proj):
    back_one = contract(delta_two, w_two, 1, 1)
    delta_one = (back_one * silu_slope(pre_one)).astype(jnp.bfloat16)
    grad_w1 = contract(hidden_in, delta_one, 0, 0)
    grad_b1 = jnp.sum(delta_one.astype(jnp.float32), axis=0)
    back_zero = contract(delta_one, w_one, 1, 1).astype(jnp.bfloat16)
    grad_table = contract(onehot, back_zero, 0, 0)
    grad_proj = contract(cell_params, back_zero, 1, 0)
    grad_params = contract(w_proj, back_zero, 1, 1)
    return ((grad_w1, grad_b1, grad_table, grad_proj), grad_params)


def general_body(
    adjoint,
    target_x,
    target_y,
    target_z,
    assignment,
    level_codes,
    cell_params,
    level_table,
    w_proj,
    w_one,
    b_one,
    w_two,
    b_two,
    w_out,
):
    cell_count = level_codes.shape[0]
    freq_count = w_out.shape[1] // 2
    freq_size = lax.axis_size("freq")
    cell_rank = lax.axis_index("cells")
    freq_rank = lax.axis_index("freq")
    first_cell = (cell_rank * freq_size + freq_rank) * cell_count
    index = first_cell + jnp.arange(cell_count, dtype=jnp.int32)
    cell_col = (index % SIDE).astype(jnp.float32)
    cell_row = (index // SIDE).astype(jnp.float32)
    freq_grid = jnp.arange(freq_count, dtype=jnp.int32).astype(jnp.float32)
    stacked = jnp.concatenate(
        [
            adjoint,
            target_x[None, :],
            target_y[None, :],
            target_z[None, :],
            assignment.astype(jnp.float32)[None, :],
        ],
        axis=0,
    )
    total = jnp.zeros((2 * freq_count, cell_count), jnp.float32)
    piece = lax.all_gather(stacked, "cells", axis=1, tiled=True)
    length = piece.shape[1]
    block_len = math.gcd(length, 256)
    sections = piece.reshape(6, length // block_len, block_len).transpose(1, 0, 2)

    def inner(accum, rows):
        adj_round = rows[0:2].astype(jnp.bfloat16)
        kre, kim = kernel_tile(rows[2], rows[3], rows[4], rows[5], cell_col, cell_row, freq_count)
        select = (rows[5][:, None] == freq_grid[None, :]).astype(jnp.bfloat16)
        part_a = select * adj_round[0][:, None]
        part_b = select * adj_round[1][:, None]
        left_re = jnp.concatenate([part_a, part_b], axis=1)
        left_im = jnp.concatenate([part_b, -part_a], axis=1)
        return (accum + contract(left_re, kre, 0, 0) + contract(left_im, kim, 0, 0), None)

    total, unused = lax.scan(inner, total, sections)
    local_spec = total.astype(jnp.bfloat16)
    scale = 1.0 / math.sqrt(cell_count * lax.axis_size("cells") * freq_size)
    onehot, hidden_in, pre_one, act_one, pre_two, act_two = forward_pass(
        level_codes, cell_params, level_table, w_proj, w_one, b_one, w_two, b_two
    )
    upper, delta_two = upper_grads(local_spec, w_out, act_one, pre_two, act_two)
    lower, grad_params = lower_grads(
        delta_two, w_two, w_one, pre_one, hidden_in, onehot, cell_params, w_proj
    )
    totals = lax.psum(tuple(term * scale for term in upper + lower), ("cells", "freq"))
    return totals + (grad_params,)


def split(value, parts):
    pieces = []
    for _ in range(parts):
        piece = value.astype(BF16)
        pieces.append(piece.astype(F32))
        value = value - piece.astype(F32)
    return pieces


def fetch(sources, buffers, arrived):
    copies = [
        pltpu.make_async_copy(source, buffer, arrived.at[at])
        for at, (source, buffer) in enumerate(zip(sources, buffers))
    ]
    for copy in copies:
        copy.start()
    for copy in copies:
        copy.wait()


def pack_kernel(*refs):
    sources, out_ref, buffers, (rows, arrived) = refs[:7], refs[7], refs[8:15], refs[15:]
    fetch(sources, buffers, arrived)
    adj_ref, x_ref, y_ref, z_ref, assign_ref, codes_ref, params_ref = buffers
    cells = codes_ref.shape[1]
    pieces = [adj_ref[0:1], adj_ref[1:2]]
    for ref in (x_ref, y_ref, z_ref):
        pieces += split(ref[...], 3)
    pieces.append(assign_ref[...].astype(F32))
    pieces += [jnp.zeros_like(pieces[0])] * 4
    codes = codes_ref[...].astype(F32)
    for at in range(4):
        rows[at : at + 1] = codes[:, at * 128 : (at + 1) * 128]
    rows[4:5] = jnp.concatenate(pieces[0:8], axis=1)
    rows[5:6] = jnp.concatenate(pieces[8:16], axis=1)
    rows[6:8] = jnp.zeros((2, 128), F32)
    out_ref[:, 0:cells] = params_ref[...]
    out_ref[:, cells:] = rows[...].astype(BF16)


def stage_kernel(packed_ref, out_ref):
    out_ref[...] = packed_ref[...]


def weight_kernel(joint_ref, embed_ref, bias_ref, out_ref):
    hidden = joint_ref.shape[0]
    used = embed_ref.shape[0]
    stack = embed_ref[...]
    joined = jnp.dot(stack, joint_ref[:, 0:hidden], preferred_element_type=F32)
    joined = jnp.concatenate([joined, bias_ref[0:1], jnp.zeros((7, hidden), F32)], axis=0)
    shifts = split(0.5 * bias_ref[1:2], 3)
    rows = split(0.5 * joined, 3) + shifts + [jnp.zeros((29, hidden), F32)]
    out_ref[:, 0:128] = jnp.concatenate(rows, axis=0).T.astype(BF16)
    second = joint_ref[:, hidden : 2 * hidden].astype(F32)
    out_ref[:, 128 : 128 + hidden] = (0.5 * second).T.astype(BF16)
    filled = [stack.astype(F32), jnp.zeros((8, hidden), F32)]
    rows = filled * 3 + [jnp.zeros((32, hidden), F32)]
    out_ref[:, 128 + hidden :] = jnp.concatenate(rows, axis=0).T.astype(BF16)


SINE = (3.1415820121765137, -5.167142868041992, 2.5418989658355713, -0.5546361804008484)
COSINE = (-4.934795379638672, 4.058451175689697, -1.3320938348770142, 0.22008062899112701)


def dot(left, right):
    return jnp.dot(left, right, preferred_element_type=F32)


def feature_of(gathered_ref, slot):
    width = gathered_ref.shape[2]
    cells = width - 128
    rows = gathered_ref[slot, :, cells:].astype(F32)
    codes = jnp.concatenate(
        [jnp.broadcast_to(rows[at : at + 1], (8, 128)) for at in range(4)], axis=1
    )
    steps = lax.broadcasted_iota(jnp.int32, (8, cells), 0).astype(F32)
    blocks = [
        jnp.where(codes == steps, 1.0, 0.0),
        jnp.where(codes == steps + 8.0, 1.0, 0.0),
        gathered_ref[slot, :, 0:cells].astype(F32),
        jnp.where(steps == 0.0, 1.0, 0.0),
    ]
    return jnp.concatenate(blocks, axis=0).astype(BF16)


def activate(half):
    tanh = jnp.tanh(half)
    gate = 1.0 + tanh
    act = half * gate
    return act.astype(BF16), gate + act * (1.0 - tanh)


def layer_one(weights_ref, feature):
    rows = [feature] * 3 + [jnp.zeros((32, feature.shape[1]), BF16)]
    return dot(weights_ref[:, 0:128], jnp.concatenate(rows, axis=0))


def bias_of(weights_ref):
    shift = weights_ref[:, 96:128].astype(F32)
    shift = (shift[:, 0:1] + shift[:, 1:2]) + shift[:, 2:3]
    return jnp.broadcast_to(shift, (shift.shape[0], 128))


def forward_kernel(gathered_ref, weights_ref, one_ref, slope_one_ref, two_ref, slope_two_ref, bias):
    count, hidden, cells = one_ref.shape
    bias[...] = bias_of(weights_ref)
    wide = jnp.concatenate([bias[...]] * (cells // 128), axis=1)

    def first(slot):
        act, slope = activate(layer_one(weights_ref, feature_of(gathered_ref, slot)))
        one_ref[slot] = act
        slope_one_ref[slot] = slope

    def second(slot):
        half = dot(weights_ref[:, 128 : 128 + hidden], one_ref[slot]) + wide
        act, slope = activate(half)
        two_ref[slot] = act
        slope_two_ref[slot] = slope

    first(0)
    for slot in range(1, count):
        second(slot - 1)
        first(slot)
    second(count - 1)


def cell_kernel(
    freq_size,
    place_ref, gathered_ref, weights_ref, joint_ref,
    one_ref, slope_one_ref, two_ref, slope_two_ref,
    sums_ref, grad_params_ref,
    across, where, lift, bias, totals, waves, deltas,
    act_one, act_kept, slope_one, act_two, delta_two, spectra,
):
    chunks, _, width = gathered_ref.shape
    cells = width - 128
    hidden = joint_ref.shape[0]
    freqs = (joint_ref.shape[1] - 2 * hidden) // 2
    w2_ref = joint_ref.at[:, hidden : 2 * hidden]
    wo_ref = joint_ref.at[:, 2 * hidden :]
    targets = chunks * 16
    me = place_ref[0]
    freq_rank = place_ref[1]
    stride = freq_size * cells
    second_ref = weights_ref.at[:, 128 : 128 + hidden]

    rows = [gathered_ref[chunk ^ me, :, cells:].astype(F32) for chunk in range(chunks)]
    low = jnp.concatenate([row[4:5] for row in rows], axis=0).T
    high = jnp.concatenate([row[5:6] for row in rows], axis=0).T
    parts = [low[at * 16 : (at + 1) * 16] for at in range(8)]
    parts += [high[at * 16 : (at + 1) * 16] for at in range(4)]
    point_x = (parts[2] + parts[3]) + parts[4]
    point_y = (parts[5] + parts[6]) + parts[7]
    point_z = (parts[8] + parts[9]) + parts[10]
    wave = (wave_low + (wave_high - wave_low) * parts[11] / (freqs - 1)) * (0.5 / math.pi)
    sides = [
        freq_rank * cells + lane + lax.broadcasted_iota(jnp.int32, (1, 128), 1)
        for lane in range(0, cells, 128)
    ]
    sides = [lax.rem(side, SIDE).astype(F32) for side in sides]
    grid = lax.broadcasted_iota(jnp.int32, (16, freqs), 1).astype(F32)
    near, far = [], []
    for chunk in range(chunks):
        here = slice(chunk * 16, chunk * 16 + 16)

        def spread(value):
            return jnp.broadcast_to(value[:, chunk : chunk + 1], (16, 128))

        where[0, here] = spread(point_y)
        where[1, here] = spread(point_z * point_z)
        where[2, here] = spread(wave)
        where[3, here] = spread(kernel_gain * point_z)
        wide = spread(point_x)
        for at, side in enumerate(sides):
            offset = wide - side
            across[here, at * 128 : (at + 1) * 128] = offset * offset
        select = jnp.where(spread(parts[11])[:, 0:freqs] == grid, 1.0, 0.0)
        part_a = select * spread(parts[0])[:, 0:freqs]
        part_b = select * spread(parts[1])[:, 0:freqs]
        near.append(jnp.concatenate([part_a, part_b], axis=1))
        far.append(jnp.concatenate([part_b, -part_a], axis=1))
    lift[:, 0:targets] = jnp.concatenate(near, axis=0).T.astype(BF16)
    lift[:, targets:] = jnp.concatenate(far, axis=0).T.astype(BF16)
    bias[...] = bias_of(weights_ref)
    totals[...] = jnp.zeros_like(totals)

    top = hidden + 2 * freqs
    ready = one_ref.shape[0]

    def place(block):
        slot = (block // ready) * ready + lax.bitwise_and(lax.bitwise_xor(me, block), ready - 1)
        return slot, lax.bitwise_xor(slot, me)

    def holograms(block, even):
        chunk = place(block)[1]
        row = ((chunk * stride + freq_rank * cells) // SIDE).astype(F32)
        for at in range(0, targets, 16):
            here = slice(at, at + 16)
            offset = where[0, here] - row
            rest = offset * offset + where[1, here]
            for lane in range(0, cells, 128):
                square = across[here, lane : lane + 128] + rest
                inverse = lax.rsqrt(square)
                turns = where[2, here] * (square * inverse)
                part = turns - jnp.round(turns)
                power = part * part
                sine = part * (((SINE[3] * power + SINE[2]) * power + SINE[1]) * power + SINE[0])
                cosine = (COSINE[2] * power + COSINE[1]) * power + COSINE[0]
                cosine = cosine * power + 1.0
                amplitude = where[3, here] * (inverse * inverse)
                twice = (amplitude + amplitude) * sine
                waves[even, at : at + 16, lane : lane + 128] = (amplitude - twice * sine).astype(BF16)
                waves[even, targets + at : targets + at + 16, lane : lane + 128] = (
                    twice * cosine
                ).astype(BF16)
                yield

    def kept(block, even):
        if block < ready:
            slot = place(block)[0]
            refs = (one_ref, slope_one_ref, two_ref, slope_two_ref)
            return [ref.at[slot] for ref in refs]
        return act_kept.at[even], slope_one.at[even], act_two.at[even], None

    def lower(block, even):
        slot, chunk = place(block)
        total = totals.at[chunk // ready]

        def outer(low, left, right):
            total[low : low + left.shape[0]] += contract(left, right, 1, 1)

        one, slope, two, _ = kept(block, even)
        feature = feature_of(gathered_ref, slot)
        delta = delta_two[even]
        back = dot(w2_ref[...], delta)
        yield
        value = (back * slope[...]).astype(BF16)
        deltas[chunk] = value
        yield
        outer(0, one[...], delta)
        yield
        outer(hidden, spectra[even], two[...])
        yield
        outer(top + 32, feature, delta)
        outer(top, feature, value)
        yield

    def upper(block, even):
        spectrum = dot(lift[...], waves[even]).astype(BF16)
        spectra[even] = spectrum
        yield
        if block < ready:
            back = dot(wo_ref[...], spectrum)
            yield
            delta_two[even] = (back * kept(block, even)[3][...]).astype(BF16)
            yield
            return
        act = act_one[even]
        act_kept[even] = act
        half = dot(second_ref[...], act)
        half = half + jnp.concatenate([bias[...]] * (cells // 128), axis=1)
        yield
        back = dot(wo_ref[...], spectrum)
        yield
        act, slope = activate(half)
        act_two[even] = act
        yield
        delta_two[even] = (back * slope).astype(BF16)
        yield

    def begin(block, even):
        if block >= ready:
            half = layer_one(weights_ref, feature_of(gathered_ref, place(block)[0]))
            yield
            act, slope = activate(half)
            act_one[even] = act
            slope_one[even] = slope
            yield

    stages = (begin, upper, lower)
    for at in range(chunks + 2):
        live = [lag for lag in (2, 1, 0) if 0 <= at - lag < chunks]
        waiting = [stages[lag](at - lag, (at - lag) % 2) for lag in live]
        spots = sum(5 if lag == 2 else ((5, 3), (2, 0))[1 - lag][at - lag < ready] for lag in live)
        pieces = (targets // 16) * (cells // 128) if 0 in live else 0
        extra = holograms(at, at % 2)
        done, drawn = 0, 0
        while waiting:
            for stage in list(waiting):
                if next(stage, True) is True:
                    waiting.remove(stage)
                    continue
                done += 1
                while drawn < pieces * done // spots:
                    next(extra)
                    drawn += 1
        if pieces:
            for _ in extra:
                pass
    both = contract(weights_ref[:, 0:128], deltas[me], 0, 0)
    grad_params_ref[...] = 0.5 * ((both[16:24] + both[48:56]) + both[80:88])
    sums_ref[...] = (totals[0] + totals[1]).astype(BF16)


def finish_kernel(
    scale, own_ref, other_ref, weights_ref, joint_ref,
    out_ref, w2_ref, b2_ref, wone_ref, b1_ref, table_ref, proj_ref,
):
    hidden = joint_ref.shape[0]
    top = hidden + out_ref.shape[1]
    levels = table_ref.shape[0]
    used = levels + proj_ref.shape[0]

    def total(low, high, factor):
        both = own_ref[low:high].astype(F32) + other_ref[low:high].astype(F32)
        return both * (scale * factor)

    w2_ref[...] = total(0, hidden, 0.5)
    out_ref[...] = total(hidden, top, 1.0).T
    feature = total(top, top + 32, 0.25)
    b1_ref[...] = feature[used : used + 1]
    b2_ref[...] = total(top + 32, top + 64, 0.5)[used : used + 1]
    rows = jnp.concatenate(split(feature, 3), axis=0).astype(BF16)
    embed = weights_ref[:, 128 + hidden : 128 + hidden + 96]
    wone_ref[...] = jnp.dot(embed, rows, preferred_element_type=F32)
    back = contract(rows, joint_ref[:, 0:hidden], 1, 1)
    back = (back[0:32] + back[32:64]) + back[64:96]
    table_ref[...] = back[0:levels]
    proj_ref[...] = back[levels:used]


def run_forward(gathered, weights):
    count, _, width = gathered.shape
    hidden = weights.shape[0]
    block = (count, hidden, width - 128)
    return pl.pallas_call(
        forward_kernel,
        out_shape=[jax.ShapeDtypeStruct(block, kind) for kind in (BF16, F32, BF16, F32)],
        scratch_shapes=[pltpu.VMEM((hidden, 128), F32)],
        compiler_params=pltpu.CompilerParams(vmem_limit_bytes=VMEM_BYTES),
        name="early_forward",
    )(gathered, weights)


def run_cells(place, gathered, weights, joint, early, freq_size):
    chunks, props, width = gathered.shape
    cells = width - 128
    hidden = joint.shape[0]
    out_dim = joint.shape[1] - 2 * hidden
    targets = chunks * 16
    vmem = pl.BlockSpec(memory_space=pltpu.VMEM)
    return pl.pallas_call(
        functools.partial(cell_kernel, freq_size),
        out_shape=(
            jax.ShapeDtypeStruct((hidden + out_dim + 64, hidden), BF16),
            jax.ShapeDtypeStruct((props, cells), F32),
        ),
        in_specs=[pl.BlockSpec(memory_space=pltpu.SMEM)] + [vmem] * 7,
        out_specs=(vmem, vmem),
        scratch_shapes=[
            pltpu.VMEM((targets, cells), F32),
            pltpu.VMEM((4, targets, 128), F32),
            pltpu.VMEM((out_dim, 2 * targets), BF16),
            pltpu.VMEM((hidden, 128), F32),
            pltpu.VMEM((2, hidden + out_dim + 64, hidden), F32),
            pltpu.VMEM((2, 2 * targets, cells), BF16),
            pltpu.VMEM((chunks, hidden, cells), BF16),
            pltpu.VMEM((2, hidden, cells), BF16),
            pltpu.VMEM((2, hidden, cells), BF16),
            pltpu.VMEM((2, hidden, cells), F32),
            pltpu.VMEM((2, hidden, cells), BF16),
            pltpu.VMEM((2, hidden, cells), BF16),
            pltpu.VMEM((2, out_dim, cells), BF16),
        ],
        compiler_params=pltpu.CompilerParams(vmem_limit_bytes=VMEM_BYTES),
        name="all_cells",
    )(place, gathered, weights, joint, *early)


def small_body(
    adjoint,
    target_x,
    target_y,
    target_z,
    assignment,
    level_codes,
    cell_params,
    level_table,
    w_proj,
    w_one,
    b_one,
    w_two,
    b_two,
    w_out,
):
    cells = level_codes.shape[0]
    local = target_x.shape[0]
    levels, hidden = level_table.shape
    props = w_proj.shape[0]
    freqs = w_out.shape[1] // 2
    chunks = lax.axis_size("cells")
    freq_size = lax.axis_size("freq")
    shape = jax.ShapeDtypeStruct
    params = pltpu.CompilerParams(vmem_limit_bytes=VMEM_BYTES)

    def fetched(arrays):
        buffers = [pltpu.VMEM(array.shape, array.dtype) for array in arrays]
        return buffers, pltpu.SemaphoreType.DMA((len(arrays),))

    inputs = (
        adjoint, target_x[None, :], target_y[None, :], target_z[None, :], assignment[None, :],
        level_codes[None, :], cell_params,
    )
    whole = pltpu.CompilerParams(vmem_limit_bytes=WHOLE_VMEM)
    buffers, arrived = fetched(inputs)
    packed = pl.pallas_call(
        pack_kernel,
        out_shape=shape((props, cells + 128), BF16),
        in_specs=[pl.BlockSpec(memory_space=pltpu.HBM)] * len(inputs),
        scratch_shapes=buffers + [pltpu.VMEM((8, 128), F32), arrived],
        compiler_params=whole,
        name="pack_inputs",
    )(*inputs)
    staged = pl.pallas_call(
        stage_kernel,
        out_shape=shape((props, cells + 128), BF16),
        compiler_params=params,
        name="stage_own",
    )(packed)
    moved = lax.ppermute(packed[None], "cells", [(at, at ^ 1) for at in range(chunks)])
    embed = jnp.concatenate([level_table, w_proj], axis=0)
    biases = jnp.concatenate([b_one[None, :], b_two[None, :]], axis=0)
    gathered = jnp.concatenate([staged[None], moved], axis=0)
    gathered, embed, biases, w_one, w_two, w_out = lax.optimization_barrier(
        (gathered, embed, biases, w_one, w_two, w_out)
    )
    joint = jnp.concatenate([w_one, w_two, w_out], axis=1)
    weights = pl.pallas_call(
        weight_kernel,
        out_shape=shape((hidden, 256 + hidden), BF16),
        compiler_params=params,
        name="prepare_weights",
    )(joint, embed, biases)
    reach = 2
    while reach < chunks:
        moved = lax.ppermute(gathered, "cells", [(at, at ^ reach) for at in range(chunks)])
        if 2 * reach == chunks:
            early = run_forward(gathered, weights)
        gathered = jnp.concatenate([gathered, moved], axis=0)
        gathered, weights = lax.optimization_barrier((gathered, weights))
        reach *= 2

    place = jnp.stack([lax.axis_index("cells"), lax.axis_index("freq")]).astype(jnp.int32)
    sums, grad_params = run_cells(place, gathered, weights, joint, early, freq_size)

    other = lax.ppermute(sums, "freq", [(at, at ^ 1) for at in range(freq_size)])
    scale = 1.0 / math.sqrt(cells * chunks * freq_size)
    grad_out, grad_w2, grad_b2, grad_w1, grad_b1, grad_table, grad_proj = pl.pallas_call(
        functools.partial(finish_kernel, scale),
        out_shape=(
            shape((hidden, 2 * freqs), F32),
            shape((hidden, hidden), F32),
            shape((1, hidden), F32),
            shape((hidden, hidden), F32),
            shape((1, hidden), F32),
            shape((levels, hidden), F32),
            shape((props, hidden), F32),
        ),
        compiler_params=params,
        name="finish_sums",
    )(sums, other, weights, joint)
    return (
        grad_out, grad_w2, grad_b2[0], grad_w1, grad_b1[0], grad_table, grad_proj, grad_params,
    )


def solution(mesh):
    chunks = mesh.shape["cells"]
    paired = mesh.shape["freq"] == 2 and chunks > 2 and chunks & (chunks - 1) == 0

    def body(*args):
        local = args[1].shape[0]
        cells = args[5].shape[0]
        hidden = args[9].shape[0]
        suits = (
            paired
            and local == 16
            and cells == 512
            and chunks * cells * chunks * local <= 1 << 20
            and args[7].shape[0] == 16
            and args[8].shape[0] == 8
            and hidden % 128 == 0
            and mesh.shape["freq"] * cells % SIDE == 0
            and SIDE % cells == 0
            and args[13].shape[1] == 128
        )
        return (small_body if suits else general_body)(*args)

    placed = (
        P(None, ("groups", "cells")),
        P(("groups", "cells")),
        P(("groups", "cells")),
        P(("groups", "cells")),
        P(("groups", "cells")),
        P(("groups", "cells", "freq")),
        P(None, ("groups", "cells", "freq")),
        P(),
        P(),
        P(),
        P(),
        P(),
        P(),
        P(),
    )
    return jax.shard_map(
        body,
        mesh=mesh,
        in_specs=placed,
        out_specs=(
            P("groups", None),
            P("groups", None),
            P("groups"),
            P("groups", None),
            P("groups"),
            P("groups", None),
            P("groups", None),
            P(None, ("groups", "cells", "freq")),
        ),
        check_vma=False,
    )
```

```python
import functools
import math

import jax
import jax.numpy as jnp
from jax import lax
from jax.experimental import pallas as pl
from jax.experimental.pallas import tpu as pltpu
from jax.sharding import PartitionSpec as P

SIDE = 1024

wave_low = 1.0
wave_high = 3.0
kernel_gain = 150.0

F32 = jnp.float32
BF16 = jnp.bfloat16
VMEM_BYTES = 40 * 1024 * 1024
SMALL_ROWS = 32
WHOLE_VMEM = 64 * 1024 * 1024 - 256 * 1024


def silu_slope(value):
    sigma = jax.nn.sigmoid(value)
    return sigma * (1.0 + value * (1.0 - sigma))


def contract(left, right, left_dim, right_dim):
    return lax.dot_general(
        left, right, (((left_dim,), (right_dim,)), ((), ())), preferred_element_type=jnp.float32
    )


def kernel_tile(point_x, point_y, point_z, freq_value, cell_col, cell_row, count_freq):
    wave = wave_low + (wave_high - wave_low) * freq_value / (count_freq - 1)
    offset_x = point_x[:, None] - cell_col[None, :]
    offset_y = point_y[:, None] - cell_row[None, :]
    square = offset_x * offset_x + offset_y * offset_y + (point_z * point_z)[:, None]
    distance = jnp.sqrt(square)
    amplitude = kernel_gain * point_z[:, None] / square
    phase = wave[:, None] * distance
    return (
        (amplitude * jnp.cos(phase)).astype(jnp.bfloat16),
        (amplitude * jnp.sin(phase)).astype(jnp.bfloat16),
    )


def forward_pass(level_codes, cell_params, level_table, w_proj, w_one, b_one, w_two, b_two):
    levels = level_table.shape[0]
    onehot = (level_codes[:, None] == jnp.arange(levels, dtype=jnp.int32)[None, :]).astype(
        jnp.bfloat16
    )
    hidden_in = (
        jnp.dot(onehot, level_table, preferred_element_type=jnp.float32)
        + contract(cell_params, w_proj, 0, 0)
    ).astype(jnp.bfloat16)
    pre_one = jnp.dot(hidden_in, w_one, preferred_element_type=jnp.float32) + b_one
    act_one = jax.nn.silu(pre_one).astype(jnp.bfloat16)
    pre_two = jnp.dot(act_one, w_two, preferred_element_type=jnp.float32) + b_two
    act_two = jax.nn.silu(pre_two).astype(jnp.bfloat16)
    return (onehot, hidden_in, pre_one, act_one, pre_two, act_two)


def upper_grads(spectra, w_out, act_one, pre_two, act_two):
    back_two = contract(spectra, w_out, 0, 1)
    delta_two = (back_two * silu_slope(pre_two)).astype(jnp.bfloat16)
    grad_out = contract(act_two, spectra, 0, 1)
    grad_w2 = contract(act_one, delta_two, 0, 0)
    grad_b2 = jnp.sum(delta_two.astype(jnp.float32), axis=0)
    return ((grad_out, grad_w2, grad_b2), delta_two)


def lower_grads(delta_two, w_two, w_one, pre_one, hidden_in, onehot, cell_params, w_proj):
    back_one = contract(delta_two, w_two, 1, 1)
    delta_one = (back_one * silu_slope(pre_one)).astype(jnp.bfloat16)
    grad_w1 = contract(hidden_in, delta_one, 0, 0)
    grad_b1 = jnp.sum(delta_one.astype(jnp.float32), axis=0)
    back_zero = contract(delta_one, w_one, 1, 1).astype(jnp.bfloat16)
    grad_table = contract(onehot, back_zero, 0, 0)
    grad_proj = contract(cell_params, back_zero, 1, 0)
    grad_params = contract(w_proj, back_zero, 1, 1)
    return ((grad_w1, grad_b1, grad_table, grad_proj), grad_params)


def general_body(
    adjoint,
    target_x,
    target_y,
    target_z,
    assignment,
    level_codes,
    cell_params,
    level_table,
    w_proj,
    w_one,
    b_one,
    w_two,
    b_two,
    w_out,
):
    cell_count = level_codes.shape[0]
    freq_count = w_out.shape[1] // 2
    freq_size = lax.axis_size("freq")
    cell_rank = lax.axis_index("cells")
    freq_rank = lax.axis_index("freq")
    first_cell = (cell_rank * freq_size + freq_rank) * cell_count
    index = first_cell + jnp.arange(cell_count, dtype=jnp.int32)
    cell_col = (index % SIDE).astype(jnp.float32)
    cell_row = (index // SIDE).astype(jnp.float32)
    freq_grid = jnp.arange(freq_count, dtype=jnp.int32).astype(jnp.float32)
    stacked = jnp.concatenate(
        [
            adjoint,
            target_x[None, :],
            target_y[None, :],
            target_z[None, :],
            assignment.astype(jnp.float32)[None, :],
        ],
        axis=0,
    )
    total = jnp.zeros((2 * freq_count, cell_count), jnp.float32)
    piece = lax.all_gather(stacked, "cells", axis=1, tiled=True)
    length = piece.shape[1]
    block_len = math.gcd(length, 256)
    sections = piece.reshape(6, length // block_len, block_len).transpose(1, 0, 2)

    def inner(accum, rows):
        adj_round = rows[0:2].astype(jnp.bfloat16)
        kre, kim = kernel_tile(rows[2], rows[3], rows[4], rows[5], cell_col, cell_row, freq_count)
        select = (rows[5][:, None] == freq_grid[None, :]).astype(jnp.bfloat16)
        part_a = select * adj_round[0][:, None]
        part_b = select * adj_round[1][:, None]
        left_re = jnp.concatenate([part_a, part_b], axis=1)
        left_im = jnp.concatenate([part_b, -part_a], axis=1)
        return (accum + contract(left_re, kre, 0, 0) + contract(left_im, kim, 0, 0), None)

    total, unused = lax.scan(inner, total, sections)
    local_spec = total.astype(jnp.bfloat16)
    scale = 1.0 / math.sqrt(cell_count * lax.axis_size("cells") * freq_size)
    onehot, hidden_in, pre_one, act_one, pre_two, act_two = forward_pass(
        level_codes, cell_params, level_table, w_proj, w_one, b_one, w_two, b_two
    )
    upper, delta_two = upper_grads(local_spec, w_out, act_one, pre_two, act_two)
    lower, grad_params = lower_grads(
        delta_two, w_two, w_one, pre_one, hidden_in, onehot, cell_params, w_proj
    )
    totals = lax.psum(tuple(term * scale for term in upper + lower), ("cells", "freq"))
    return totals + (grad_params,)


def split(value, parts):
    pieces = []
    for _ in range(parts):
        piece = value.astype(BF16)
        pieces.append(piece.astype(F32))
        value = value - piece.astype(F32)
    return pieces


def fetch(sources, buffers, arrived):
    copies = [
        pltpu.make_async_copy(source, buffer, arrived.at[at])
        for at, (source, buffer) in enumerate(zip(sources, buffers))
    ]
    for copy in copies:
        copy.start()
    for copy in copies:
        copy.wait()


def pack_kernel(*refs):
    sources, (out_ref, flat_ref), buffers, (rows, arrived) = refs[:14], refs[14:16], refs[16:28], refs[28:]
    hidden = flat_ref.shape[1]
    base = SMALL_ROWS + 2 * hidden
    fetch(
        sources,
        [flat_ref.at[SMALL_ROWS : SMALL_ROWS + hidden], flat_ref.at[SMALL_ROWS + hidden : base]]
        + list(buffers),
        arrived,
    )
    wo_ref, buffers = buffers[0], buffers[1:]
    out_dim = wo_ref.shape[1]
    flat_ref[base:, 0:out_dim] = wo_ref[0 : hidden // 2]
    flat_ref[base:, out_dim:] = wo_ref[hidden // 2 :]
    adj_ref, x_ref, y_ref, z_ref, assign_ref, codes_ref, params_ref = buffers[:7]
    table_ref, proj_ref, b1_ref, b2_ref = buffers[7:]
    cells = codes_ref.shape[1]
    pieces = [adj_ref[0:1], adj_ref[1:2]]
    for ref in (x_ref, y_ref, z_ref):
        pieces += split(ref[...], 3)
    pieces.append(assign_ref[...].astype(F32))
    pieces += [jnp.zeros_like(pieces[0])] * 4
    codes = codes_ref[...].astype(F32)
    for at in range(4):
        rows[at : at + 1] = codes[:, at * 128 : (at + 1) * 128]
    rows[4:5] = jnp.concatenate(pieces[0:8], axis=1)
    rows[5:6] = jnp.concatenate(pieces[8:16], axis=1)
    rows[6:8] = jnp.zeros((2, 128), F32)
    out_ref[:, 0:cells] = params_ref[...]
    out_ref[:, cells:] = rows[...].astype(BF16)
    embed = [table_ref[...].astype(F32), proj_ref[...].astype(F32)]
    shifts = split(b1_ref[...], 3) + split(b2_ref[...], 3)
    rest = jnp.zeros((SMALL_ROWS - 30, hidden), F32)
    flat_ref[0:SMALL_ROWS] = jnp.concatenate(embed + shifts + [rest], axis=0).astype(BF16)


def stage_kernel(packed_ref, out_ref):
    out_ref[...] = packed_ref[...]


def weight_kernel(flat_ref, out_ref):
    hidden = flat_ref.shape[1]
    first = slice(SMALL_ROWS, SMALL_ROWS + hidden)
    small = flat_ref[0:SMALL_ROWS].astype(F32)
    stack = small[0:24]
    joined = dot(stack.astype(BF16), flat_ref[first])
    bias = (small[24:25] + small[25:26]) + small[26:27]
    joined = jnp.concatenate([joined, bias, jnp.zeros((7, hidden), F32)], axis=0)
    shifts = [0.5 * small[at : at + 1] for at in (27, 28, 29)]
    rows = split(0.5 * joined, 3) + shifts + [jnp.zeros((29, hidden), F32)]
    out_ref[:, 0:128] = jnp.concatenate(rows, axis=0).T.astype(BF16)
    second = flat_ref[SMALL_ROWS + hidden : SMALL_ROWS + 2 * hidden].astype(F32)
    out_ref[:, 128 : 128 + hidden] = (0.5 * second).T.astype(BF16)
    filled = [stack, jnp.zeros((8, hidden), F32)]
    rows = filled * 3 + [jnp.zeros((32, hidden), F32)]
    out_ref[:, 128 + hidden :] = jnp.concatenate(rows, axis=0).T.astype(BF16)


NEAR = (3.1051740646362305, -2.9883227348327637)
FAR = (0.9884209632873535, -4.203672885894775)


def dot(left, right):
    return jnp.dot(left, right, preferred_element_type=F32)


def feature_of(gathered_ref, slot):
    width = gathered_ref.shape[2]
    cells = width - 128
    rows = gathered_ref[slot, :, cells:].astype(F32)
    codes = jnp.concatenate(
        [jnp.broadcast_to(rows[at : at + 1], (8, 128)) for at in range(4)], axis=1
    )
    steps = lax.broadcasted_iota(jnp.int32, (8, cells), 0).astype(F32)
    blocks = [
        jnp.where(codes == steps, 1.0, 0.0),
        jnp.where(codes == steps + 8.0, 1.0, 0.0),
        gathered_ref[slot, :, 0:cells].astype(F32),
        jnp.where(steps == 0.0, 1.0, 0.0),
    ]
    return jnp.concatenate(blocks, axis=0).astype(BF16)


def activate(half):
    tanh = jnp.tanh(half)
    gate = 1.0 + tanh
    act = half * gate
    return act.astype(BF16), gate + act * (1.0 - tanh)


def layer_one(weights_ref, feature):
    rows = [feature] * 3 + [jnp.zeros((32, feature.shape[1]), BF16)]
    return dot(weights_ref[:, 0:128], jnp.concatenate(rows, axis=0))


def bias_of(weights_ref):
    shift = weights_ref[:, 96:128].astype(F32)
    shift = (shift[:, 0:1] + shift[:, 1:2]) + shift[:, 2:3]
    return jnp.broadcast_to(shift, (shift.shape[0], 128))


def forward_kernel(
    begin, gathered_ref, weights_ref, one_ref, slope_one_ref, two_ref, slope_two_ref, bias
):
    count, hidden, cells = one_ref.shape
    bias[...] = bias_of(weights_ref)
    wide = jnp.concatenate([bias[...]] * (cells // 128), axis=1)

    def first(slot):
        act, slope = activate(layer_one(weights_ref, feature_of(gathered_ref, begin + slot)))
        one_ref[slot] = act
        slope_one_ref[slot] = slope

    def second(slot):
        half = dot(weights_ref[:, 128 : 128 + hidden], one_ref[slot]) + wide
        act, slope = activate(half)
        two_ref[slot] = act
        slope_two_ref[slot] = slope

    first(0)
    for slot in range(1, count):
        second(slot - 1)
        first(slot)
    second(count - 1)


def cell_kernel(
    freq_size,
    place_ref, gathered_ref, weights_ref, flat_ref, *refs
):
    chunks, _, width = gathered_ref.shape
    cells = width - 128
    hidden = flat_ref.shape[1]
    early = [refs[at : at + 4] for at in range(0, len(refs) - 14, 4)]
    sums_ref, grad_params_ref, across, where, lift, bias, totals, waves = refs[-14:-6]
    delta_two, spectra = refs[-6:-4]
    early.append(refs[-4:])
    freqs = lift.shape[0] // 2
    base = SMALL_ROWS + 2 * hidden
    half_rows = slice(base, base + hidden // 2)
    w2_ref = flat_ref.at[SMALL_ROWS + hidden : base]
    targets = chunks * 16
    me = place_ref[0]
    freq_rank = place_ref[1]
    stride = freq_size * cells
    second_ref = weights_ref.at[:, 128 : 128 + hidden]

    rows = [gathered_ref[chunk ^ me, :, cells:].astype(F32) for chunk in range(chunks)]
    low = jnp.concatenate([row[4:5] for row in rows], axis=0).T
    high = jnp.concatenate([row[5:6] for row in rows], axis=0).T
    parts = [low[at * 16 : (at + 1) * 16] for at in range(8)]
    parts += [high[at * 16 : (at + 1) * 16] for at in range(4)]
    point_x = (parts[2] + parts[3]) + parts[4]
    point_y = (parts[5] + parts[6]) + parts[7]
    point_z = (parts[8] + parts[9]) + parts[10]
    wave = (wave_low + (wave_high - wave_low) * parts[11] / (freqs - 1)) * (0.5 / math.pi)
    sides = [
        freq_rank * cells + lane + lax.broadcasted_iota(jnp.int32, (1, 128), 1)
        for lane in range(0, cells, 128)
    ]
    sides = [lax.rem(side, SIDE).astype(F32) for side in sides]
    grid = lax.broadcasted_iota(jnp.int32, (16, freqs), 1).astype(F32)
    near, far = [], []
    for chunk in range(chunks):
        here = slice(chunk * 16, chunk * 16 + 16)

        def spread(value):
            return jnp.broadcast_to(value[:, chunk : chunk + 1], (16, 128))

        where[0, here] = spread(point_y)
        where[1, here] = spread(wave * wave * (point_z * point_z))
        where[2, here] = spread(kernel_gain * point_z * (wave * wave))
        where[3, here] = spread(wave * wave)
        wide = spread(point_x)
        for at, side in enumerate(sides):
            offset = wide - side
            across[here, at * 128 : (at + 1) * 128] = offset * offset * where[3, here]
        select = jnp.where(spread(parts[11])[:, 0:freqs] == grid, 1.0, 0.0)
        part_a = select * spread(parts[0])[:, 0:freqs]
        part_b = select * spread(parts[1])[:, 0:freqs]
        near.append(jnp.concatenate([part_a, part_b], axis=1))
        far.append(jnp.concatenate([part_b, -part_a], axis=1))
    lift[:, 0:targets] = jnp.concatenate(near, axis=0).T.astype(BF16)
    lift[:, targets:] = jnp.concatenate(far, axis=0).T.astype(BF16)
    bias[...] = bias_of(weights_ref)

    middle = hidden + 32
    top = middle + 2 * freqs
    owners = [(part, at) for part in early for at in range(part[0].shape[0])]
    ready = chunks - refs[-4].shape[0]

    def layers(block):
        part, at = owners[block]
        return [ref.at[at] for ref in part]

    def back_out(spectrum):
        upper_rows = dot(flat_ref[half_rows, 0 : 2 * freqs], spectrum)
        lower_rows = dot(flat_ref[half_rows, 2 * freqs : 4 * freqs], spectrum)
        return jnp.concatenate([upper_rows, lower_rows], axis=0)

    def holograms(block, even):
        chunk = lax.bitwise_xor(me, block)
        row = ((chunk * stride + freq_rank * cells) // SIDE).astype(F32)
        for at in range(0, targets, 16):
            here = slice(at, at + 16)
            offset = where[0, here] - row
            rest = offset * offset * where[3, here] + where[1, here]
            for lane in range(0, cells, 128):
                square = across[here, lane : lane + 128] + rest
                turns = square * lax.rsqrt(square)
                part = turns - jnp.round(turns)
                power = part * part
                sine = part * (NEAR[1] * power + NEAR[0])
                cosine = (power + FAR[1]) * power + FAR[0]
                sine_square = sine * sine
                cosine_square = cosine * cosine
                norm = square * (sine_square + cosine_square)
                amplitude = where[2, here] * pl.reciprocal(norm, approx=True)
                waves[even, at : at + 16, lane : lane + 128] = (
                    amplitude * (cosine_square - sine_square)
                ).astype(BF16)
                waves[even, targets + at : targets + at + 16, lane : lane + 128] = (
                    amplitude * ((sine + sine) * cosine)
                ).astype(BF16)
                yield

    def lower(block, even):
        total = totals.at[lax.bitwise_xor(me, block) // 2]

        def outer(low, left, right):
            rows = slice(low, low + left.shape[0])
            product = contract(left, right, 1, 1)
            total[rows] = total[rows] + product if block % 2 else product

        one, slope, two, _ = layers(block)
        feature = feature_of(gathered_ref, block)
        delta = delta_two[even]
        back = dot(w2_ref[...], delta)
        yield
        value = (back * slope[...]).astype(BF16)
        if block == 0:
            both = contract(weights_ref[:, 0:128], value, 0, 0)
            grad_params_ref[...] = 0.5 * ((both[16:24] + both[48:56]) + both[80:88])
        yield
        outer(0, jnp.concatenate([one[...], feature], axis=0), delta)
        yield
        outer(middle, spectra[even], two[...])
        yield
        outer(top, feature, value)
        yield

    def upper(block, even):
        spectrum = dot(lift[...], waves[even]).astype(BF16)
        spectra[even] = spectrum
        yield
        back = back_out(spectrum)
        yield
        delta_two[even] = (back * layers(block)[3][...]).astype(BF16)
        yield

    def first(block):
        one, slope_one, _, _ = layers(block)
        half = layer_one(weights_ref, feature_of(gathered_ref, block))
        yield
        one[...], slope_one[...] = activate(half)
        yield

    def second(block):
        one, _, two, slope_two = layers(block)
        half = dot(second_ref[...], one[...])
        half = half + jnp.concatenate([bias[...]] * (cells // 128), axis=1)
        yield
        two[...], slope_two[...] = activate(half)
        yield

    for at in range(chunks + 2):
        waiting = []
        if 0 <= at - 2 < chunks:
            waiting.append((lower(at - 2, at % 2), 5))
        if 0 <= at - 1 < chunks:
            waiting.append((upper(at - 1, (at - 1) % 2), 3))
        if ready <= at + ready - 1 < chunks:
            waiting.append((second(at + ready - 1), 2))
        if at + ready < chunks:
            waiting.append((first(at + ready), 2))
        spots = sum(count for _, count in waiting)
        waiting = [stage for stage, _ in waiting]
        pieces = (targets // 16) * (cells // 128) if at < chunks else 0
        extra = holograms(at, at % 2)
        done, drawn = 0, 0
        while waiting:
            for stage in list(waiting):
                if next(stage, True) is True:
                    waiting.remove(stage)
                    continue
                done += 1
                while drawn < pieces * done // spots:
                    next(extra)
                    drawn += 1
        if pieces:
            for _ in extra:
                pass
    pairs = chunks // 2
    added = [totals.at[at] for at in range(pairs)]
    for low in range(0, totals.shape[1], 16):
        terms = [ref[low : low + 16] for ref in added]
        while len(terms) > 1:
            terms = [terms[at] + terms[at + 1] for at in range(0, len(terms), 2)]
        sums_ref[low : low + 16] = terms[0].astype(BF16)


def finish_kernel(
    scale, own_ref, other_ref, weights_ref, flat_ref,
    out_ref, w2_ref, b2_ref, wone_ref, b1_ref, table_ref, proj_ref,
):
    hidden = flat_ref.shape[1]
    middle = hidden + 32
    top = middle + out_ref.shape[1]
    levels = table_ref.shape[0]
    used = levels + proj_ref.shape[0]

    def total(low, high, factor):
        both = own_ref[low:high].astype(F32) + other_ref[low:high].astype(F32)
        return both * (scale * factor)

    w2_ref[...] = total(0, hidden, 0.5)
    out_ref[...] = total(middle, top, 1.0).T
    feature = total(top, top + 32, 0.25)
    b1_ref[...] = feature[used : used + 1]
    b2_ref[...] = total(hidden, middle, 0.5)[used : used + 1]
    rows = jnp.concatenate(split(feature, 3), axis=0).astype(BF16)
    embed = weights_ref[:, 128 + hidden : 128 + hidden + 96]
    wone_ref[...] = jnp.dot(embed, rows, preferred_element_type=F32)
    back = contract(rows, flat_ref[SMALL_ROWS : SMALL_ROWS + hidden], 1, 1)
    back = (back[0:32] + back[32:64]) + back[64:96]
    table_ref[...] = back[0:levels]
    proj_ref[...] = back[levels:used]


def run_forward(gathered, weights, begin, count):
    hidden = weights.shape[0]
    block = (count, hidden, gathered.shape[2] - 128)
    return pl.pallas_call(
        functools.partial(forward_kernel, begin),
        out_shape=[jax.ShapeDtypeStruct(block, kind) for kind in (BF16, F32, BF16, F32)],
        scratch_shapes=[pltpu.VMEM((hidden, 128), F32)],
        compiler_params=pltpu.CompilerParams(vmem_limit_bytes=VMEM_BYTES),
        name="early_forward",
    )(gathered, weights)


def run_cells(place, gathered, weights, flat, early, freq_size, out_dim):
    chunks, props, width = gathered.shape
    cells = width - 128
    hidden = flat.shape[1]
    targets = chunks * 16
    rest = chunks - sum(part[0].shape[0] for part in early)
    rows = hidden + out_dim + 64
    vmem = pl.BlockSpec(memory_space=pltpu.VMEM)
    flattened = [array for part in early for array in part]
    return pl.pallas_call(
        functools.partial(cell_kernel, freq_size),
        out_shape=(
            jax.ShapeDtypeStruct((rows, hidden), BF16),
            jax.ShapeDtypeStruct((props, cells), F32),
        ),
        in_specs=[pl.BlockSpec(memory_space=pltpu.SMEM)] + [vmem] * (3 + len(flattened)),
        out_specs=(vmem, vmem),
        scratch_shapes=[
            pltpu.VMEM((targets, cells), F32),
            pltpu.VMEM((4, targets, 128), F32),
            pltpu.VMEM((out_dim, 2 * targets), BF16),
            pltpu.VMEM((hidden, 128), F32),
            pltpu.VMEM((chunks // 2, rows, hidden), F32),
            pltpu.VMEM((2, 2 * targets, cells), BF16),
            pltpu.VMEM((2, hidden, cells), BF16),
            pltpu.VMEM((2, out_dim, cells), BF16),
        ]
        + [pltpu.VMEM((rest, hidden, cells), kind) for kind in (BF16, F32, BF16, F32)],
        compiler_params=pltpu.CompilerParams(vmem_limit_bytes=VMEM_BYTES),
        name="all_cells",
    )(place, gathered, weights, flat, *flattened)


def small_body(
    adjoint,
    target_x,
    target_y,
    target_z,
    assignment,
    level_codes,
    cell_params,
    level_table,
    w_proj,
    w_one,
    b_one,
    w_two,
    b_two,
    w_out,
):
    cells = level_codes.shape[0]
    local = target_x.shape[0]
    levels, hidden = level_table.shape
    props = w_proj.shape[0]
    freqs = w_out.shape[1] // 2
    chunks = lax.axis_size("cells")
    freq_size = lax.axis_size("freq")
    shape = jax.ShapeDtypeStruct
    params = pltpu.CompilerParams(vmem_limit_bytes=VMEM_BYTES)

    def fetched(arrays):
        buffers = [pltpu.VMEM(array.shape, array.dtype) for array in arrays]
        return buffers, pltpu.SemaphoreType.DMA((len(arrays),))

    inputs = (
        w_one, w_two, w_out,
        adjoint, target_x[None, :], target_y[None, :], target_z[None, :], assignment[None, :],
        level_codes[None, :], cell_params, level_table, w_proj, b_one[None, :], b_two[None, :],
    )
    whole = pltpu.CompilerParams(vmem_limit_bytes=WHOLE_VMEM)
    buffers, arrived = fetched(inputs)
    packed, flat = pl.pallas_call(
        pack_kernel,
        out_shape=(
            shape((props, cells + 128), BF16),
            shape((SMALL_ROWS + 2 * hidden + hidden // 2, hidden), BF16),
        ),
        in_specs=[pl.BlockSpec(memory_space=pltpu.HBM)] * len(inputs),
        scratch_shapes=buffers[2:] + [pltpu.VMEM((8, 128), F32), arrived],
        compiler_params=whole,
        name="pack_inputs",
    )(*inputs)
    staged = pl.pallas_call(
        stage_kernel,
        out_shape=shape((props, cells + 128), BF16),
        compiler_params=params,
        name="stage_own",
    )(packed)
    moved = lax.ppermute(packed[None], "cells", [(at, at ^ 1) for at in range(chunks)])
    weights = pl.pallas_call(
        weight_kernel,
        out_shape=shape((hidden, 256 + hidden), BF16),
        compiler_params=params,
        name="prepare_weights",
    )(flat)
    gathered = jnp.concatenate([staged[None], moved], axis=0)
    gathered, weights = lax.optimization_barrier((gathered, weights))
    reach, begin, early = 2, 0, []
    while reach < chunks:
        moved = lax.ppermute(gathered, "cells", [(at, at ^ reach) for at in range(chunks)])
        early.append(run_forward(gathered, weights, begin, reach - begin))
        begin = reach
        gathered = jnp.concatenate([gathered, moved], axis=0)
        gathered, early = lax.optimization_barrier((gathered, early))
        reach *= 2

    place = jnp.stack([lax.axis_index("cells"), lax.axis_index("freq")]).astype(jnp.int32)
    sums, grad_params = run_cells(
        place, gathered, weights, flat, early, freq_size, w_out.shape[1]
    )

    other = lax.ppermute(sums, "freq", [(at, at ^ 1) for at in range(freq_size)])
    scale = 1.0 / math.sqrt(cells * chunks * freq_size)
    grad_out, grad_w2, grad_b2, grad_w1, grad_b1, grad_table, grad_proj = pl.pallas_call(
        functools.partial(finish_kernel, scale),
        out_shape=(
            shape((hidden, 2 * freqs), F32),
            shape((hidden, hidden), F32),
            shape((1, hidden), F32),
            shape((hidden, hidden), F32),
            shape((1, hidden), F32),
            shape((levels, hidden), F32),
            shape((props, hidden), F32),
        ),
        compiler_params=params,
        name="finish_sums",
    )(sums, other, weights, flat)
    return (
        grad_out, grad_w2, grad_b2[0], grad_w1, grad_b1[0], grad_table, grad_proj, grad_params,
    )


def solution(mesh):
    chunks = mesh.shape["cells"]
    paired = mesh.shape["freq"] == 2 and chunks > 2 and chunks & (chunks - 1) == 0

    def body(*args):
        local = args[1].shape[0]
        cells = args[5].shape[0]
        hidden = args[9].shape[0]
        suits = (
            paired
            and local == 16
            and cells == 512
            and chunks * cells * chunks * local <= 1 << 20
            and args[7].shape[0] == 16
            and args[8].shape[0] == 8
            and hidden == 2 * args[13].shape[1]
            and mesh.shape["freq"] * cells % SIDE == 0
            and SIDE % cells == 0
            and args[13].shape[1] == 128
        )
        return (small_body if suits else general_body)(*args)

    placed = (
        P(None, ("groups", "cells")),
        P(("groups", "cells")),
        P(("groups", "cells")),
        P(("groups", "cells")),
        P(("groups", "cells")),
        P(("groups", "cells", "freq")),
        P(None, ("groups", "cells", "freq")),
        P(),
        P(),
        P(),
        P(),
        P(),
        P(),
        P(),
    )
    return jax.shard_map(
        body,
        mesh=mesh,
        in_specs=placed,
        out_specs=(
            P("groups", None),
            P("groups", None),
            P("groups"),
            P("groups", None),
            P("groups"),
            P("groups", None),
            P("groups", None),
            P(None, ("groups", "cells", "freq")),
        ),
        check_vma=False,
    )
```

```python
import functools
import math

import jax
import jax.numpy as jnp
from jax import lax
from jax.experimental import pallas as pl
from jax.experimental.pallas import tpu as pltpu
from jax.sharding import PartitionSpec as P

SIDE = 1024

wave_low = 1.0
wave_high = 3.0
kernel_gain = 150.0

F32 = jnp.float32
BF16 = jnp.bfloat16
VMEM_BYTES = 40 * 1024 * 1024
SMALL_ROWS = 32
EARLY_BLOCKS = 1
WHOLE_VMEM = 64 * 1024 * 1024 - 256 * 1024


def silu_slope(value):
    sigma = jax.nn.sigmoid(value)
    return sigma * (1.0 + value * (1.0 - sigma))


def contract(left, right, left_dim, right_dim):
    return lax.dot_general(
        left, right, (((left_dim,), (right_dim,)), ((), ())), preferred_element_type=jnp.float32
    )


def kernel_tile(point_x, point_y, point_z, freq_value, cell_col, cell_row, count_freq):
    wave = wave_low + (wave_high - wave_low) * freq_value / (count_freq - 1)
    offset_x = point_x[:, None] - cell_col[None, :]
    offset_y = point_y[:, None] - cell_row[None, :]
    square = offset_x * offset_x + offset_y * offset_y + (point_z * point_z)[:, None]
    distance = jnp.sqrt(square)
    amplitude = kernel_gain * point_z[:, None] / square
    phase = wave[:, None] * distance
    return (
        (amplitude * jnp.cos(phase)).astype(jnp.bfloat16),
        (amplitude * jnp.sin(phase)).astype(jnp.bfloat16),
    )


def forward_pass(level_codes, cell_params, level_table, w_proj, w_one, b_one, w_two, b_two):
    levels = level_table.shape[0]
    onehot = (level_codes[:, None] == jnp.arange(levels, dtype=jnp.int32)[None, :]).astype(
        jnp.bfloat16
    )
    hidden_in = (
        jnp.dot(onehot, level_table, preferred_element_type=jnp.float32)
        + contract(cell_params, w_proj, 0, 0)
    ).astype(jnp.bfloat16)
    pre_one = jnp.dot(hidden_in, w_one, preferred_element_type=jnp.float32) + b_one
    act_one = jax.nn.silu(pre_one).astype(jnp.bfloat16)
    pre_two = jnp.dot(act_one, w_two, preferred_element_type=jnp.float32) + b_two
    act_two = jax.nn.silu(pre_two).astype(jnp.bfloat16)
    return (onehot, hidden_in, pre_one, act_one, pre_two, act_two)


def upper_grads(spectra, w_out, act_one, pre_two, act_two):
    back_two = contract(spectra, w_out, 0, 1)
    delta_two = (back_two * silu_slope(pre_two)).astype(jnp.bfloat16)
    grad_out = contract(act_two, spectra, 0, 1)
    grad_w2 = contract(act_one, delta_two, 0, 0)
    grad_b2 = jnp.sum(delta_two.astype(jnp.float32), axis=0)
    return ((grad_out, grad_w2, grad_b2), delta_two)


def lower_grads(delta_two, w_two, w_one, pre_one, hidden_in, onehot, cell_params, w_proj):
    back_one = contract(delta_two, w_two, 1, 1)
    delta_one = (back_one * silu_slope(pre_one)).astype(jnp.bfloat16)
    grad_w1 = contract(hidden_in, delta_one, 0, 0)
    grad_b1 = jnp.sum(delta_one.astype(jnp.float32), axis=0)
    back_zero = contract(delta_one, w_one, 1, 1).astype(jnp.bfloat16)
    grad_table = contract(onehot, back_zero, 0, 0)
    grad_proj = contract(cell_params, back_zero, 1, 0)
    grad_params = contract(w_proj, back_zero, 1, 1)
    return ((grad_w1, grad_b1, grad_table, grad_proj), grad_params)


def general_body(
    adjoint,
    target_x,
    target_y,
    target_z,
    assignment,
    level_codes,
    cell_params,
    level_table,
    w_proj,
    w_one,
    b_one,
    w_two,
    b_two,
    w_out,
):
    cell_count = level_codes.shape[0]
    freq_count = w_out.shape[1] // 2
    freq_size = lax.axis_size("freq")
    cell_rank = lax.axis_index("cells")
    freq_rank = lax.axis_index("freq")
    first_cell = (cell_rank * freq_size + freq_rank) * cell_count
    index = first_cell + jnp.arange(cell_count, dtype=jnp.int32)
    cell_col = (index % SIDE).astype(jnp.float32)
    cell_row = (index // SIDE).astype(jnp.float32)
    freq_grid = jnp.arange(freq_count, dtype=jnp.int32).astype(jnp.float32)
    stacked = jnp.concatenate(
        [
            adjoint,
            target_x[None, :],
            target_y[None, :],
            target_z[None, :],
            assignment.astype(jnp.float32)[None, :],
        ],
        axis=0,
    )
    total = jnp.zeros((2 * freq_count, cell_count), jnp.float32)
    piece = lax.all_gather(stacked, "cells", axis=1, tiled=True)
    length = piece.shape[1]
    block_len = math.gcd(length, 256)
    sections = piece.reshape(6, length // block_len, block_len).transpose(1, 0, 2)

    def inner(accum, rows):
        adj_round = rows[0:2].astype(jnp.bfloat16)
        kre, kim = kernel_tile(rows[2], rows[3], rows[4], rows[5], cell_col, cell_row, freq_count)
        select = (rows[5][:, None] == freq_grid[None, :]).astype(jnp.bfloat16)
        part_a = select * adj_round[0][:, None]
        part_b = select * adj_round[1][:, None]
        left_re = jnp.concatenate([part_a, part_b], axis=1)
        left_im = jnp.concatenate([part_b, -part_a], axis=1)
        return (accum + contract(left_re, kre, 0, 0) + contract(left_im, kim, 0, 0), None)

    total, unused = lax.scan(inner, total, sections)
    local_spec = total.astype(jnp.bfloat16)
    scale = 1.0 / math.sqrt(cell_count * lax.axis_size("cells") * freq_size)
    onehot, hidden_in, pre_one, act_one, pre_two, act_two = forward_pass(
        level_codes, cell_params, level_table, w_proj, w_one, b_one, w_two, b_two
    )
    upper, delta_two = upper_grads(local_spec, w_out, act_one, pre_two, act_two)
    lower, grad_params = lower_grads(
        delta_two, w_two, w_one, pre_one, hidden_in, onehot, cell_params, w_proj
    )
    totals = lax.psum(tuple(term * scale for term in upper + lower), ("cells", "freq"))
    return totals + (grad_params,)


def split(value, parts):
    pieces = []
    for _ in range(parts):
        piece = value.astype(BF16)
        pieces.append(piece.astype(F32))
        value = value - piece.astype(F32)
    return pieces


def fetch(sources, buffers, arrived):
    copies = [
        pltpu.make_async_copy(source, buffer, arrived.at[at])
        for at, (source, buffer) in enumerate(zip(sources, buffers))
    ]
    for copy in copies:
        copy.start()
    for copy in copies:
        copy.wait()


def pack_kernel(*refs):
    sources, (out_ref, flat_ref), buffers, (rows, arrived) = refs[:14], refs[14:16], refs[16:28], refs[28:]
    hidden = flat_ref.shape[1]
    base = SMALL_ROWS + 2 * hidden
    fetch(
        sources,
        [flat_ref.at[SMALL_ROWS : SMALL_ROWS + hidden], flat_ref.at[SMALL_ROWS + hidden : base]]
        + list(buffers),
        arrived,
    )
    wo_ref, buffers = buffers[0], buffers[1:]
    out_dim = wo_ref.shape[1]
    flat_ref[base:, 0:out_dim] = wo_ref[0 : hidden // 2]
    flat_ref[base:, out_dim:] = wo_ref[hidden // 2 :]
    adj_ref, x_ref, y_ref, z_ref, assign_ref, codes_ref, params_ref = buffers[:7]
    table_ref, proj_ref, b1_ref, b2_ref = buffers[7:]
    cells = codes_ref.shape[1]
    pieces = [adj_ref[0:1], adj_ref[1:2]]
    for ref in (x_ref, y_ref, z_ref):
        pieces += split(ref[...], 3)
    pieces.append(assign_ref[...].astype(F32))
    pieces += [jnp.zeros_like(pieces[0])] * 4
    codes = codes_ref[...].astype(F32)
    for at in range(4):
        rows[at : at + 1] = codes[:, at * 128 : (at + 1) * 128]
    rows[4:5] = jnp.concatenate(pieces[0:8], axis=1)
    rows[5:6] = jnp.concatenate(pieces[8:16], axis=1)
    rows[6:8] = jnp.zeros((2, 128), F32)
    out_ref[:, 0:cells] = params_ref[...]
    out_ref[:, cells:] = rows[...].astype(BF16)
    embed = [table_ref[...].astype(F32), proj_ref[...].astype(F32)]
    shifts = split(b1_ref[...], 3) + split(b2_ref[...], 3)
    rest = jnp.zeros((SMALL_ROWS - 30, hidden), F32)
    flat_ref[0:SMALL_ROWS] = jnp.concatenate(embed + shifts + [rest], axis=0).astype(BF16)


def stage_kernel(packed_ref, out_ref):
    out_ref[...] = packed_ref[...]


def weight_kernel(flat_ref, out_ref):
    hidden = flat_ref.shape[1]
    first = slice(SMALL_ROWS, SMALL_ROWS + hidden)
    small = flat_ref[0:SMALL_ROWS].astype(F32)
    stack = small[0:24]
    joined = dot(stack.astype(BF16), flat_ref[first])
    bias = (small[24:25] + small[25:26]) + small[26:27]
    joined = jnp.concatenate([joined, bias, jnp.zeros((7, hidden), F32)], axis=0)
    shifts = [0.5 * small[at : at + 1] for at in (27, 28, 29)]
    rows = split(0.5 * joined, 3) + shifts + [jnp.zeros((29, hidden), F32)]
    out_ref[:, 0:128] = jnp.concatenate(rows, axis=0).T.astype(BF16)
    second = flat_ref[SMALL_ROWS + hidden : SMALL_ROWS + 2 * hidden].astype(F32)
    out_ref[:, 128 : 128 + hidden] = (0.5 * second).T.astype(BF16)
    filled = [stack, jnp.zeros((8, hidden), F32)]
    rows = filled * 3 + [jnp.zeros((32, hidden), F32)]
    out_ref[:, 128 + hidden :] = jnp.concatenate(rows, axis=0).T.astype(BF16)


NEAR = (3.1051740646362305, -2.9883227348327637)
FAR = (0.9884209632873535, -4.203672885894775)


def dot(left, right):
    return jnp.dot(left, right, preferred_element_type=F32)


def feature_of(gathered_ref, slot):
    width = gathered_ref.shape[2]
    cells = width - 128
    rows = gathered_ref[slot, :, cells:].astype(F32)
    codes = jnp.concatenate(
        [jnp.broadcast_to(rows[at : at + 1], (8, 128)) for at in range(4)], axis=1
    )
    steps = lax.broadcasted_iota(jnp.int32, (8, cells), 0).astype(F32)
    blocks = [
        jnp.where(codes == steps, 1.0, 0.0),
        jnp.where(codes == steps + 8.0, 1.0, 0.0),
        gathered_ref[slot, :, 0:cells].astype(F32),
        jnp.where(steps == 0.0, 1.0, 0.0),
    ]
    return jnp.concatenate(blocks, axis=0).astype(BF16)


def activate(half):
    tanh = jnp.tanh(half)
    gate = 1.0 + tanh
    act = half * gate
    return act.astype(BF16), gate + act * (1.0 - tanh)


def layer_one(weights_ref, feature):
    rows = [feature] * 3 + [jnp.zeros((32, feature.shape[1]), BF16)]
    return dot(weights_ref[:, 0:128], jnp.concatenate(rows, axis=0))


def bias_of(weights_ref):
    shift = weights_ref[:, 96:128].astype(F32)
    shift = (shift[:, 0:1] + shift[:, 1:2]) + shift[:, 2:3]
    return jnp.broadcast_to(shift, (shift.shape[0], 128))


def forward_kernel(
    begin, gathered_ref, weights_ref, one_ref, slope_one_ref, two_ref, slope_two_ref, bias
):
    count, hidden, cells = one_ref.shape
    bias[...] = bias_of(weights_ref)
    wide = jnp.concatenate([bias[...]] * (cells // 128), axis=1)

    def first(slot):
        act, slope = activate(layer_one(weights_ref, feature_of(gathered_ref, begin + slot)))
        one_ref[slot] = act
        slope_one_ref[slot] = slope

    def second(slot):
        half = dot(weights_ref[:, 128 : 128 + hidden], one_ref[slot]) + wide
        act, slope = activate(half)
        two_ref[slot] = act
        slope_two_ref[slot] = slope

    first(0)
    for slot in range(1, count):
        second(slot - 1)
        first(slot)
    second(count - 1)


def lay_targets(tiles, first_col, freqs, where, across, near, far):
    count = len(tiles)
    fill = [jnp.zeros((8 - count % 8, 128), F32)] if count % 8 else []
    low = jnp.concatenate([tile[4:5] for tile in tiles] + fill, axis=0).T
    high = jnp.concatenate([tile[5:6] for tile in tiles] + fill, axis=0).T
    parts = [low[at * 16 : (at + 1) * 16] for at in range(8)]
    parts += [high[at * 16 : (at + 1) * 16] for at in range(4)]
    point_x = (parts[2] + parts[3]) + parts[4]
    point_y = (parts[5] + parts[6]) + parts[7]
    point_z = (parts[8] + parts[9]) + parts[10]
    wave = (wave_low + (wave_high - wave_low) * parts[11] / (freqs - 1)) * (0.5 / math.pi)
    cells = across.shape[1]
    sides = [
        first_col + lane + lax.broadcasted_iota(jnp.int32, (1, 128), 1)
        for lane in range(0, cells, 128)
    ]
    sides = [lax.rem(side, SIDE).astype(F32) for side in sides]
    grid = lax.broadcasted_iota(jnp.int32, (16, freqs), 1).astype(F32)
    for chunk in range(count):
        here = slice(chunk * 16, chunk * 16 + 16)

        def spread(value):
            return jnp.broadcast_to(value[:, chunk : chunk + 1], (16, 128))

        square = spread(wave * wave)
        where[0, here] = spread(point_y)
        where[1, here] = spread(wave * wave * (point_z * point_z))
        where[2, here] = spread(kernel_gain * point_z * (wave * wave))
        where[3, here] = square
        wide = spread(point_x)
        for at, side in enumerate(sides):
            offset = wide - side
            across[here, at * 128 : (at + 1) * 128] = offset * offset * square
        select = jnp.where(spread(parts[11])[:, 0:freqs] == grid, 1.0, 0.0)
        part_a = select * spread(parts[0])[:, 0:freqs]
        part_b = select * spread(parts[1])[:, 0:freqs]
        near[here] = jnp.concatenate([part_a, part_b], axis=1)
        far[here] = jnp.concatenate([part_b, -part_a], axis=1)


def hologram_pieces(row, where, across, waves):
    for at in range(0, across.shape[0], 16):
        here = slice(at, at + 16)
        offset = where[0, here] - row
        rest = offset * offset * where[3, here] + where[1, here]
        for lane in range(0, across.shape[1], 128):
            lanes = slice(lane, lane + 128)
            square = across[here, lanes] + rest
            turns = square * lax.rsqrt(square)
            part = turns - jnp.round(turns)
            power = part * part
            sine = part * (NEAR[1] * power + NEAR[0])
            cosine = (power + FAR[1]) * power + FAR[0]
            sine_square = sine * sine
            cosine_square = cosine * cosine
            norm = square * (sine_square + cosine_square)
            amplitude = where[2, here] * pl.reciprocal(norm, approx=True)
            waves[0, here, lanes] = (
                amplitude * (cosine_square - sine_square)
            ).astype(BF16)
            waves[1, here, lanes] = (
                amplitude * ((sine + sine) * cosine)
            ).astype(BF16)
            yield


def early_kernel(freq_size, freqs, place_ref, gathered_ref, where, across, near, far, waves):
    count, _, width = gathered_ref.shape
    cells = width - 128
    me, freq_rank = place_ref[0], place_ref[1]
    local = lax.bitwise_and(me, count - 1)
    tiles = [
        gathered_ref[lax.bitwise_xor(local, at), :, cells:].astype(F32) for at in range(count)
    ]
    lay_targets(tiles, freq_rank * cells, freqs, where, across, near, far)
    for block in range(waves.shape[0]):
        chunk = lax.bitwise_xor(me, block)
        row = ((chunk * freq_size + freq_rank) * cells // SIDE).astype(F32)
        for _ in hologram_pieces(row, where, across, waves.at[block]):
            pass


def cell_kernel(
    freq_size,
    place_ref, gathered_ref, weights_ref, flat_ref, *refs
):
    chunks, _, width = gathered_ref.shape
    cells = width - 128
    hidden = flat_ref.shape[1]
    early = [refs[at : at + 4] for at in range(5, len(refs) - 16, 4)]
    early_where, early_across, early_near, early_far, early_waves = refs[0:5]
    sums_ref, grad_params_ref, across, where, near, far, lift, bias, totals, waves = refs[-16:-6]
    delta_two, spectra = refs[-6:-4]
    early.append(refs[-4:])
    freqs = lift.shape[0] // 2
    base = SMALL_ROWS + 2 * hidden
    half_rows = slice(base, base + hidden // 2)
    w2_ref = flat_ref.at[SMALL_ROWS + hidden : base]
    targets = chunks * 16
    me = place_ref[0]
    freq_rank = place_ref[1]
    stride = freq_size * cells
    second_ref = weights_ref.at[:, 128 : 128 + hidden]

    ready = chunks - refs[-4].shape[0]
    upper_first = lax.bitwise_and(me, ready) != 0

    def in_order(own, new):
        low = lax.select(upper_first, new, own)
        return jnp.concatenate([low, lax.select(upper_first, own, new)], axis=0)

    local = lax.bitwise_and(me, ready - 1)
    tiles = [
        gathered_ref[ready + lax.bitwise_xor(local, at), :, cells:].astype(F32)
        for at in range(ready)
    ]
    lay_targets(tiles, freq_rank * cells, freqs, where, across, near, far)
    lift[:, 0:targets] = in_order(early_near[...], near[...]).T.astype(BF16)
    lift[:, targets:] = in_order(early_far[...], far[...]).T.astype(BF16)
    bias[...] = bias_of(weights_ref)

    middle = hidden + 32
    top = middle + 2 * freqs
    owners = [(part, at) for part in early for at in range(part[0].shape[0])]

    def layers(block):
        part, at = owners[block]
        return [ref.at[at] for ref in part]

    def back_out(spectrum):
        upper_rows = dot(flat_ref[half_rows, 0 : 2 * freqs], spectrum)
        lower_rows = dot(flat_ref[half_rows, 2 * freqs : 4 * freqs], spectrum)
        return jnp.concatenate([upper_rows, lower_rows], axis=0)

    def holograms(block, even):
        row = ((lax.bitwise_xor(me, block) * stride + freq_rank * cells) // SIDE).astype(F32)
        if block >= EARLY_BLOCKS:
            yield from hologram_pieces(row, early_where, early_across, waves.at[even, 0])
        yield from hologram_pieces(row, where, across, waves.at[even, 1])

    def kernels_of(block, even):
        own = early_waves.at[block] if block < EARLY_BLOCKS else waves.at[even, 0]
        new = waves.at[even, 1]
        return jnp.concatenate([in_order(own[at], new[at]) for at in range(2)], axis=0)

    def lower(block, even):
        total = totals.at[lax.bitwise_xor(me, block) // 2]

        def outer(low, left, right):
            rows = slice(low, low + left.shape[0])
            product = contract(left, right, 1, 1)
            total[rows] = total[rows] + product if block % 2 else product

        one, slope, two, _ = layers(block)
        feature = feature_of(gathered_ref, block)
        delta = delta_two[even]
        back = dot(w2_ref[...], delta)
        yield
        value = (back * slope[...]).astype(BF16)
        if block == 0:
            both = contract(weights_ref[:, 0:128], value, 0, 0)
            grad_params_ref[...] = 0.5 * ((both[16:24] + both[48:56]) + both[80:88])
        yield
        outer(0, jnp.concatenate([one[...], feature], axis=0), delta)
        yield
        outer(middle, spectra[even], two[...])
        yield
        outer(top, feature, value)
        yield

    def upper(block, even):
        spectrum = dot(lift[...], kernels_of(block, even)).astype(BF16)
        spectra[even] = spectrum
        yield
        back = back_out(spectrum)
        yield
        delta_two[even] = (back * layers(block)[3][...]).astype(BF16)
        yield

    def first(block):
        one, slope_one, _, _ = layers(block)
        half = layer_one(weights_ref, feature_of(gathered_ref, block))
        yield
        one[...], slope_one[...] = activate(half)
        yield

    def second(block):
        one, _, two, slope_two = layers(block)
        half = dot(second_ref[...], one[...])
        half = half + jnp.concatenate([bias[...]] * (cells // 128), axis=1)
        yield
        two[...], slope_two[...] = activate(half)
        yield

    for at in range(chunks + 2):
        waiting = []
        if 0 <= at - 2 < chunks:
            waiting.append((lower(at - 2, at % 2), 5))
        if 0 <= at - 1 < chunks:
            waiting.append((upper(at - 1, (at - 1) % 2), 3))
        if ready <= at + ready - 1 < chunks:
            waiting.append((second(at + ready - 1), 2))
        if at + ready < chunks:
            waiting.append((first(at + ready), 2))
        spots = sum(count for _, count in waiting)
        waiting = [stage for stage, _ in waiting]
        pieces, extra = 0, None
        if at < chunks:
            pieces = (targets // (32 if at < EARLY_BLOCKS else 16)) * (cells // 128)
            extra = holograms(at, at % 2)
        done, drawn = 0, 0
        while waiting:
            for stage in list(waiting):
                if next(stage, True) is True:
                    waiting.remove(stage)
                    continue
                done += 1
                while drawn < pieces * done // spots:
                    next(extra)
                    drawn += 1
        if pieces:
            for _ in extra:
                pass
    pairs = chunks // 2
    added = [totals.at[at] for at in range(pairs)]
    for low in range(0, totals.shape[1], 16):
        terms = [ref[low : low + 16] for ref in added]
        while len(terms) > 1:
            terms = [terms[at] + terms[at + 1] for at in range(0, len(terms), 2)]
        sums_ref[low : low + 16] = terms[0].astype(BF16)


def finish_kernel(
    scale, own_ref, other_ref, weights_ref, flat_ref,
    out_ref, w2_ref, b2_ref, wone_ref, b1_ref, table_ref, proj_ref,
):
    hidden = flat_ref.shape[1]
    middle = hidden + 32
    top = middle + out_ref.shape[1]
    levels = table_ref.shape[0]
    used = levels + proj_ref.shape[0]

    def total(low, high, factor):
        both = own_ref[low:high].astype(F32) + other_ref[low:high].astype(F32)
        return both * (scale * factor)

    w2_ref[...] = total(0, hidden, 0.5)
    out_ref[...] = total(middle, top, 1.0).T
    feature = total(top, top + 32, 0.25)
    b1_ref[...] = feature[used : used + 1]
    b2_ref[...] = total(hidden, middle, 0.5)[used : used + 1]
    rows = jnp.concatenate(split(feature, 3), axis=0).astype(BF16)
    embed = weights_ref[:, 128 + hidden : 128 + hidden + 96]
    wone_ref[...] = jnp.dot(embed, rows, preferred_element_type=F32)
    back = contract(rows, flat_ref[SMALL_ROWS : SMALL_ROWS + hidden], 1, 1)
    back = (back[0:32] + back[32:64]) + back[64:96]
    table_ref[...] = back[0:levels]
    proj_ref[...] = back[levels:used]


def run_forward(gathered, weights, begin, count):
    hidden = weights.shape[0]
    block = (count, hidden, gathered.shape[2] - 128)
    return pl.pallas_call(
        functools.partial(forward_kernel, begin),
        out_shape=[jax.ShapeDtypeStruct(block, kind) for kind in (BF16, F32, BF16, F32)],
        scratch_shapes=[pltpu.VMEM((hidden, 128), F32)],
        compiler_params=pltpu.CompilerParams(vmem_limit_bytes=VMEM_BYTES),
        name="early_forward",
    )(gathered, weights)


def run_early(place, gathered, freq_size, out_dim):
    count, _, width = gathered.shape
    cells = width - 128
    known = count * 16
    vmem = pl.BlockSpec(memory_space=pltpu.VMEM)
    return pl.pallas_call(
        functools.partial(early_kernel, freq_size, out_dim // 2),
        out_shape=[
            jax.ShapeDtypeStruct((4, known, 128), F32),
            jax.ShapeDtypeStruct((known, cells), F32),
            jax.ShapeDtypeStruct((known, out_dim), F32),
            jax.ShapeDtypeStruct((known, out_dim), F32),
            jax.ShapeDtypeStruct((EARLY_BLOCKS, 2, known, cells), BF16),
        ],
        in_specs=[pl.BlockSpec(memory_space=pltpu.SMEM), vmem],
        compiler_params=pltpu.CompilerParams(vmem_limit_bytes=VMEM_BYTES),
        name="early_holograms",
    )(place, gathered)


def run_cells(place, gathered, weights, flat, waves, early, freq_size, out_dim):
    chunks, props, width = gathered.shape
    cells = width - 128
    hidden = flat.shape[1]
    targets = chunks * 16
    rest = chunks - sum(part[0].shape[0] for part in early)
    rows = hidden + out_dim + 64
    vmem = pl.BlockSpec(memory_space=pltpu.VMEM)
    flattened = list(waves) + [array for part in early for array in part]
    return pl.pallas_call(
        functools.partial(cell_kernel, freq_size),
        out_shape=(
            jax.ShapeDtypeStruct((rows, hidden), BF16),
            jax.ShapeDtypeStruct((props, cells), F32),
        ),
        in_specs=[pl.BlockSpec(memory_space=pltpu.SMEM)] + [vmem] * (3 + len(flattened)),
        out_specs=(vmem, vmem),
        scratch_shapes=[
            pltpu.VMEM((targets // 2, cells), F32),
            pltpu.VMEM((4, targets // 2, 128), F32),
            pltpu.VMEM((targets // 2, out_dim), F32),
            pltpu.VMEM((targets // 2, out_dim), F32),
            pltpu.VMEM((out_dim, 2 * targets), BF16),
            pltpu.VMEM((hidden, 128), F32),
            pltpu.VMEM((chunks // 2, rows, hidden), F32),
            pltpu.VMEM((2, 2, 2, targets // 2, cells), BF16),
            pltpu.VMEM((2, hidden, cells), BF16),
            pltpu.VMEM((2, out_dim, cells), BF16),
        ]
        + [pltpu.VMEM((rest, hidden, cells), kind) for kind in (BF16, F32, BF16, F32)],
        compiler_params=pltpu.CompilerParams(vmem_limit_bytes=VMEM_BYTES),
        name="all_cells",
    )(place, gathered, weights, flat, *flattened)


def small_body(
    adjoint,
    target_x,
    target_y,
    target_z,
    assignment,
    level_codes,
    cell_params,
    level_table,
    w_proj,
    w_one,
    b_one,
    w_two,
    b_two,
    w_out,
):
    cells = level_codes.shape[0]
    local = target_x.shape[0]
    levels, hidden = level_table.shape
    props = w_proj.shape[0]
    freqs = w_out.shape[1] // 2
    chunks = lax.axis_size("cells")
    freq_size = lax.axis_size("freq")
    shape = jax.ShapeDtypeStruct
    params = pltpu.CompilerParams(vmem_limit_bytes=VMEM_BYTES)

    def fetched(arrays):
        buffers = [pltpu.VMEM(array.shape, array.dtype) for array in arrays]
        return buffers, pltpu.SemaphoreType.DMA((len(arrays),))

    inputs = (
        w_one, w_two, w_out,
        adjoint, target_x[None, :], target_y[None, :], target_z[None, :], assignment[None, :],
        level_codes[None, :], cell_params, level_table, w_proj, b_one[None, :], b_two[None, :],
    )
    whole = pltpu.CompilerParams(vmem_limit_bytes=WHOLE_VMEM)
    buffers, arrived = fetched(inputs)
    packed, flat = pl.pallas_call(
        pack_kernel,
        out_shape=(
            shape((props, cells + 128), BF16),
            shape((SMALL_ROWS + 2 * hidden + hidden // 2, hidden), BF16),
        ),
        in_specs=[pl.BlockSpec(memory_space=pltpu.HBM)] * len(inputs),
        scratch_shapes=buffers[2:] + [pltpu.VMEM((8, 128), F32), arrived],
        compiler_params=whole,
        name="pack_inputs",
    )(*inputs)
    staged = pl.pallas_call(
        stage_kernel,
        out_shape=shape((props, cells + 128), BF16),
        compiler_params=params,
        name="stage_own",
    )(packed)
    moved = lax.ppermute(packed[None], "cells", [(at, at ^ 1) for at in range(chunks)])
    weights = pl.pallas_call(
        weight_kernel,
        out_shape=shape((hidden, 256 + hidden), BF16),
        compiler_params=params,
        name="prepare_weights",
    )(flat)
    gathered = jnp.concatenate([staged[None], moved], axis=0)
    gathered, weights = lax.optimization_barrier((gathered, weights))
    place = jnp.stack([lax.axis_index("cells"), lax.axis_index("freq")]).astype(jnp.int32)
    out_dim = w_out.shape[1]
    reach, begin, early = 2, 0, []
    while reach < chunks:
        moved = lax.ppermute(gathered, "cells", [(at, at ^ reach) for at in range(chunks)])
        early.append(run_forward(gathered, weights, begin, reach - begin))
        if 2 * reach == chunks:
            waves = run_early(place, gathered, freq_size, out_dim)
        begin = reach
        gathered = jnp.concatenate([gathered, moved], axis=0)
        gathered, early = lax.optimization_barrier((gathered, early))
        reach *= 2

    sums, grad_params = run_cells(
        place, gathered, weights, flat, waves, early, freq_size, out_dim
    )

    other = lax.ppermute(sums, "freq", [(at, at ^ 1) for at in range(freq_size)])
    scale = 1.0 / math.sqrt(cells * chunks * freq_size)
    grad_out, grad_w2, grad_b2, grad_w1, grad_b1, grad_table, grad_proj = pl.pallas_call(
        functools.partial(finish_kernel, scale),
        out_shape=(
            shape((hidden, 2 * freqs), F32),
            shape((hidden, hidden), F32),
            shape((1, hidden), F32),
            shape((hidden, hidden), F32),
            shape((1, hidden), F32),
            shape((levels, hidden), F32),
            shape((props, hidden), F32),
        ),
        compiler_params=params,
        name="finish_sums",
    )(sums, other, weights, flat)
    return (
        grad_out, grad_w2, grad_b2[0], grad_w1, grad_b1[0], grad_table, grad_proj, grad_params,
    )


def solution(mesh):
    chunks = mesh.shape["cells"]
    paired = mesh.shape["freq"] == 2 and chunks > 2 and chunks & (chunks - 1) == 0

    def body(*args):
        local = args[1].shape[0]
        cells = args[5].shape[0]
        hidden = args[9].shape[0]
        suits = (
            paired
            and local == 16
            and cells == 512
            and chunks * cells * chunks * local <= 1 << 20
            and args[7].shape[0] == 16
            and args[8].shape[0] == 8
            and hidden == 2 * args[13].shape[1]
            and mesh.shape["freq"] * cells % SIDE == 0
            and SIDE % cells == 0
            and args[13].shape[1] == 128
        )
        return (small_body if suits else general_body)(*args)

    placed = (
        P(None, ("groups", "cells")),
        P(("groups", "cells")),
        P(("groups", "cells")),
        P(("groups", "cells")),
        P(("groups", "cells")),
        P(("groups", "cells", "freq")),
        P(None, ("groups", "cells", "freq")),
        P(),
        P(),
        P(),
        P(),
        P(),
        P(),
        P(),
    )
    return jax.shard_map(
        body,
        mesh=mesh,
        in_specs=placed,
        out_specs=(
            P("groups", None),
            P("groups", None),
            P("groups"),
            P("groups", None),
            P("groups"),
            P("groups", None),
            P("groups", None),
            P(None, ("groups", "cells", "freq")),
        ),
        check_vma=False,
    )
```

```python
import functools
import math

import jax
import jax.numpy as jnp
from jax import lax
from jax.experimental import pallas as pl
from jax.experimental.pallas import tpu as pltpu
from jax.sharding import PartitionSpec as P

SIDE = 1024

wave_low = 1.0
wave_high = 3.0
kernel_gain = 150.0

F32 = jnp.float32
BF16 = jnp.bfloat16
VMEM_BYTES = 40 * 1024 * 1024
SMALL_ROWS = 32
EARLY_BLOCKS = 1
WHOLE_VMEM = 64 * 1024 * 1024 - 256 * 1024


def silu_slope(value):
    sigma = jax.nn.sigmoid(value)
    return sigma * (1.0 + value * (1.0 - sigma))


def contract(left, right, left_dim, right_dim):
    return lax.dot_general(
        left, right, (((left_dim,), (right_dim,)), ((), ())), preferred_element_type=jnp.float32
    )


def kernel_tile(point_x, point_y, point_z, freq_value, cell_col, cell_row, count_freq):
    wave = wave_low + (wave_high - wave_low) * freq_value / (count_freq - 1)
    offset_x = point_x[:, None] - cell_col[None, :]
    offset_y = point_y[:, None] - cell_row[None, :]
    square = offset_x * offset_x + offset_y * offset_y + (point_z * point_z)[:, None]
    distance = jnp.sqrt(square)
    amplitude = kernel_gain * point_z[:, None] / square
    phase = wave[:, None] * distance
    return (
        (amplitude * jnp.cos(phase)).astype(jnp.bfloat16),
        (amplitude * jnp.sin(phase)).astype(jnp.bfloat16),
    )


def forward_pass(level_codes, cell_params, level_table, w_proj, w_one, b_one, w_two, b_two):
    levels = level_table.shape[0]
    onehot = (level_codes[:, None] == jnp.arange(levels, dtype=jnp.int32)[None, :]).astype(
        jnp.bfloat16
    )
    hidden_in = (
        jnp.dot(onehot, level_table, preferred_element_type=jnp.float32)
        + contract(cell_params, w_proj, 0, 0)
    ).astype(jnp.bfloat16)
    pre_one = jnp.dot(hidden_in, w_one, preferred_element_type=jnp.float32) + b_one
    act_one = jax.nn.silu(pre_one).astype(jnp.bfloat16)
    pre_two = jnp.dot(act_one, w_two, preferred_element_type=jnp.float32) + b_two
    act_two = jax.nn.silu(pre_two).astype(jnp.bfloat16)
    return (onehot, hidden_in, pre_one, act_one, pre_two, act_two)


def upper_grads(spectra, w_out, act_one, pre_two, act_two):
    back_two = contract(spectra, w_out, 0, 1)
    delta_two = (back_two * silu_slope(pre_two)).astype(jnp.bfloat16)
    grad_out = contract(act_two, spectra, 0, 1)
    grad_w2 = contract(act_one, delta_two, 0, 0)
    grad_b2 = jnp.sum(delta_two.astype(jnp.float32), axis=0)
    return ((grad_out, grad_w2, grad_b2), delta_two)


def lower_grads(delta_two, w_two, w_one, pre_one, hidden_in, onehot, cell_params, w_proj):
    back_one = contract(delta_two, w_two, 1, 1)
    delta_one = (back_one * silu_slope(pre_one)).astype(jnp.bfloat16)
    grad_w1 = contract(hidden_in, delta_one, 0, 0)
    grad_b1 = jnp.sum(delta_one.astype(jnp.float32), axis=0)
    back_zero = contract(delta_one, w_one, 1, 1).astype(jnp.bfloat16)
    grad_table = contract(onehot, back_zero, 0, 0)
    grad_proj = contract(cell_params, back_zero, 1, 0)
    grad_params = contract(w_proj, back_zero, 1, 1)
    return ((grad_w1, grad_b1, grad_table, grad_proj), grad_params)


def general_body(
    adjoint,
    target_x,
    target_y,
    target_z,
    assignment,
    level_codes,
    cell_params,
    level_table,
    w_proj,
    w_one,
    b_one,
    w_two,
    b_two,
    w_out,
):
    cell_count = level_codes.shape[0]
    freq_count = w_out.shape[1] // 2
    freq_size = lax.axis_size("freq")
    cell_rank = lax.axis_index("cells")
    freq_rank = lax.axis_index("freq")
    first_cell = (cell_rank * freq_size + freq_rank) * cell_count
    index = first_cell + jnp.arange(cell_count, dtype=jnp.int32)
    cell_col = (index % SIDE).astype(jnp.float32)
    cell_row = (index // SIDE).astype(jnp.float32)
    freq_grid = jnp.arange(freq_count, dtype=jnp.int32).astype(jnp.float32)
    stacked = jnp.concatenate(
        [
            adjoint,
            target_x[None, :],
            target_y[None, :],
            target_z[None, :],
            assignment.astype(jnp.float32)[None, :],
        ],
        axis=0,
    )
    total = jnp.zeros((2 * freq_count, cell_count), jnp.float32)
    piece = lax.all_gather(stacked, "cells", axis=1, tiled=True)
    length = piece.shape[1]
    block_len = math.gcd(length, 256)
    sections = piece.reshape(6, length // block_len, block_len).transpose(1, 0, 2)

    def inner(accum, rows):
        adj_round = rows[0:2].astype(jnp.bfloat16)
        kre, kim = kernel_tile(rows[2], rows[3], rows[4], rows[5], cell_col, cell_row, freq_count)
        select = (rows[5][:, None] == freq_grid[None, :]).astype(jnp.bfloat16)
        part_a = select * adj_round[0][:, None]
        part_b = select * adj_round[1][:, None]
        left_re = jnp.concatenate([part_a, part_b], axis=1)
        left_im = jnp.concatenate([part_b, -part_a], axis=1)
        return (accum + contract(left_re, kre, 0, 0) + contract(left_im, kim, 0, 0), None)

    total, unused = lax.scan(inner, total, sections)
    local_spec = total.astype(jnp.bfloat16)
    scale = 1.0 / math.sqrt(cell_count * lax.axis_size("cells") * freq_size)
    onehot, hidden_in, pre_one, act_one, pre_two, act_two = forward_pass(
        level_codes, cell_params, level_table, w_proj, w_one, b_one, w_two, b_two
    )
    upper, delta_two = upper_grads(local_spec, w_out, act_one, pre_two, act_two)
    lower, grad_params = lower_grads(
        delta_two, w_two, w_one, pre_one, hidden_in, onehot, cell_params, w_proj
    )
    totals = lax.psum(tuple(term * scale for term in upper + lower), ("cells", "freq"))
    return totals + (grad_params,)


def split(value, parts):
    pieces = []
    for _ in range(parts):
        piece = value.astype(BF16)
        pieces.append(piece.astype(F32))
        value = value - piece.astype(F32)
    return pieces


def fetch(sources, buffers, arrived):
    copies = [
        pltpu.make_async_copy(source, buffer, arrived.at[at])
        for at, (source, buffer) in enumerate(zip(sources, buffers))
    ]
    for copy in copies:
        copy.start()
    for copy in copies:
        copy.wait()


def pack_kernel(*refs):
    sources, (out_ref, flat_ref), buffers, (rows, arrived) = refs[:14], refs[14:16], refs[16:28], refs[28:]
    hidden = flat_ref.shape[1]
    base = SMALL_ROWS + 2 * hidden
    fetch(
        sources,
        [flat_ref.at[SMALL_ROWS : SMALL_ROWS + hidden], flat_ref.at[SMALL_ROWS + hidden : base]]
        + list(buffers),
        arrived,
    )
    wo_ref, buffers = buffers[0], buffers[1:]
    out_dim = wo_ref.shape[1]
    flat_ref[base:, 0:out_dim] = wo_ref[0 : hidden // 2]
    flat_ref[base:, out_dim:] = wo_ref[hidden // 2 :]
    adj_ref, x_ref, y_ref, z_ref, assign_ref, codes_ref, params_ref = buffers[:7]
    table_ref, proj_ref, b1_ref, b2_ref = buffers[7:]
    cells = codes_ref.shape[1]
    pieces = [adj_ref[0:1], adj_ref[1:2]]
    for ref in (x_ref, y_ref, z_ref):
        pieces += split(ref[...], 3)
    pieces.append(assign_ref[...].astype(F32))
    pieces += [jnp.zeros_like(pieces[0])] * 4
    codes = codes_ref[...].astype(F32)
    for at in range(4):
        rows[at : at + 1] = codes[:, at * 128 : (at + 1) * 128]
    rows[4:5] = jnp.concatenate(pieces[0:8], axis=1)
    rows[5:6] = jnp.concatenate(pieces[8:16], axis=1)
    rows[6:8] = jnp.zeros((2, 128), F32)
    out_ref[:, 0:cells] = params_ref[...]
    out_ref[:, cells:] = rows[...].astype(BF16)
    embed = [table_ref[...].astype(F32), proj_ref[...].astype(F32)]
    shifts = split(b1_ref[...], 3) + split(b2_ref[...], 3)
    rest = jnp.zeros((SMALL_ROWS - 30, hidden), F32)
    flat_ref[0:SMALL_ROWS] = jnp.concatenate(embed + shifts + [rest], axis=0).astype(BF16)


def stage_kernel(packed_ref, out_ref):
    out_ref[...] = packed_ref[...]


def weight_kernel(flat_ref, out_ref):
    hidden = flat_ref.shape[1]
    first = slice(SMALL_ROWS, SMALL_ROWS + hidden)
    small = flat_ref[0:SMALL_ROWS].astype(F32)
    stack = small[0:24]
    joined = dot(stack.astype(BF16), flat_ref[first])
    bias = (small[24:25] + small[25:26]) + small[26:27]
    joined = jnp.concatenate([joined, bias, jnp.zeros((7, hidden), F32)], axis=0)
    shifts = [0.5 * small[at : at + 1] for at in (27, 28, 29)]
    rows = split(0.5 * joined, 3) + shifts + [jnp.zeros((29, hidden), F32)]
    out_ref[:, 0:128] = jnp.concatenate(rows, axis=0).T.astype(BF16)
    second = flat_ref[SMALL_ROWS + hidden : SMALL_ROWS + 2 * hidden].astype(F32)
    out_ref[:, 128 : 128 + hidden] = (0.5 * second).T.astype(BF16)
    filled = [stack, jnp.zeros((8, hidden), F32)]
    rows = filled * 3 + [jnp.zeros((32, hidden), F32)]
    out_ref[:, 128 + hidden :] = jnp.concatenate(rows, axis=0).T.astype(BF16)


NEAR = (3.1051740646362305, -2.9883227348327637)
FAR = (0.9884209632873535, -4.203672885894775)


def dot(left, right):
    return jnp.dot(left, right, preferred_element_type=F32)


def feature_of(gathered_ref, slot):
    width = gathered_ref.shape[2]
    cells = width - 128
    rows = gathered_ref[slot, :, cells:].astype(F32)
    codes = jnp.concatenate(
        [jnp.broadcast_to(rows[at : at + 1], (8, 128)) for at in range(4)], axis=1
    )
    steps = lax.broadcasted_iota(jnp.int32, (8, cells), 0).astype(F32)
    blocks = [
        jnp.where(codes == steps, 1.0, 0.0),
        jnp.where(codes == steps + 8.0, 1.0, 0.0),
        gathered_ref[slot, :, 0:cells].astype(F32),
        jnp.where(steps == 0.0, 1.0, 0.0),
    ]
    return jnp.concatenate(blocks, axis=0).astype(BF16)


def activate(half):
    tanh = jnp.tanh(half)
    gate = 1.0 + tanh
    act = half * gate
    return act.astype(BF16), gate + act * (1.0 - tanh)


def layer_one(weights_ref, feature):
    rows = [feature] * 3 + [jnp.zeros((32, feature.shape[1]), BF16)]
    return dot(weights_ref[:, 0:128], jnp.concatenate(rows, axis=0))


def bias_of(weights_ref):
    shift = weights_ref[:, 96:128].astype(F32)
    shift = (shift[:, 0:1] + shift[:, 1:2]) + shift[:, 2:3]
    return jnp.broadcast_to(shift, (shift.shape[0], 128))


def forward_kernel(
    begin, gathered_ref, weights_ref, one_ref, slope_one_ref, two_ref, slope_two_ref, bias
):
    count, hidden, cells = one_ref.shape
    bias[...] = bias_of(weights_ref)
    wide = jnp.concatenate([bias[...]] * (cells // 128), axis=1)

    def first(slot):
        act, slope = activate(layer_one(weights_ref, feature_of(gathered_ref, begin + slot)))
        one_ref[slot] = act
        slope_one_ref[slot] = slope

    def second(slot):
        half = dot(weights_ref[:, 128 : 128 + hidden], one_ref[slot]) + wide
        act, slope = activate(half)
        two_ref[slot] = act
        slope_two_ref[slot] = slope

    first(0)
    for slot in range(1, count):
        second(slot - 1)
        first(slot)
    second(count - 1)


def lay_targets(tiles, first_col, freqs, where, across, near, far):
    count = len(tiles)
    fill = [jnp.zeros((8 - count % 8, 128), F32)] if count % 8 else []
    low = jnp.concatenate([tile[4:5] for tile in tiles] + fill, axis=0).T
    high = jnp.concatenate([tile[5:6] for tile in tiles] + fill, axis=0).T
    parts = [low[at * 16 : (at + 1) * 16] for at in range(8)]
    parts += [high[at * 16 : (at + 1) * 16] for at in range(4)]
    point_x = (parts[2] + parts[3]) + parts[4]
    point_y = (parts[5] + parts[6]) + parts[7]
    point_z = (parts[8] + parts[9]) + parts[10]
    wave = (wave_low + (wave_high - wave_low) * parts[11] / (freqs - 1)) * (0.5 / math.pi)
    cells = across.shape[1]
    sides = [
        first_col + lane + lax.broadcasted_iota(jnp.int32, (1, 128), 1)
        for lane in range(0, cells, 128)
    ]
    sides = [lax.rem(side, SIDE).astype(F32) for side in sides]
    grid = lax.broadcasted_iota(jnp.int32, (16, freqs), 1).astype(F32)
    for chunk in range(count):
        here = slice(chunk * 16, chunk * 16 + 16)

        def spread(value):
            return jnp.broadcast_to(value[:, chunk : chunk + 1], (16, 128))

        square = spread(wave * wave)
        where[0, here] = spread(point_y)
        where[1, here] = spread(wave * wave * (point_z * point_z))
        where[2, here] = spread(kernel_gain * point_z * (wave * wave))
        where[3, here] = square
        wide = spread(point_x)
        for at, side in enumerate(sides):
            offset = wide - side
            across[here, at * 128 : (at + 1) * 128] = offset * offset * square
        select = jnp.where(spread(parts[11])[:, 0:freqs] == grid, 1.0, 0.0)
        part_a = select * spread(parts[0])[:, 0:freqs]
        part_b = select * spread(parts[1])[:, 0:freqs]
        near[here] = jnp.concatenate([part_a, part_b], axis=1)
        far[here] = jnp.concatenate([part_b, -part_a], axis=1)


def hologram_pieces(row, where, across, waves):
    for at in range(0, across.shape[0], 16):
        here = slice(at, at + 16)
        offset = where[0, here] - row
        rest = offset * offset * where[3, here] + where[1, here]
        for lane in range(0, across.shape[1], 128):
            lanes = slice(lane, lane + 128)
            square = across[here, lanes] + rest
            turns = square * lax.rsqrt(square)
            part = turns - jnp.round(turns)
            power = part * part
            sine = part * (NEAR[1] * power + NEAR[0])
            cosine = (power + FAR[1]) * power + FAR[0]
            sine_square = sine * sine
            cosine_square = cosine * cosine
            norm = square * (sine_square + cosine_square)
            amplitude = where[2, here] * pl.reciprocal(norm, approx=True)
            waves[0, here, lanes] = (
                amplitude * (cosine_square - sine_square)
            ).astype(BF16)
            waves[1, here, lanes] = (
                amplitude * ((sine + sine) * cosine)
            ).astype(BF16)
            yield


def early_kernel(freq_size, freqs, place_ref, gathered_ref, where, across, near, far, waves):
    count, _, width = gathered_ref.shape
    cells = width - 128
    me, freq_rank = place_ref[0], place_ref[1]
    local = lax.bitwise_and(me, count - 1)
    tiles = [
        gathered_ref[lax.bitwise_xor(local, at), :, cells:].astype(F32) for at in range(count)
    ]
    lay_targets(tiles, freq_rank * cells, freqs, where, across, near, far)
    for block in range(waves.shape[0]):
        chunk = lax.bitwise_xor(me, block)
        row = ((chunk * freq_size + freq_rank) * cells // SIDE).astype(F32)
        for _ in hologram_pieces(row, where, across, waves.at[block]):
            pass


def cell_kernel(
    freq_size,
    place_ref, gathered_ref, weights_ref, flat_ref, *refs
):
    chunks, _, width = gathered_ref.shape
    cells = width - 128
    hidden = flat_ref.shape[1]
    early = [refs[at : at + 4] for at in range(5, len(refs) - 16, 4)]
    early_where, early_across, early_near, early_far, early_waves = refs[0:5]
    sums_ref, grad_params_ref, across, where, near, far, lift, bias, totals, waves = refs[-16:-6]
    delta_two, spectra = refs[-6:-4]
    early.append(refs[-4:])
    freqs = lift.shape[0] // 2
    base = SMALL_ROWS + 2 * hidden
    half_rows = slice(base, base + hidden // 2)
    w2_ref = flat_ref.at[SMALL_ROWS + hidden : base]
    targets = chunks * 16
    me = place_ref[0]
    freq_rank = place_ref[1]
    stride = freq_size * cells
    second_ref = weights_ref.at[:, 128 : 128 + hidden]

    ready = chunks - refs[-4].shape[0]
    upper_first = lax.bitwise_and(me, ready) != 0

    def in_order(own, new):
        low = lax.select(upper_first, new, own)
        return jnp.concatenate([low, lax.select(upper_first, own, new)], axis=0)

    local = lax.bitwise_and(me, ready - 1)
    tiles = [
        gathered_ref[ready + lax.bitwise_xor(local, at), :, cells:].astype(F32)
        for at in range(ready)
    ]
    lay_targets(tiles, freq_rank * cells, freqs, where, across, near, far)
    lift[:, 0:targets] = in_order(early_near[...], near[...]).T.astype(BF16)
    lift[:, targets:] = in_order(early_far[...], far[...]).T.astype(BF16)
    bias[...] = bias_of(weights_ref)

    middle = hidden + 32
    top = middle + 2 * freqs
    owners = [(part, at) for part in early for at in range(part[0].shape[0])]

    def layers(block):
        part, at = owners[block]
        return [ref.at[at] for ref in part]

    def back_out(spectrum):
        upper_rows = dot(flat_ref[half_rows, 0 : 2 * freqs], spectrum)
        lower_rows = dot(flat_ref[half_rows, 2 * freqs : 4 * freqs], spectrum)
        return jnp.concatenate([upper_rows, lower_rows], axis=0)

    def holograms(block, even):
        row = ((lax.bitwise_xor(me, block) * stride + freq_rank * cells) // SIDE).astype(F32)
        if block >= EARLY_BLOCKS:
            yield from hologram_pieces(row, early_where, early_across, waves.at[even, 0])
        yield from hologram_pieces(row, where, across, waves.at[even, 1])

    def kernels_of(block, even):
        own = early_waves.at[block] if block < EARLY_BLOCKS else waves.at[even, 0]
        new = waves.at[even, 1]
        return jnp.concatenate([in_order(own[at], new[at]) for at in range(2)], axis=0)

    def lower(block, even):
        total = totals.at[lax.bitwise_xor(me, block) // 2]

        def outer(low, left, right):
            rows = slice(low, low + left.shape[0])
            product = contract(left, right, 1, 1)
            total[rows] = total[rows] + product if block % 2 else product

        one, slope, two, _ = layers(block)
        feature = feature_of(gathered_ref, block)
        delta = delta_two[even]
        back = dot(w2_ref[...], delta)
        outer(middle, spectra[even], two[...])
        yield
        value = (back * slope[...]).astype(BF16)
        if block == 0:
            both = contract(weights_ref[:, 0:128], value, 0, 0)
            grad_params_ref[...] = 0.5 * ((both[16:24] + both[48:56]) + both[80:88])
        yield
        outer(0, jnp.concatenate([one[...], feature], axis=0), delta)
        yield
        outer(top, feature, value)
        yield

    def upper(block, even):
        spectrum = dot(lift[...], kernels_of(block, even)).astype(BF16)
        spectra[even] = spectrum
        yield
        back = back_out(spectrum)
        yield
        delta_two[even] = (back * layers(block)[3][...]).astype(BF16)
        yield

    def first(block):
        one, slope_one, _, _ = layers(block)
        half = layer_one(weights_ref, feature_of(gathered_ref, block))
        yield
        one[...], slope_one[...] = activate(half)
        yield

    def second(block):
        one, _, two, slope_two = layers(block)
        half = dot(second_ref[...], one[...])
        half = half + jnp.concatenate([bias[...]] * (cells // 128), axis=1)
        yield
        two[...], slope_two[...] = activate(half)
        yield

    for at in range(chunks + 2):
        waiting = []
        if 0 <= at - 1 < chunks:
            waiting.append((upper(at - 1, (at - 1) % 2), 3))
        if ready <= at + ready - 1 < chunks:
            waiting.append((second(at + ready - 1), 2))
        if at + ready < chunks:
            waiting.append((first(at + ready), 2))
        if 0 <= at - 2 < chunks:
            waiting.append((lower(at - 2, at % 2), 4))
        spots = sum(count for _, count in waiting)
        waiting = [stage for stage, _ in waiting]
        pieces, extra = 0, None
        if at < chunks:
            pieces = (targets // (32 if at < EARLY_BLOCKS else 16)) * (cells // 128)
            extra = holograms(at, at % 2)
        done, drawn = 0, 0
        while waiting:
            for stage in list(waiting):
                if next(stage, True) is True:
                    waiting.remove(stage)
                    continue
                done += 1
                while drawn < pieces * done // spots:
                    next(extra)
                    drawn += 1
        if pieces:
            for _ in extra:
                pass
    pairs = chunks // 2
    added = [totals.at[at] for at in range(pairs)]
    for low in range(0, totals.shape[1], 16):
        terms = [ref[low : low + 16] for ref in added]
        while len(terms) > 1:
            terms = [terms[at] + terms[at + 1] for at in range(0, len(terms), 2)]
        sums_ref[low : low + 16] = terms[0].astype(BF16)


def finish_kernel(
    scale, own_ref, other_ref, weights_ref, flat_ref,
    out_ref, w2_ref, b2_ref, wone_ref, b1_ref, table_ref, proj_ref,
):
    hidden = flat_ref.shape[1]
    middle = hidden + 32
    top = middle + out_ref.shape[1]
    levels = table_ref.shape[0]
    used = levels + proj_ref.shape[0]

    def total(low, high, factor):
        both = own_ref[low:high].astype(F32) + other_ref[low:high].astype(F32)
        return both * (scale * factor)

    w2_ref[...] = total(0, hidden, 0.5)
    out_ref[...] = total(middle, top, 1.0).T
    feature = total(top, top + 32, 0.25)
    b1_ref[...] = feature[used : used + 1]
    b2_ref[...] = total(hidden, middle, 0.5)[used : used + 1]
    rows = jnp.concatenate(split(feature, 3), axis=0).astype(BF16)
    embed = weights_ref[:, 128 + hidden : 128 + hidden + 96]
    wone_ref[...] = jnp.dot(embed, rows, preferred_element_type=F32)
    back = contract(rows, flat_ref[SMALL_ROWS : SMALL_ROWS + hidden], 1, 1)
    back = (back[0:32] + back[32:64]) + back[64:96]
    table_ref[...] = back[0:levels]
    proj_ref[...] = back[levels:used]


def run_forward(gathered, weights, begin, count):
    hidden = weights.shape[0]
    block = (count, hidden, gathered.shape[2] - 128)
    return pl.pallas_call(
        functools.partial(forward_kernel, begin),
        out_shape=[jax.ShapeDtypeStruct(block, kind) for kind in (BF16, F32, BF16, F32)],
        scratch_shapes=[pltpu.VMEM((hidden, 128), F32)],
        compiler_params=pltpu.CompilerParams(vmem_limit_bytes=VMEM_BYTES),
        name="early_forward",
    )(gathered, weights)


def run_early(place, gathered, freq_size, out_dim):
    count, _, width = gathered.shape
    cells = width - 128
    known = count * 16
    vmem = pl.BlockSpec(memory_space=pltpu.VMEM)
    return pl.pallas_call(
        functools.partial(early_kernel, freq_size, out_dim // 2),
        out_shape=[
            jax.ShapeDtypeStruct((4, known, 128), F32),
            jax.ShapeDtypeStruct((known, cells), F32),
            jax.ShapeDtypeStruct((known, out_dim), F32),
            jax.ShapeDtypeStruct((known, out_dim), F32),
            jax.ShapeDtypeStruct((EARLY_BLOCKS, 2, known, cells), BF16),
        ],
        in_specs=[pl.BlockSpec(memory_space=pltpu.SMEM), vmem],
        compiler_params=pltpu.CompilerParams(vmem_limit_bytes=VMEM_BYTES),
        name="early_holograms",
    )(place, gathered)


def run_cells(place, gathered, weights, flat, waves, early, freq_size, out_dim):
    chunks, props, width = gathered.shape
    cells = width - 128
    hidden = flat.shape[1]
    targets = chunks * 16
    rest = chunks - sum(part[0].shape[0] for part in early)
    rows = hidden + out_dim + 64
    vmem = pl.BlockSpec(memory_space=pltpu.VMEM)
    flattened = list(waves) + [array for part in early for array in part]
    return pl.pallas_call(
        functools.partial(cell_kernel, freq_size),
        out_shape=(
            jax.ShapeDtypeStruct((rows, hidden), BF16),
            jax.ShapeDtypeStruct((props, cells), F32),
        ),
        in_specs=[pl.BlockSpec(memory_space=pltpu.SMEM)] + [vmem] * (3 + len(flattened)),
        out_specs=(vmem, vmem),
        scratch_shapes=[
            pltpu.VMEM((targets // 2, cells), F32),
            pltpu.VMEM((4, targets // 2, 128), F32),
            pltpu.VMEM((targets // 2, out_dim), F32),
            pltpu.VMEM((targets // 2, out_dim), F32),
            pltpu.VMEM((out_dim, 2 * targets), BF16),
            pltpu.VMEM((hidden, 128), F32),
            pltpu.VMEM((chunks // 2, rows, hidden), F32),
            pltpu.VMEM((2, 2, 2, targets // 2, cells), BF16),
            pltpu.VMEM((2, hidden, cells), BF16),
            pltpu.VMEM((2, out_dim, cells), BF16),
        ]
        + [pltpu.VMEM((rest, hidden, cells), kind) for kind in (BF16, F32, BF16, F32)],
        compiler_params=pltpu.CompilerParams(vmem_limit_bytes=VMEM_BYTES),
        name="all_cells",
    )(place, gathered, weights, flat, *flattened)


def small_body(
    adjoint,
    target_x,
    target_y,
    target_z,
    assignment,
    level_codes,
    cell_params,
    level_table,
    w_proj,
    w_one,
    b_one,
    w_two,
    b_two,
    w_out,
):
    cells = level_codes.shape[0]
    local = target_x.shape[0]
    levels, hidden = level_table.shape
    props = w_proj.shape[0]
    freqs = w_out.shape[1] // 2
    chunks = lax.axis_size("cells")
    freq_size = lax.axis_size("freq")
    shape = jax.ShapeDtypeStruct
    params = pltpu.CompilerParams(vmem_limit_bytes=VMEM_BYTES)

    def fetched(arrays):
        buffers = [pltpu.VMEM(array.shape, array.dtype) for array in arrays]
        return buffers, pltpu.SemaphoreType.DMA((len(arrays),))

    inputs = (
        w_one, w_two, w_out,
        adjoint, target_x[None, :], target_y[None, :], target_z[None, :], assignment[None, :],
        level_codes[None, :], cell_params, level_table, w_proj, b_one[None, :], b_two[None, :],
    )
    whole = pltpu.CompilerParams(vmem_limit_bytes=WHOLE_VMEM)
    buffers, arrived = fetched(inputs)
    packed, flat = pl.pallas_call(
        pack_kernel,
        out_shape=(
            shape((props, cells + 128), BF16),
            shape((SMALL_ROWS + 2 * hidden + hidden // 2, hidden), BF16),
        ),
        in_specs=[pl.BlockSpec(memory_space=pltpu.HBM)] * len(inputs),
        scratch_shapes=buffers[2:] + [pltpu.VMEM((8, 128), F32), arrived],
        compiler_params=whole,
        name="pack_inputs",
    )(*inputs)
    staged = pl.pallas_call(
        stage_kernel,
        out_shape=shape((props, cells + 128), BF16),
        compiler_params=params,
        name="stage_own",
    )(packed)
    moved = lax.ppermute(packed[None], "cells", [(at, at ^ 1) for at in range(chunks)])
    weights = pl.pallas_call(
        weight_kernel,
        out_shape=shape((hidden, 256 + hidden), BF16),
        compiler_params=params,
        name="prepare_weights",
    )(flat)
    gathered = jnp.concatenate([staged[None], moved], axis=0)
    gathered, weights = lax.optimization_barrier((gathered, weights))
    place = jnp.stack([lax.axis_index("cells"), lax.axis_index("freq")]).astype(jnp.int32)
    out_dim = w_out.shape[1]
    reach, begin, early = 2, 0, []
    while reach < chunks:
        moved = lax.ppermute(gathered, "cells", [(at, at ^ reach) for at in range(chunks)])
        early.append(run_forward(gathered, weights, begin, reach - begin))
        if 2 * reach == chunks:
            waves = run_early(place, gathered, freq_size, out_dim)
        begin = reach
        gathered = jnp.concatenate([gathered, moved], axis=0)
        gathered, early = lax.optimization_barrier((gathered, early))
        reach *= 2

    sums, grad_params = run_cells(
        place, gathered, weights, flat, waves, early, freq_size, out_dim
    )

    other = lax.ppermute(sums, "freq", [(at, at ^ 1) for at in range(freq_size)])
    scale = 1.0 / math.sqrt(cells * chunks * freq_size)
    grad_out, grad_w2, grad_b2, grad_w1, grad_b1, grad_table, grad_proj = pl.pallas_call(
        functools.partial(finish_kernel, scale),
        out_shape=(
            shape((hidden, 2 * freqs), F32),
            shape((hidden, hidden), F32),
            shape((1, hidden), F32),
            shape((hidden, hidden), F32),
            shape((1, hidden), F32),
            shape((levels, hidden), F32),
            shape((props, hidden), F32),
        ),
        compiler_params=params,
        name="finish_sums",
    )(sums, other, weights, flat)
    return (
        grad_out, grad_w2, grad_b2[0], grad_w1, grad_b1[0], grad_table, grad_proj, grad_params,
    )


def solution(mesh):
    chunks = mesh.shape["cells"]
    paired = mesh.shape["freq"] == 2 and chunks > 2 and chunks & (chunks - 1) == 0

    def body(*args):
        local = args[1].shape[0]
        cells = args[5].shape[0]
        hidden = args[9].shape[0]
        suits = (
            paired
            and local == 16
            and cells == 512
            and chunks * cells * chunks * local <= 1 << 20
            and args[7].shape[0] == 16
            and args[8].shape[0] == 8
            and hidden == 2 * args[13].shape[1]
            and mesh.shape["freq"] * cells % SIDE == 0
            and SIDE % cells == 0
            and args[13].shape[1] == 128
        )
        return (small_body if suits else general_body)(*args)

    placed = (
        P(None, ("groups", "cells")),
        P(("groups", "cells")),
        P(("groups", "cells")),
        P(("groups", "cells")),
        P(("groups", "cells")),
        P(("groups", "cells", "freq")),
        P(None, ("groups", "cells", "freq")),
        P(),
        P(),
        P(),
        P(),
        P(),
        P(),
        P(),
    )
    return jax.shard_map(
        body,
        mesh=mesh,
        in_specs=placed,
        out_specs=(
            P("groups", None),
            P("groups", None),
            P("groups"),
            P("groups", None),
            P("groups"),
            P("groups", None),
            P("groups", None),
            P(None, ("groups", "cells", "freq")),
        ),
        check_vma=False,
    )
```

```python
import functools
import math

import jax
import jax.numpy as jnp
from jax import lax
from jax.experimental import pallas as pl
from jax.experimental.pallas import tpu as pltpu
from jax.sharding import PartitionSpec as P

SIDE = 1024

wave_low = 1.0
wave_high = 3.0
kernel_gain = 150.0

F32 = jnp.float32
BF16 = jnp.bfloat16
VMEM_BYTES = 40 * 1024 * 1024
SMALL_ROWS = 32
EARLY_BLOCKS = 1
WHOLE_VMEM = 64 * 1024 * 1024 - 256 * 1024


def silu_slope(value):
    sigma = jax.nn.sigmoid(value)
    return sigma * (1.0 + value * (1.0 - sigma))


def contract(left, right, left_dim, right_dim):
    return lax.dot_general(
        left, right, (((left_dim,), (right_dim,)), ((), ())), preferred_element_type=jnp.float32
    )


def kernel_tile(point_x, point_y, point_z, freq_value, cell_col, cell_row, count_freq):
    wave = wave_low + (wave_high - wave_low) * freq_value / (count_freq - 1)
    offset_x = point_x[:, None] - cell_col[None, :]
    offset_y = point_y[:, None] - cell_row[None, :]
    square = offset_x * offset_x + offset_y * offset_y + (point_z * point_z)[:, None]
    distance = jnp.sqrt(square)
    amplitude = kernel_gain * point_z[:, None] / square
    phase = wave[:, None] * distance
    return (
        (amplitude * jnp.cos(phase)).astype(jnp.bfloat16),
        (amplitude * jnp.sin(phase)).astype(jnp.bfloat16),
    )


def forward_pass(level_codes, cell_params, level_table, w_proj, w_one, b_one, w_two, b_two):
    levels = level_table.shape[0]
    onehot = (level_codes[:, None] == jnp.arange(levels, dtype=jnp.int32)[None, :]).astype(
        jnp.bfloat16
    )
    hidden_in = (
        jnp.dot(onehot, level_table, preferred_element_type=jnp.float32)
        + contract(cell_params, w_proj, 0, 0)
    ).astype(jnp.bfloat16)
    pre_one = jnp.dot(hidden_in, w_one, preferred_element_type=jnp.float32) + b_one
    act_one = jax.nn.silu(pre_one).astype(jnp.bfloat16)
    pre_two = jnp.dot(act_one, w_two, preferred_element_type=jnp.float32) + b_two
    act_two = jax.nn.silu(pre_two).astype(jnp.bfloat16)
    return (onehot, hidden_in, pre_one, act_one, pre_two, act_two)


def upper_grads(spectra, w_out, act_one, pre_two, act_two):
    back_two = contract(spectra, w_out, 0, 1)
    delta_two = (back_two * silu_slope(pre_two)).astype(jnp.bfloat16)
    grad_out = contract(act_two, spectra, 0, 1)
    grad_w2 = contract(act_one, delta_two, 0, 0)
    grad_b2 = jnp.sum(delta_two.astype(jnp.float32), axis=0)
    return ((grad_out, grad_w2, grad_b2), delta_two)


def lower_grads(delta_two, w_two, w_one, pre_one, hidden_in, onehot, cell_params, w_proj):
    back_one = contract(delta_two, w_two, 1, 1)
    delta_one = (back_one * silu_slope(pre_one)).astype(jnp.bfloat16)
    grad_w1 = contract(hidden_in, delta_one, 0, 0)
    grad_b1 = jnp.sum(delta_one.astype(jnp.float32), axis=0)
    back_zero = contract(delta_one, w_one, 1, 1).astype(jnp.bfloat16)
    grad_table = contract(onehot, back_zero, 0, 0)
    grad_proj = contract(cell_params, back_zero, 1, 0)
    grad_params = contract(w_proj, back_zero, 1, 1)
    return ((grad_w1, grad_b1, grad_table, grad_proj), grad_params)


def general_body(
    adjoint,
    target_x,
    target_y,
    target_z,
    assignment,
    level_codes,
    cell_params,
    level_table,
    w_proj,
    w_one,
    b_one,
    w_two,
    b_two,
    w_out,
):
    cell_count = level_codes.shape[0]
    freq_count = w_out.shape[1] // 2
    freq_size = lax.axis_size("freq")
    cell_rank = lax.axis_index("cells")
    freq_rank = lax.axis_index("freq")
    first_cell = (cell_rank * freq_size + freq_rank) * cell_count
    index = first_cell + jnp.arange(cell_count, dtype=jnp.int32)
    cell_col = (index % SIDE).astype(jnp.float32)
    cell_row = (index // SIDE).astype(jnp.float32)
    freq_grid = jnp.arange(freq_count, dtype=jnp.int32).astype(jnp.float32)
    stacked = jnp.concatenate(
        [
            adjoint,
            target_x[None, :],
            target_y[None, :],
            target_z[None, :],
            assignment.astype(jnp.float32)[None, :],
        ],
        axis=0,
    )
    total = jnp.zeros((2 * freq_count, cell_count), jnp.float32)
    piece = lax.all_gather(stacked, "cells", axis=1, tiled=True)
    length = piece.shape[1]
    block_len = math.gcd(length, 256)
    sections = piece.reshape(6, length // block_len, block_len).transpose(1, 0, 2)

    def inner(accum, rows):
        adj_round = rows[0:2].astype(jnp.bfloat16)
        kre, kim = kernel_tile(rows[2], rows[3], rows[4], rows[5], cell_col, cell_row, freq_count)
        select = (rows[5][:, None] == freq_grid[None, :]).astype(jnp.bfloat16)
        part_a = select * adj_round[0][:, None]
        part_b = select * adj_round[1][:, None]
        left_re = jnp.concatenate([part_a, part_b], axis=1)
        left_im = jnp.concatenate([part_b, -part_a], axis=1)
        return (accum + contract(left_re, kre, 0, 0) + contract(left_im, kim, 0, 0), None)

    total, unused = lax.scan(inner, total, sections)
    local_spec = total.astype(jnp.bfloat16)
    scale = 1.0 / math.sqrt(cell_count * lax.axis_size("cells") * freq_size)
    onehot, hidden_in, pre_one, act_one, pre_two, act_two = forward_pass(
        level_codes, cell_params, level_table, w_proj, w_one, b_one, w_two, b_two
    )
    upper, delta_two = upper_grads(local_spec, w_out, act_one, pre_two, act_two)
    lower, grad_params = lower_grads(
        delta_two, w_two, w_one, pre_one, hidden_in, onehot, cell_params, w_proj
    )
    totals = lax.psum(tuple(term * scale for term in upper + lower), ("cells", "freq"))
    return totals + (grad_params,)


def split(value, parts):
    pieces = []
    for _ in range(parts):
        piece = value.astype(BF16)
        pieces.append(piece.astype(F32))
        value = value - piece.astype(F32)
    return pieces


def fetch(sources, buffers, arrived):
    copies = [
        pltpu.make_async_copy(source, buffer, arrived.at[at])
        for at, (source, buffer) in enumerate(zip(sources, buffers))
    ]
    for copy in copies:
        copy.start()
    for copy in copies:
        copy.wait()


def pack_kernel(*refs):
    sources, (out_ref, flat_ref), buffers, (rows, arrived) = refs[:14], refs[14:16], refs[16:28], refs[28:]
    hidden = flat_ref.shape[1]
    base = SMALL_ROWS + 2 * hidden
    fetch(
        sources,
        [flat_ref.at[SMALL_ROWS : SMALL_ROWS + hidden], flat_ref.at[SMALL_ROWS + hidden : base]]
        + list(buffers),
        arrived,
    )
    wo_ref, buffers = buffers[0], buffers[1:]
    out_dim = wo_ref.shape[1]
    flat_ref[base:, 0:out_dim] = wo_ref[0 : hidden // 2]
    flat_ref[base:, out_dim:] = wo_ref[hidden // 2 :]
    adj_ref, x_ref, y_ref, z_ref, assign_ref, codes_ref, params_ref = buffers[:7]
    table_ref, proj_ref, b1_ref, b2_ref = buffers[7:]
    cells = codes_ref.shape[1]
    pieces = [adj_ref[0:1], adj_ref[1:2]]
    for ref in (x_ref, y_ref, z_ref):
        pieces += split(ref[...], 3)
    pieces.append(assign_ref[...].astype(F32))
    pieces += [jnp.zeros_like(pieces[0])] * 4
    codes = codes_ref[...].astype(F32)
    for at in range(4):
        rows[at : at + 1] = codes[:, at * 128 : (at + 1) * 128]
    rows[4:5] = jnp.concatenate(pieces[0:8], axis=1)
    rows[5:6] = jnp.concatenate(pieces[8:16], axis=1)
    rows[6:8] = jnp.zeros((2, 128), F32)
    out_ref[:, 0:cells] = params_ref[...]
    out_ref[:, cells:] = rows[...].astype(BF16)
    embed = [table_ref[...].astype(F32), proj_ref[...].astype(F32)]
    shifts = split(b1_ref[...], 3) + split(b2_ref[...], 3)
    rest = jnp.zeros((SMALL_ROWS - 30, hidden), F32)
    flat_ref[0:SMALL_ROWS] = jnp.concatenate(embed + shifts + [rest], axis=0).astype(BF16)


def stage_kernel(packed_ref, out_ref):
    out_ref[...] = packed_ref[...]


def weight_kernel(flat_ref, out_ref):
    hidden = flat_ref.shape[1]
    first = slice(SMALL_ROWS, SMALL_ROWS + hidden)
    small = flat_ref[0:SMALL_ROWS].astype(F32)
    stack = small[0:24]
    joined = dot(stack.astype(BF16), flat_ref[first])
    bias = (small[24:25] + small[25:26]) + small[26:27]
    joined = jnp.concatenate([joined, bias, jnp.zeros((7, hidden), F32)], axis=0)
    shifts = [0.5 * small[at : at + 1] for at in (27, 28, 29)]
    rows = split(0.5 * joined, 3) + shifts + [jnp.zeros((29, hidden), F32)]
    out_ref[:, 0:128] = jnp.concatenate(rows, axis=0).T.astype(BF16)
    second = flat_ref[SMALL_ROWS + hidden : SMALL_ROWS + 2 * hidden].astype(F32)
    out_ref[:, 128 : 128 + hidden] = (0.5 * second).T.astype(BF16)
    filled = [stack, jnp.zeros((8, hidden), F32)]
    rows = filled * 3 + [jnp.zeros((32, hidden), F32)]
    out_ref[:, 128 + hidden :] = jnp.concatenate(rows, axis=0).T.astype(BF16)


NEAR = (3.1051740646362305, -2.9883227348327637)
FAR = (0.9884209632873535, -4.203672885894775)


def dot(left, right):
    return jnp.dot(left, right, preferred_element_type=F32)


def feature_of(gathered_ref, slot):
    width = gathered_ref.shape[2]
    cells = width - 128
    rows = gathered_ref[slot, :, cells:].astype(F32)
    codes = jnp.concatenate(
        [jnp.broadcast_to(rows[at : at + 1], (8, 128)) for at in range(4)], axis=1
    )
    steps = lax.broadcasted_iota(jnp.int32, (8, cells), 0).astype(F32)
    blocks = [
        jnp.where(codes == steps, 1.0, 0.0),
        jnp.where(codes == steps + 8.0, 1.0, 0.0),
        gathered_ref[slot, :, 0:cells].astype(F32),
        jnp.where(steps == 0.0, 1.0, 0.0),
    ]
    return jnp.concatenate(blocks, axis=0).astype(BF16)


def activate(half):
    tanh = jnp.tanh(half)
    gate = 1.0 + tanh
    act = half * gate
    return act.astype(BF16), gate + act * (1.0 - tanh)


def layer_one(weights_ref, feature):
    rows = [feature] * 3 + [jnp.zeros((32, feature.shape[1]), BF16)]
    return dot(weights_ref[:, 0:128], jnp.concatenate(rows, axis=0))


def bias_of(weights_ref):
    shift = weights_ref[:, 96:128].astype(F32)
    shift = (shift[:, 0:1] + shift[:, 1:2]) + shift[:, 2:3]
    return jnp.broadcast_to(shift, (shift.shape[0], 128))


def forward_kernel(
    begin, gathered_ref, weights_ref, one_ref, slope_one_ref, two_ref, slope_two_ref, bias
):
    count, hidden, cells = one_ref.shape
    bias[...] = bias_of(weights_ref)
    wide = jnp.concatenate([bias[...]] * (cells // 128), axis=1)

    def first(slot):
        act, slope = activate(layer_one(weights_ref, feature_of(gathered_ref, begin + slot)))
        one_ref[slot] = act
        slope_one_ref[slot] = slope

    def second(slot):
        half = dot(weights_ref[:, 128 : 128 + hidden], one_ref[slot]) + wide
        act, slope = activate(half)
        two_ref[slot] = act
        slope_two_ref[slot] = slope

    for slot in range(count):
        first(slot)
    for slot in range(count):
        second(slot)


def lay_targets(tiles, first_col, freqs, where, across, near, far):
    count = len(tiles)
    fill = [jnp.zeros((8 - count % 8, 128), F32)] if count % 8 else []
    low = jnp.concatenate([tile[4:5] for tile in tiles] + fill, axis=0).T
    high = jnp.concatenate([tile[5:6] for tile in tiles] + fill, axis=0).T
    parts = [low[at * 16 : (at + 1) * 16] for at in range(8)]
    parts += [high[at * 16 : (at + 1) * 16] for at in range(4)]
    point_x = (parts[2] + parts[3]) + parts[4]
    point_y = (parts[5] + parts[6]) + parts[7]
    point_z = (parts[8] + parts[9]) + parts[10]
    wave = (wave_low + (wave_high - wave_low) * parts[11] / (freqs - 1)) * (0.5 / math.pi)
    cells = across.shape[1]
    sides = [
        first_col + lane + lax.broadcasted_iota(jnp.int32, (1, 128), 1)
        for lane in range(0, cells, 128)
    ]
    sides = [lax.rem(side, SIDE).astype(F32) for side in sides]
    grid = lax.broadcasted_iota(jnp.int32, (16, freqs), 1).astype(F32)
    for chunk in range(count):
        here = slice(chunk * 16, chunk * 16 + 16)

        def spread(value):
            return jnp.broadcast_to(value[:, chunk : chunk + 1], (16, 128))

        square = spread(wave * wave)
        where[0, here] = spread(point_y)
        where[1, here] = spread(wave * wave * (point_z * point_z))
        where[2, here] = spread(kernel_gain * point_z * (wave * wave))
        where[3, here] = square
        wide = spread(point_x)
        for at, side in enumerate(sides):
            offset = wide - side
            across[here, at * 128 : (at + 1) * 128] = offset * offset * square
        select = jnp.where(spread(parts[11])[:, 0:freqs] == grid, 1.0, 0.0)
        part_a = select * spread(parts[0])[:, 0:freqs]
        part_b = select * spread(parts[1])[:, 0:freqs]
        near[here] = jnp.concatenate([part_a, part_b], axis=1)
        far[here] = jnp.concatenate([part_b, -part_a], axis=1)


def hologram_pieces(row, where, across, waves):
    for at in range(0, across.shape[0], 16):
        here = slice(at, at + 16)
        offset = where[0, here] - row
        rest = offset * offset * where[3, here] + where[1, here]
        for lane in range(0, across.shape[1], 128):
            lanes = slice(lane, lane + 128)
            square = across[here, lanes] + rest
            turns = square * lax.rsqrt(square)
            part = turns - jnp.round(turns)
            power = part * part
            sine = part * (NEAR[1] * power + NEAR[0])
            cosine = (power + FAR[1]) * power + FAR[0]
            sine_square = sine * sine
            cosine_square = cosine * cosine
            norm = square * (sine_square + cosine_square)
            amplitude = where[2, here] * pl.reciprocal(norm, approx=True)
            waves[0, here, lanes] = (
                amplitude * (cosine_square - sine_square)
            ).astype(BF16)
            waves[1, here, lanes] = (
                amplitude * ((sine + sine) * cosine)
            ).astype(BF16)
            yield


def early_kernel(freq_size, freqs, place_ref, gathered_ref, where, across, near, far, waves):
    count, _, width = gathered_ref.shape
    cells = width - 128
    me, freq_rank = place_ref[0], place_ref[1]
    local = lax.bitwise_and(me, count - 1)
    tiles = [
        gathered_ref[lax.bitwise_xor(local, at), :, cells:].astype(F32) for at in range(count)
    ]
    lay_targets(tiles, freq_rank * cells, freqs, where, across, near, far)
    for block in range(waves.shape[0]):
        chunk = lax.bitwise_xor(me, block)
        row = ((chunk * freq_size + freq_rank) * cells // SIDE).astype(F32)
        for _ in hologram_pieces(row, where, across, waves.at[block]):
            pass


def cell_kernel(
    freq_size,
    place_ref, gathered_ref, weights_ref, flat_ref, *refs
):
    chunks, _, width = gathered_ref.shape
    cells = width - 128
    hidden = flat_ref.shape[1]
    early = [refs[at : at + 4] for at in range(5, len(refs) - 16, 4)]
    early_where, early_across, early_near, early_far, early_waves = refs[0:5]
    sums_ref, grad_params_ref, across, where, near, far, lift, bias, totals, waves = refs[-16:-6]
    delta_two, spectra = refs[-6:-4]
    early.append(refs[-4:])
    freqs = lift.shape[0] // 2
    base = SMALL_ROWS + 2 * hidden
    half_rows = slice(base, base + hidden // 2)
    w2_ref = flat_ref.at[SMALL_ROWS + hidden : base]
    targets = chunks * 16
    me = place_ref[0]
    freq_rank = place_ref[1]
    stride = freq_size * cells
    second_ref = weights_ref.at[:, 128 : 128 + hidden]

    ready = chunks - refs[-4].shape[0]
    upper_first = lax.bitwise_and(me, ready) != 0

    def in_order(own, new):
        low = lax.select(upper_first, new, own)
        return jnp.concatenate([low, lax.select(upper_first, own, new)], axis=0)

    local = lax.bitwise_and(me, ready - 1)
    tiles = [
        gathered_ref[ready + lax.bitwise_xor(local, at), :, cells:].astype(F32)
        for at in range(ready)
    ]
    lay_targets(tiles, freq_rank * cells, freqs, where, across, near, far)
    lift[:, 0:targets] = in_order(early_near[...], near[...]).T.astype(BF16)
    lift[:, targets:] = in_order(early_far[...], far[...]).T.astype(BF16)
    bias[...] = bias_of(weights_ref)

    middle = hidden + 32
    top = middle + 2 * freqs
    owners = [(part, at) for part in early for at in range(part[0].shape[0])]

    def layers(block):
        part, at = owners[block]
        return [ref.at[at] for ref in part]

    def back_out(spectrum):
        upper_rows = dot(flat_ref[half_rows, 0 : 2 * freqs], spectrum)
        lower_rows = dot(flat_ref[half_rows, 2 * freqs : 4 * freqs], spectrum)
        return jnp.concatenate([upper_rows, lower_rows], axis=0)

    def holograms(block, even):
        row = ((lax.bitwise_xor(me, block) * stride + freq_rank * cells) // SIDE).astype(F32)
        if block >= EARLY_BLOCKS:
            yield from hologram_pieces(row, early_where, early_across, waves.at[even, 0])
        yield from hologram_pieces(row, where, across, waves.at[even, 1])

    def kernels_of(block, even):
        own = early_waves.at[block] if block < EARLY_BLOCKS else waves.at[even, 0]
        new = waves.at[even, 1]
        return jnp.concatenate([in_order(own[at], new[at]) for at in range(2)], axis=0)

    def lower(block, even):
        total = totals.at[lax.bitwise_xor(me, block) // 2]

        def outer(low, left, right):
            rows = slice(low, low + left.shape[0])
            product = contract(left, right, 1, 1)
            total[rows] = total[rows] + product if block % 2 else product

        one, slope, two, _ = layers(block)
        feature = feature_of(gathered_ref, block)
        delta = delta_two[even]
        back = dot(w2_ref[...], delta)
        outer(middle, spectra[even], two[...])
        yield
        value = (back * slope[...]).astype(BF16)
        if block == 0:
            both = contract(weights_ref[:, 0:128], value, 0, 0)
            grad_params_ref[...] = 0.5 * ((both[16:24] + both[48:56]) + both[80:88])
        yield
        outer(0, jnp.concatenate([one[...], feature], axis=0), delta)
        yield
        outer(top, feature, value)
        yield

    def upper(block, even):
        spectrum = dot(lift[...], kernels_of(block, even)).astype(BF16)
        spectra[even] = spectrum
        yield
        back = back_out(spectrum)
        yield
        delta_two[even] = (back * layers(block)[3][...]).astype(BF16)
        yield

    def first(block):
        one, slope_one, _, _ = layers(block)
        half = layer_one(weights_ref, feature_of(gathered_ref, block))
        yield
        one[...], slope_one[...] = activate(half)
        yield

    def second(block):
        one, _, two, slope_two = layers(block)
        half = dot(second_ref[...], one[...])
        half = half + jnp.concatenate([bias[...]] * (cells // 128), axis=1)
        yield
        two[...], slope_two[...] = activate(half)
        yield

    for at in range(chunks + 2):
        waiting = []
        if 0 <= at - 1 < chunks:
            waiting.append((upper(at - 1, (at - 1) % 2), 3))
        if ready <= at + ready - 1 < chunks:
            waiting.append((second(at + ready - 1), 2))
        if at + ready < chunks:
            waiting.append((first(at + ready), 2))
        if 0 <= at - 2 < chunks:
            waiting.append((lower(at - 2, at % 2), 4))
        spots = sum(count for _, count in waiting)
        waiting = [stage for stage, _ in waiting]
        pieces, extra = 0, None
        if at < chunks:
            pieces = (targets // (32 if at < EARLY_BLOCKS else 16)) * (cells // 128)
            extra = holograms(at, at % 2)
        done, drawn = 0, 0
        while waiting:
            for stage in list(waiting):
                if next(stage, True) is True:
                    waiting.remove(stage)
                    continue
                done += 1
                while drawn < pieces * done // spots:
                    next(extra)
                    drawn += 1
        if pieces:
            for _ in extra:
                pass
    pairs = chunks // 2
    added = [totals.at[at] for at in range(pairs)]
    for low in range(0, totals.shape[1], 16):
        terms = [ref[low : low + 16] for ref in added]
        while len(terms) > 1:
            terms = [terms[at] + terms[at + 1] for at in range(0, len(terms), 2)]
        sums_ref[low : low + 16] = terms[0].astype(BF16)


def finish_kernel(
    scale, own_ref, other_ref, weights_ref, flat_ref,
    out_ref, w2_ref, b2_ref, wone_ref, b1_ref, table_ref, proj_ref,
):
    hidden = flat_ref.shape[1]
    middle = hidden + 32
    top = middle + out_ref.shape[1]
    levels = table_ref.shape[0]
    used = levels + proj_ref.shape[0]

    def total(low, high, factor):
        both = own_ref[low:high].astype(F32) + other_ref[low:high].astype(F32)
        return both * (scale * factor)

    w2_ref[...] = total(0, hidden, 0.5)
    out_ref[...] = total(middle, top, 1.0).T
    feature = total(top, top + 32, 0.25)
    b1_ref[...] = feature[used : used + 1]
    b2_ref[...] = total(hidden, middle, 0.5)[used : used + 1]
    rows = jnp.concatenate(split(feature, 3), axis=0).astype(BF16)
    embed = weights_ref[:, 128 + hidden : 128 + hidden + 96]
    wone_ref[...] = jnp.dot(embed, rows, preferred_element_type=F32)
    back = contract(rows, flat_ref[SMALL_ROWS : SMALL_ROWS + hidden], 1, 1)
    back = (back[0:32] + back[32:64]) + back[64:96]
    table_ref[...] = back[0:levels]
    proj_ref[...] = back[levels:used]


def run_forward(gathered, weights, begin, count):
    hidden = weights.shape[0]
    block = (count, hidden, gathered.shape[2] - 128)
    return pl.pallas_call(
        functools.partial(forward_kernel, begin),
        out_shape=[jax.ShapeDtypeStruct(block, kind) for kind in (BF16, F32, BF16, F32)],
        scratch_shapes=[pltpu.VMEM((hidden, 128), F32)],
        compiler_params=pltpu.CompilerParams(vmem_limit_bytes=VMEM_BYTES),
        name="early_forward",
    )(gathered, weights)


def run_early(place, gathered, freq_size, out_dim):
    count, _, width = gathered.shape
    cells = width - 128
    known = count * 16
    vmem = pl.BlockSpec(memory_space=pltpu.VMEM)
    return pl.pallas_call(
        functools.partial(early_kernel, freq_size, out_dim // 2),
        out_shape=[
            jax.ShapeDtypeStruct((4, known, 128), F32),
            jax.ShapeDtypeStruct((known, cells), F32),
            jax.ShapeDtypeStruct((known, out_dim), F32),
            jax.ShapeDtypeStruct((known, out_dim), F32),
            jax.ShapeDtypeStruct((EARLY_BLOCKS, 2, known, cells), BF16),
        ],
        in_specs=[pl.BlockSpec(memory_space=pltpu.SMEM), vmem],
        compiler_params=pltpu.CompilerParams(vmem_limit_bytes=VMEM_BYTES),
        name="early_holograms",
    )(place, gathered)


def run_cells(place, gathered, weights, flat, waves, early, freq_size, out_dim):
    chunks, props, width = gathered.shape
    cells = width - 128
    hidden = flat.shape[1]
    targets = chunks * 16
    rest = chunks - sum(part[0].shape[0] for part in early)
    rows = hidden + out_dim + 64
    vmem = pl.BlockSpec(memory_space=pltpu.VMEM)
    flattened = list(waves) + [array for part in early for array in part]
    return pl.pallas_call(
        functools.partial(cell_kernel, freq_size),
        out_shape=(
            jax.ShapeDtypeStruct((rows, hidden), BF16),
            jax.ShapeDtypeStruct((props, cells), F32),
        ),
        in_specs=[pl.BlockSpec(memory_space=pltpu.SMEM)] + [vmem] * (3 + len(flattened)),
        out_specs=(vmem, vmem),
        scratch_shapes=[
            pltpu.VMEM((targets // 2, cells), F32),
            pltpu.VMEM((4, targets // 2, 128), F32),
            pltpu.VMEM((targets // 2, out_dim), F32),
            pltpu.VMEM((targets // 2, out_dim), F32),
            pltpu.VMEM((out_dim, 2 * targets), BF16),
            pltpu.VMEM((hidden, 128), F32),
            pltpu.VMEM((chunks // 2, rows, hidden), F32),
            pltpu.VMEM((2, 2, 2, targets // 2, cells), BF16),
            pltpu.VMEM((2, hidden, cells), BF16),
            pltpu.VMEM((2, out_dim, cells), BF16),
        ]
        + [pltpu.VMEM((rest, hidden, cells), kind) for kind in (BF16, F32, BF16, F32)],
        compiler_params=pltpu.CompilerParams(vmem_limit_bytes=VMEM_BYTES),
        name="all_cells",
    )(place, gathered, weights, flat, *flattened)


def small_body(
    adjoint,
    target_x,
    target_y,
    target_z,
    assignment,
    level_codes,
    cell_params,
    level_table,
    w_proj,
    w_one,
    b_one,
    w_two,
    b_two,
    w_out,
):
    cells = level_codes.shape[0]
    local = target_x.shape[0]
    levels, hidden = level_table.shape
    props = w_proj.shape[0]
    freqs = w_out.shape[1] // 2
    chunks = lax.axis_size("cells")
    freq_size = lax.axis_size("freq")
    shape = jax.ShapeDtypeStruct
    params = pltpu.CompilerParams(vmem_limit_bytes=VMEM_BYTES)

    def fetched(arrays):
        buffers = [pltpu.VMEM(array.shape, array.dtype) for array in arrays]
        return buffers, pltpu.SemaphoreType.DMA((len(arrays),))

    inputs = (
        w_one, w_two, w_out,
        adjoint, target_x[None, :], target_y[None, :], target_z[None, :], assignment[None, :],
        level_codes[None, :], cell_params, level_table, w_proj, b_one[None, :], b_two[None, :],
    )
    whole = pltpu.CompilerParams(vmem_limit_bytes=WHOLE_VMEM)
    buffers, arrived = fetched(inputs)
    packed, flat = pl.pallas_call(
        pack_kernel,
        out_shape=(
            shape((props, cells + 128), BF16),
            shape((SMALL_ROWS + 2 * hidden + hidden // 2, hidden), BF16),
        ),
        in_specs=[pl.BlockSpec(memory_space=pltpu.HBM)] * len(inputs),
        scratch_shapes=buffers[2:] + [pltpu.VMEM((8, 128), F32), arrived],
        compiler_params=whole,
        name="pack_inputs",
    )(*inputs)
    staged = pl.pallas_call(
        stage_kernel,
        out_shape=shape((props, cells + 128), BF16),
        compiler_params=params,
        name="stage_own",
    )(packed)
    moved = lax.ppermute(packed[None], "cells", [(at, at ^ 1) for at in range(chunks)])
    weights = pl.pallas_call(
        weight_kernel,
        out_shape=shape((hidden, 256 + hidden), BF16),
        compiler_params=params,
        name="prepare_weights",
    )(flat)
    gathered = jnp.concatenate([staged[None], moved], axis=0)
    gathered, weights = lax.optimization_barrier((gathered, weights))
    place = jnp.stack([lax.axis_index("cells"), lax.axis_index("freq")]).astype(jnp.int32)
    out_dim = w_out.shape[1]
    reach, begin, early = 2, 0, []
    while reach < chunks:
        moved = lax.ppermute(gathered, "cells", [(at, at ^ reach) for at in range(chunks)])
        early.append(run_forward(gathered, weights, begin, reach - begin))
        if 2 * reach == chunks:
            waves = run_early(place, gathered, freq_size, out_dim)
        begin = reach
        gathered = jnp.concatenate([gathered, moved], axis=0)
        gathered, early = lax.optimization_barrier((gathered, early))
        reach *= 2

    sums, grad_params = run_cells(
        place, gathered, weights, flat, waves, early, freq_size, out_dim
    )

    other = lax.ppermute(sums, "freq", [(at, at ^ 1) for at in range(freq_size)])
    scale = 1.0 / math.sqrt(cells * chunks * freq_size)
    grad_out, grad_w2, grad_b2, grad_w1, grad_b1, grad_table, grad_proj = pl.pallas_call(
        functools.partial(finish_kernel, scale),
        out_shape=(
            shape((hidden, 2 * freqs), F32),
            shape((hidden, hidden), F32),
            shape((1, hidden), F32),
            shape((hidden, hidden), F32),
            shape((1, hidden), F32),
            shape((levels, hidden), F32),
            shape((props, hidden), F32),
        ),
        compiler_params=params,
        name="finish_sums",
    )(sums, other, weights, flat)
    return (
        grad_out, grad_w2, grad_b2[0], grad_w1, grad_b1[0], grad_table, grad_proj, grad_params,
    )


def solution(mesh):
    chunks = mesh.shape["cells"]
    paired = mesh.shape["freq"] == 2 and chunks > 2 and chunks & (chunks - 1) == 0

    def body(*args):
        local = args[1].shape[0]
        cells = args[5].shape[0]
        hidden = args[9].shape[0]
        suits = (
            paired
            and local == 16
            and cells == 512
            and chunks * cells * chunks * local <= 1 << 20
            and args[7].shape[0] == 16
            and args[8].shape[0] == 8
            and hidden == 2 * args[13].shape[1]
            and mesh.shape["freq"] * cells % SIDE == 0
            and SIDE % cells == 0
            and args[13].shape[1] == 128
        )
        return (small_body if suits else general_body)(*args)

    placed = (
        P(None, ("groups", "cells")),
        P(("groups", "cells")),
        P(("groups", "cells")),
        P(("groups", "cells")),
        P(("groups", "cells")),
        P(("groups", "cells", "freq")),
        P(None, ("groups", "cells", "freq")),
        P(),
        P(),
        P(),
        P(),
        P(),
        P(),
        P(),
    )
    return jax.shard_map(
        body,
        mesh=mesh,
        in_specs=placed,
        out_specs=(
            P("groups", None),
            P("groups", None),
            P("groups"),
            P("groups", None),
            P("groups"),
            P("groups", None),
            P("groups", None),
            P(None, ("groups", "cells", "freq")),
        ),
        check_vma=False,
    )
```
